1024 devices in a mesh: expert: 8 (over x), tensor: 16 (over y, core), dp: 8 (over z).
Axes of the slice: x: 8, y: 8, z: 8, core: 2. Of those that a mesh axis runs over, the one named last changes fastest.
Arguments:
- tokens: bfloat16 [512, 6144], P(('expert', 'tensor'), 'dp'), may hold values from -6 to 6
- grad_output: bfloat16 [512, 6144], P(('expert', 'tensor'), 'dp'), may hold values from -6 to 6
- expert_ids: int32 [512, 4], P(('expert', 'tensor')), may hold values from 0 to 7, all different within a row; in each aligned block of 4 rows (0 to 3, 4 to 7, ...) at most 3 rows name the same one
- gate_weights: bfloat16 [512, 4], P(('expert', 'tensor')), may hold values from 0.099609375 to 1
- w_in: bfloat16 [8, 6144, 12288], P('expert', 'dp', 'tensor'), may hold values from -0.078125 to 0.078125
- scale_in: bfloat16 [8, 12288], P('expert', 'tensor'), may hold values from 1.3953799e-05 to 8.685528e-05, as said below
- w_out: bfloat16 [8, 6144, 6144], P('expert', 'tensor', 'dp'), may hold values from -0.078125 to 0.078125
- scale_out: bfloat16 [8, 6144], P('expert', 'dp'), may hold values from 1.3953799e-05 to 8.685528e-05, as said below
Outputs:
- grad_tokens: bfloat16 [512, 6144], P(('expert', 'tensor'), 'dp')
- grad_in: bfloat16 [8, 6144, 12288], P('expert', 'dp', 'tensor')
- grad_out: bfloat16 [8, 6144, 6144], P('expert', 'tensor', 'dp')
The draws below stay inside these ranges and needn't reach their ends.
Inputs may be any that keep to these rules, and one draw needn't show every extreme that they name: `expert_ids`: each row names 4 different experts; within each aligned block of 4 tokens no expert is named by more than 3 tokens, a bound that some block reaches. `scale_in`: positive per-column scales. `scale_out`: positive per-column scales.
All inputs are finite; a program needn't handle non-finite values.
Results may differ from the reference program's by a relative error of at most 0.01.
Values may be sent and summed in bfloat16 or wider, within the bound.
No kernel may reach another device: no remote copies, remote signals or barrier semaphores. Data moves between devices by JAX's collectives and lax.ppermute only.
A program may use at most 32 MiB of HBM per device.

```python
import math
import jax
import jax.numpy as jnp
import numpy as np
from jax import lax

D = 6144
FF = 6144
EXPERTS = 8
TOP = 4
TOK_DEV = 4
FF_DEV = 384
CAP = 3
TOKENS = 512
N_TENSOR = 16


def draw_scale_in(key, part):
    key = jax.random.fold_in(key, 11)
    level = jax.random.uniform(key, (EXPERTS, 2 * FF), jnp.float32, math.log(0.5), math.log(3.0))
    return (jnp.exp(level) / (448.0 * math.sqrt(D))).astype(jnp.bfloat16)


def draw_scale_out(key, part):
    key = jax.random.fold_in(key, 23)
    level = jax.random.uniform(key, (EXPERTS, D), jnp.float32, math.log(0.5), math.log(3.0))
    return (jnp.exp(level) / (448.0 * math.sqrt(FF))).astype(jnp.bfloat16)


def level_of(own_key, extent, split, low, largest):
    level = 1.0
    for axis_at, shards_of in split:
        heights = jax.random.uniform(jax.random.fold_in(jax.random.fold_in(own_key, 6), axis_at), (shards_of,), jnp.float32, low / len(split), largest / len(split))
        level = level * jnp.repeat(jnp.exp(heights), extent[axis_at] // shards_of).reshape((-1,) + (1,) * (len(extent) - 1 - axis_at))
    return level


def routed_block(own_key, own, number, rows, amount, top, most, lean):
    order = jax.random.permutation(own_key, amount)
    crowded, common = portions_of(amount, rows * top, most, lean, True), portions_of(amount, rows * top, most, lean, False)
    places = jnp.arange(amount)

    def named(sizes, rotation):
        used = int((sizes > 0).sum())
        fixed = max(1, used // 4)
        shifted = fixed + (places - fixed + rotation * (used - fixed)) % max(1, amount - fixed)
        return jnp.zeros((amount,), jnp.int32).at[order[jnp.where(places < fixed, places, shifted)]].set(jnp.asarray(sizes, jnp.int32))

    sizes = jnp.where(number % 4 == 0, named(crowded, number // 4), named(common, number - number // 4 - 1))
    mixed = jax.random.permutation(jax.random.fold_in(own, 3), amount)
    giver, sink = mixed[0:amount // 2 * 2:2], mixed[1:amount // 2 * 2:2]
    slack = jnp.minimum(sizes[giver] - 1, most - sizes[sink]) // 2
    slack = jnp.where((giver == order[0]) | (sink == order[0]) | (sizes[sink] == 0), 0, jnp.maximum(slack, 0))
    shifted = jax.random.randint(jax.random.fold_in(own, 4), (amount // 2,), 0, 1 << 20) % (slack + 1)
    sizes = sizes.at[giver].add(-shifted).at[sink].add(shifted)
    members = jnp.searchsorted(jnp.cumsum(sizes), jnp.arange(rows * top), side="right").astype(jnp.int32)
    grid = members.reshape(top, rows).T
    grid = grid[jax.random.permutation(jax.random.fold_in(own, 1), rows)]
    rotation = jax.random.randint(jax.random.fold_in(own, 2), (rows, 1), 0, top)
    return jnp.take_along_axis(grid, (jnp.arange(top)[None, :] + rotation) % top, axis=1)


def portions_of(amount, total, most, skew, full):
    loads = [(1 << 20) // math.isqrt(grade ** skew) + 1 for grade in range(1, amount + 1)]
    largest = most if full else min(most, max(-(-total // amount), total * loads[0] // sum(loads)))
    least = 1 if total - largest >= amount - 1 else 0
    counts, spare = [largest] + [least] * (amount - 1), total - largest - least * (amount - 1)
    while spare > 0:
        free = [i for i in range(1, amount) if counts[i] < largest] or [i for i in range(1, amount) if counts[i] < most]
        mass, remaining = sum([loads[i] for i in free]), spare
        for i in free:
            more = min(most - counts[i], max(1, remaining * loads[i] // mass), spare)
            counts[i] = counts[i] + more
            spare = spare - more
    return np.array(counts)


def noise(rng, shape, spread, reach, shards=(), held_as=jnp.bfloat16):
    entries = spread * jax.random.normal(rng, shape, jnp.float32)
    if shards:
        entries = entries * level_of(rng, shape, shards, -0.22, 0.18)
    return jnp.clip(entries, -reach, reach).astype(held_as)


def setup_inputs(seed: int = 0) -> dict:
    arg_keys = jax.random.split(jax.random.key(seed), 9)
    tokens = noise(arg_keys[0], (TOKENS, D), 1.0, 6.0, ((0, 128), (1, 8)))
    grad_output = noise(arg_keys[1], (TOKENS, D), 1.0, 6.0, ((0, 128), (1, 8)))
    expert_ids_keys = jax.random.split(jax.random.fold_in(arg_keys[2], 1), TOKENS // TOK_DEV)
    expert_ids_turns = jax.random.permutation(jax.random.fold_in(arg_keys[2], 3), TOKENS // TOK_DEV)
    expert_ids = jax.vmap(lambda own, number: routed_block(jax.random.fold_in(arg_keys[2], 2), own, number, TOK_DEV, EXPERTS, TOP, CAP, 2))(expert_ids_keys, expert_ids_turns).reshape((TOKENS, TOP))
    gate_weights = jnp.clip(0.099609375 + 0.9003906 * jax.random.uniform(arg_keys[3], (TOKENS, TOP), jnp.float32) ** level_of(arg_keys[3], (TOKENS, TOP), ((0, 128),), -0.2, 0.2), 0.099609375, 1.0).astype(jnp.bfloat16)
    w_in = noise(arg_keys[4], (EXPERTS, D, 2 * FF), D ** -0.5, 0.078125, ((0, 8), (1, 8), (2, 16)))
    scale_in = draw_scale_in(jax.random.fold_in(arg_keys[8], 71), 0)
    w_out = noise(arg_keys[6], (EXPERTS, FF, D), FF ** -0.5, 0.078125, ((0, 8), (1, 16), (2, 8)))
    scale_out = draw_scale_out(jax.random.fold_in(arg_keys[8], 71), 0)
    return {"tokens": tokens, "grad_output": grad_output, "expert_ids": expert_ids, "gate_weights": gate_weights, "w_in": w_in, "scale_in": scale_in, "w_out": w_out, "scale_out": scale_out}


def clip_weights(weights, scales):
    wide = weights.astype(jnp.float32)
    bound = 448.0 * scales.astype(jnp.float32)
    return jnp.clip(wide, -bound, bound).astype(jnp.bfloat16), (jnp.abs(wide) <= bound).astype(jnp.float32)


def reference(tokens, grad_output, expert_ids, gate_weights, w_in, scale_in, w_out, scale_out):
    slot_count = (TOKENS // TOK_DEV) * CAP
    pad_x = jnp.concatenate([tokens, jnp.zeros((1, D), jnp.bfloat16)], axis=0)
    pad_dy = jnp.concatenate([grad_output, jnp.zeros((1, D), jnp.bfloat16)], axis=0)
    gates = gate_weights.astype(jnp.float32)

    def per_expert(totals, expert):
        matched = expert_ids == expert
        weight = jnp.sum(jnp.where(matched, gates, 0.0), axis=-1)
        routed = jnp.any(matched, axis=-1)
        picked = jnp.nonzero(routed, size=slot_count, fill_value=TOKENS)[0].astype(jnp.int32)
        x_rows = pad_x[picked].astype(jnp.float32)
        dy_rows = pad_dy[picked].astype(jnp.float32)
        weight_pad = jnp.concatenate([weight, jnp.zeros((1,), weight.dtype)], axis=0)
        gate_rows = weight_pad[picked][:, None]
        wq_in, keep_in = clip_weights(w_in[expert], scale_in[expert][None, :])
        wq_out, keep_out = clip_weights(w_out[expert], scale_out[expert][None, :])
        prelim = jnp.einsum("rd,df->rf", x_rows, wq_in.astype(jnp.float32))
        layout = prelim.reshape(slot_count, N_TENSOR, 2, FF_DEV)
        gate_pre = layout[:, :, 0, :].reshape(slot_count, FF)
        up_pre = layout[:, :, 1, :].reshape(slot_count, FF)
        back_raw = jnp.einsum("rd,fd->rf", dy_rows, wq_out.astype(jnp.float32))
        d_act = gate_rows * back_raw
        sigmoid_gate = jax.nn.sigmoid(gate_pre)
        silu_gate = gate_pre * sigmoid_gate
        slope = sigmoid_gate * (1.0 + gate_pre * (1.0 - sigmoid_gate))
        scaled_act = (gate_rows * silu_gate * up_pre).astype(jnp.bfloat16)
        d_gate = (d_act * up_pre * slope).reshape(slot_count, N_TENSOR, FF_DEV)
        d_up = (d_act * silu_gate).reshape(slot_count, N_TENSOR, FF_DEV)
        d_hidden = jnp.stack([d_gate, d_up], axis=2).reshape(slot_count, 2 * FF).astype(jnp.bfloat16)
        d_wide = d_hidden.astype(jnp.float32)
        dx_rows = jnp.einsum("rf,df->rd", d_wide, wq_in.astype(jnp.float32))
        grad_in_e = (jnp.einsum("rd,rf->df", x_rows, d_wide) * keep_in).astype(jnp.bfloat16)
        grad_out_e = (jnp.einsum("rf,rd->fd", scaled_act.astype(jnp.float32), dy_rows) * keep_out).astype(jnp.bfloat16)
        totals = totals.at[picked].add(dx_rows)
        return totals, (grad_in_e, grad_out_e)

    initial = jnp.zeros((TOKENS + 1, D), jnp.float32)
    totals, (grad_in, grad_out) = lax.scan(per_expert, initial, jnp.arange(EXPERTS, dtype=jnp.int32))
    return totals[:TOKENS].astype(jnp.bfloat16), grad_in, grad_out
```

```python
import jax
import jax.numpy as jnp
from jax import lax
from jax.sharding import Mesh, PartitionSpec as P

CAP = 3
CORES = 2
LANE = 128


def clip_only(weights, scales):
    bound = 448.0 * scales.astype(jnp.float32)
    return jnp.clip(weights.astype(jnp.float32), -bound, bound).astype(jnp.bfloat16)


def keep_mask(weights, scales):
    return jnp.abs(weights.astype(jnp.float32)) <= 448.0 * scales.astype(jnp.float32)


def swap(x):
    return lax.ppermute(x, "core", [(0, 1), (1, 0)])


def exchange(x, axes):
    return lax.all_to_all(x, axes, split_axis=0, concat_axis=0, tiled=True)


def dot(a, b, dims):
    return lax.dot_general(a, b, (dims, ((), ())), preferred_element_type=jnp.float32)


def per_device(tokens, grad_output, expert_ids, gate_weights, w_in, scale_in, w_out, scale_out):
    n_expert = lax.axis_size("expert")
    n_y = lax.axis_size("y")
    n_dp = lax.axis_size("dp")
    tok_rows, width = tokens.shape
    units = w_out.shape[1]
    hidden = 2 * units
    bf16 = jnp.bfloat16
    w_in, w_out = w_in[0], w_out[0]
    parties = n_expert * n_y
    rows = parties * CAP
    share = rows // n_dp

    wq_in = clip_only(w_in, scale_in)
    wq_out = clip_only(w_out, scale_out)
    other = swap(jnp.concatenate([wq_in, wq_out], axis=0))
    wo_in, wo_out = other[:width], other[width:]

    experts = jnp.arange(n_expert, dtype=jnp.int32)
    named = expert_ids[:, :, None] == experts[None, None, :]
    matched = jnp.any(named, axis=1)
    gate_of = jnp.sum(jnp.where(named, gate_weights.astype(jnp.float32)[:, :, None], 0.0), axis=1)
    rank = jnp.cumsum(matched.astype(jnp.int32), axis=0) - 1
    place = matched[:, :, None] & (rank[:, :, None] == jnp.arange(CAP, dtype=jnp.int32))
    place = place.astype(jnp.float32).reshape(tok_rows, n_expert * CAP)
    gates = jnp.sum(place.reshape(tok_rows, n_expert, CAP) * gate_of[:, :, None], axis=0)
    packed = jnp.concatenate([tokens, grad_output], axis=1)
    slots = dot(place.astype(bf16), packed, ((0,), (0,))).astype(bf16)
    slots = slots.reshape(n_expert, CAP, 2 * width)
    gate_cols = jnp.broadcast_to(gates.astype(bf16)[..., None], (n_expert, CAP, LANE))
    slots = jnp.concatenate([slots, gate_cols], axis=2)
    slots = jnp.broadcast_to(slots[:, None], (n_expert, n_y, CAP, 2 * width + LANE))
    got = exchange(slots.reshape(parties, CAP, 2 * width + LANE), ("expert", "y"))
    got = got.reshape(rows, 2 * width + LANE)
    x, dy = got[:, :width], got[:, width : 2 * width]
    gate_rows = got[:, 2 * width : 2 * width + 1]

    part = jnp.concatenate(
        [
            dot(x, wq_in, ((1,), (0,))).astype(bf16),
            dot(x, wo_in, ((1,), (0,))).astype(bf16),
            dot(dy, wq_out, ((1,), (1,))).astype(bf16),
            dot(dy, wo_out, ((1,), (1,))).astype(bf16),
        ],
        axis=1,
    )
    parts = exchange(part.reshape(n_dp, share, 3 * hidden), "dp")
    total = jnp.sum(parts.astype(jnp.float32), axis=0)

    z = lax.axis_index("dp")
    gate = lax.dynamic_slice_in_dim(gate_rows, z * share, share, 0).astype(jnp.float32)

    def activate(pre, back):
        gate_pre, up_pre = pre[:, :units], pre[:, units:]
        d_act = gate * back
        sigmoid_gate = jax.nn.sigmoid(gate_pre)
        silu_gate = gate_pre * sigmoid_gate
        slope = sigmoid_gate * (1.0 + gate_pre * (1.0 - sigmoid_gate))
        act = gate * silu_gate * up_pre
        return d_act * up_pre * slope, d_act * silu_gate, act

    own = activate(total[:, :hidden], total[:, 2 * hidden : 2 * hidden + units])
    oth = activate(total[:, hidden : 2 * hidden], total[:, 2 * hidden + units :])
    mine = jnp.concatenate([own[0], own[1], own[2], oth[0], oth[1], oth[2]], axis=1).astype(bf16)
    copies = jnp.broadcast_to(mine[None], (n_dp, share, 3 * hidden))
    full = exchange(copies, "dp").reshape(rows, 3 * hidden)
    half = hidden + units
    dh_own, act_own = full[:, :hidden], full[:, hidden:half]
    dh_oth = full[:, half : half + hidden]

    dx = dot(dh_own, wq_in, ((1,), (1,))) + dot(dh_oth, wo_in, ((1,), (1,)))
    back = exchange(dx.astype(bf16).reshape(parties, CAP, width), ("expert", "y"))
    spread = place.reshape(tok_rows, n_expert, 1, CAP)
    spread = jnp.broadcast_to(spread, (tok_rows, n_expert, n_y, CAP)).reshape(tok_rows, rows)
    grad_tokens = dot(spread.astype(bf16), back.reshape(rows, width), ((1,), (0,))).astype(bf16)

    got_r = swap(got)
    full_r = swap(full[:, half:])
    x_r, dy_r = got_r[:, :width], got_r[:, width : 2 * width]
    dh_r, act_r = full_r[:, :hidden], full_r[:, hidden:]
    sum_in = dot(x, dh_own, ((0,), (0,))) + dot(x_r, dh_r, ((0,), (0,)))
    sum_out = dot(act_own, dy, ((0,), (0,))) + dot(act_r, dy_r, ((0,), (0,)))
    grad_in = jnp.where(keep_mask(w_in, scale_in), sum_in, 0.0).astype(bf16)
    grad_out = jnp.where(keep_mask(w_out, scale_out), sum_out, 0.0).astype(bf16)
    return grad_tokens, grad_in[None], grad_out[None]


def solution(mesh):
    names = ("expert", "y", "core", "dp")
    n_expert, n_tensor, n_dp = (mesh.shape[a] for a in ("expert", "tensor", "dp"))
    fine = Mesh(mesh.devices.reshape(n_expert, n_tensor // CORES, CORES, n_dp), names)
    tensor = ("y", "core")
    block = ("expert", "y", "core")
    placed = (
        P(block, "dp"),
        P(block, "dp"),
        P(block, None),
        P(block, None),
        P("expert", "dp", tensor),
        P("expert", tensor),
        P("expert", tensor, "dp"),
        P("expert", "dp"),
    )
    return jax.shard_map(
        per_device,
        mesh=fine,
        in_specs=placed,
        out_specs=(P(block, "dp"), P("expert", "dp", tensor), P("expert", tensor, "dp")),
        check_vma=False,
    )
```

```python
import functools
import jax
import jax.numpy as jnp
from jax import lax
from jax.experimental import pallas as pl
from jax.experimental.pallas import tpu as pltpu
from jax.sharding import Mesh, PartitionSpec as P

CAP = 3
CORES = 2
LANE = 128
VMEM_LIMIT = 24 * 1024 * 1024
F32 = jnp.float32
BF16 = jnp.bfloat16


def clip_only(weights, scales):
    bound = 448.0 * scales.astype(F32)
    return jnp.clip(weights.astype(F32), -bound, bound).astype(BF16)


def keep_mask(weights, scales):
    return jnp.abs(weights.astype(F32)) <= 448.0 * scales.astype(F32)


def swap(x):
    return lax.ppermute(x, "core", [(0, 1), (1, 0)])


def exchange(x, axes):
    return lax.all_to_all(x, axes, split_axis=0, concat_axis=0, tiled=True)


def dot(a, b, dims):
    return lax.dot_general(a, b, (dims, ((), ())), preferred_element_type=F32)


def up(n, m):
    return -(-n // m) * m


def routing(ids, n_expert):
    tok_rows, top = ids.shape
    at = lax.broadcasted_iota(jnp.int32, (n_expert, LANE), 0)
    seen = jnp.zeros((n_expert, LANE), jnp.int32)
    masks, named = [], []
    for i in range(tok_rows):
        hits = [jnp.broadcast_to(ids[i : i + 1, k : k + 1], at.shape) == at for k in range(top)]
        any_hit = functools.reduce(jnp.logical_or, hits)
        masks.append([any_hit & (seen == j) for j in range(CAP)])
        named.append(hits)
        seen = seen + any_hit.astype(jnp.int32)
    return masks, named


def slots_kernel(n_expert, n_y, size, ids_ref, gates_ref, tok_ref, cot_ref, out_ref, wide):
    tok_rows, width = tok_ref.shape
    tiles = width // LANE
    masks, named = routing(ids_ref[...], n_expert)
    gates = gates_ref[...].astype(F32)
    lane = lax.broadcasted_iota(jnp.int32, (n_expert, LANE), 1)
    wide[...] = jnp.zeros_like(wide)
    gate_row = jnp.zeros((n_expert, LANE), F32)
    for i in range(tok_rows):
        weight = jnp.zeros((n_expert, LANE), F32)
        for k, hit in enumerate(named[i]):
            weight = jnp.where(hit, jnp.broadcast_to(gates[i : i + 1, k : k + 1], hit.shape), weight)
        for j in range(CAP):
            gate_row = jnp.where(masks[i][j] & (lane == j), weight, gate_row)
    wide[pl.ds(2 * tiles * CAP, n_expert, stride=size), :] = gate_row
    both = [tok_ref[...].astype(F32), cot_ref[...].astype(F32)]
    for k in range(2 * tiles):
        at = (k % tiles) * LANE
        cols = both[k // tiles][:, at : at + LANE]
        for j in range(CAP):
            value = jnp.zeros((n_expert, LANE), F32)
            for i in range(tok_rows):
                value = jnp.where(masks[i][j], jnp.broadcast_to(cols[i : i + 1], value.shape), value)
            wide[pl.ds(j * 2 * tiles + k, n_expert, stride=size), :] = value
    for e in range(n_expert):
        message = wide[e * size : (e + 1) * size, :].astype(BF16)
        for y in range(n_y):
            out_ref[e * n_y + y] = message


def gather_kernel(parties, size, got_ref, own_ref, oth_ref, part_ref, rows_ref, gate_ref, got, wide, own, oth, sems):
    width = own.shape[1]
    hidden = width
    units = own.shape[0] - width
    tiles = width // LANE
    copies = [
        pltpu.make_async_copy(src, dst, sems.at[n])
        for n, (src, dst) in enumerate([(got_ref, got), (own_ref, own), (oth_ref, oth)])
    ]
    for c in copies:
        c.start()
    copies[0].wait()
    wide[...] = got[...].astype(F32)
    gates = wide[pl.ds(2 * tiles * CAP, parties, stride=size), :]
    for j in range(CAP):
        at = slice(j * parties, (j + 1) * parties)
        gate_ref[at, :] = jnp.broadcast_to(gates[:, j : j + 1], (parties, LANE))
        for k in range(2 * tiles):
            value = wide[pl.ds(j * 2 * tiles + k, parties, stride=size), :]
            rows_ref[at, k * LANE : (k + 1) * LANE] = value.astype(BF16)
    for n, weights in enumerate((own, oth)):
        copies[n + 1].wait()
        pre = dot(rows_ref[:, :width], weights[:width, :], ((1,), (0,)))
        part_ref[:, n * hidden : (n + 1) * hidden] = pre.astype(BF16)
        back = dot(rows_ref[:, width:], weights[width:, :], ((1,), (1,)))
        start = 2 * hidden + n * units
        part_ref[:, start : start + units] = back.astype(BF16)


def scatter_kernel(parties, size, offset, full_ref, own_ref, oth_ref, out_ref, dh, own, oth, wide, sems):
    width = own.shape[0]
    hidden = own.shape[1]
    tiles = width // LANE
    pairs = [
        (full_ref.at[:, 0:hidden], dh.at[0]),
        (own_ref.at[0:width, :], own),
        (full_ref.at[:, offset : offset + hidden], dh.at[1]),
        (oth_ref.at[0:width, :], oth),
    ]
    copies = [pltpu.make_async_copy(src, dst, sems.at[n]) for n, (src, dst) in enumerate(pairs)]
    for c in copies:
        c.start()
    wide[...] = jnp.zeros_like(wide)
    copies[0].wait()
    copies[1].wait()
    dx = dot(dh[0], own[...], ((1,), (1,)))
    copies[2].wait()
    copies[3].wait()
    dx = dx + dot(dh[1], oth[...], ((1,), (1,)))
    for j in range(CAP):
        for k in range(tiles):
            value = dx[j * parties : (j + 1) * parties, k * LANE : (k + 1) * LANE]
            wide[pl.ds(j * tiles + k, parties, stride=size), :] = value
    out_ref[...] = wide[...].astype(BF16)


def combine_kernel(n_expert, n_y, size, ids_ref, back_ref, out_ref, wide):
    tok_rows, width = out_ref.shape
    tiles = width // LANE
    parties = n_expert * n_y
    masks, _ = routing(ids_ref[...], n_expert)
    wide[...] = back_ref[...].astype(F32)
    for k in range(tiles):
        totals = [jnp.zeros((1, LANE), F32) for _ in range(tok_rows)]
        for j in range(CAP):
            value = wide[pl.ds(j * tiles + k, parties, stride=size), :]
            value = jnp.sum(value.reshape(n_expert, n_y, LANE), axis=1)
            for i in range(tok_rows):
                totals[i] = totals[i] + jnp.sum(jnp.where(masks[i][j], value, 0.0), axis=0, keepdims=True)
        out_ref[:, k * LANE : (k + 1) * LANE] = jnp.concatenate(totals, axis=0).astype(BF16)


def call(kernel, out_shape, in_specs, out_specs, scratch, flops, moved):
    return pl.pallas_call(
        kernel,
        out_shape=out_shape,
        in_specs=in_specs,
        out_specs=out_specs,
        scratch_shapes=scratch,
        compiler_params=pltpu.CompilerParams(vmem_limit_bytes=VMEM_LIMIT),
        cost_estimate=pl.CostEstimate(flops=flops, bytes_accessed=moved, transcendentals=0),
    )


VM = pl.BlockSpec(memory_space=pltpu.VMEM)
ANY = pl.BlockSpec(memory_space=pl.ANY)


def make_slots(ids, gates, tokens, cotangents, n_expert, n_y):
    width = tokens.shape[1]
    size = up(2 * CAP * width // LANE + 1, 8)
    shape = jax.ShapeDtypeStruct((n_expert * n_y, size, LANE), BF16)
    scratch = [pltpu.VMEM((n_expert * size, LANE), F32)]
    kernel = functools.partial(slots_kernel, n_expert, n_y, size)
    return call(kernel, shape, [VM] * 4, VM, scratch, 1 << 20, 1 << 20)(ids, gates, tokens, cotangents)


def gather(got, own, oth):
    parties, size, _ = got.shape
    width = own.shape[1]
    rows = parties * CAP
    shapes = (
        jax.ShapeDtypeStruct((rows, 2 * own.shape[0]), BF16),
        jax.ShapeDtypeStruct((rows, 2 * width), BF16),
        jax.ShapeDtypeStruct((rows, LANE), F32),
    )
    scratch = [
        pltpu.VMEM((parties * size, LANE), BF16),
        pltpu.VMEM((parties * size, LANE), F32),
        pltpu.VMEM(own.shape, BF16),
        pltpu.VMEM(own.shape, BF16),
        pltpu.SemaphoreType.DMA((3,)),
    ]
    kernel = functools.partial(gather_kernel, parties, size)
    moved = 4 * own.size + 6 * got.size
    return call(kernel, shapes, [ANY] * 3, (VM,) * 3, scratch, 4 * rows * own.size, moved)(
        got.reshape(parties * size, LANE), own, oth
    )


def scatter(full, own, oth, parties):
    rows = full.shape[0]
    width = own.shape[1]
    hidden = width
    size = up(CAP * width // LANE, 8)
    shape = jax.ShapeDtypeStruct((parties * size, LANE), BF16)
    scratch = [
        pltpu.VMEM((2, rows, hidden), BF16),
        pltpu.VMEM((width, hidden), BF16),
        pltpu.VMEM((width, hidden), BF16),
        pltpu.VMEM((parties * size, LANE), F32),
        pltpu.SemaphoreType.DMA((4,)),
    ]
    kernel = functools.partial(scatter_kernel, parties, size, own.shape[0])
    out = call(kernel, shape, [ANY] * 3, VM, scratch, 4 * rows * width * hidden, 4 * own.size)(full, own, oth)
    return out.reshape(parties, size, LANE)


def combine(ids, back, tok_rows, width, n_expert, n_y):
    parties, size, _ = back.shape
    shape = jax.ShapeDtypeStruct((tok_rows, width), BF16)
    scratch = [pltpu.VMEM((parties * size, LANE), F32)]
    kernel = functools.partial(combine_kernel, n_expert, n_y, size)
    return call(kernel, shape, [VM] * 2, VM, scratch, 1 << 20, 1 << 20)(ids, back.reshape(parties * size, LANE))


def per_device(tokens, grad_output, expert_ids, gate_weights, w_in, scale_in, w_out, scale_out):
    n_expert = lax.axis_size("expert")
    n_y = lax.axis_size("y")
    n_dp = lax.axis_size("dp")
    tok_rows, width = tokens.shape
    units = w_out.shape[1]
    hidden = 2 * units
    w_in, w_out = w_in[0], w_out[0]
    parties = n_expert * n_y
    rows = parties * CAP
    share = rows // n_dp

    messages = make_slots(expert_ids, gate_weights, tokens, grad_output, n_expert, n_y)
    got = exchange(messages, ("expert", "y"))

    own = jnp.concatenate([clip_only(w_in, scale_in), clip_only(w_out, scale_out)], axis=0)
    oth = swap(own)

    part, xdy, gate_rows = gather(got, own, oth)
    parts = exchange(part.reshape(n_dp, share, 3 * hidden), "dp")
    total = jnp.sum(parts.astype(F32), axis=0)

    z = lax.axis_index("dp")
    gate = lax.dynamic_slice_in_dim(gate_rows, z * share, share, 0)[:, :1]

    def activate(pre, back):
        gate_pre, up_pre = pre[:, :units], pre[:, units:]
        d_act = gate * back
        sigmoid_gate = jax.nn.sigmoid(gate_pre)
        silu_gate = gate_pre * sigmoid_gate
        slope = sigmoid_gate * (1.0 + gate_pre * (1.0 - sigmoid_gate))
        act = gate * silu_gate * up_pre
        return d_act * up_pre * slope, d_act * silu_gate, act

    first = activate(total[:, :hidden], total[:, 2 * hidden : 2 * hidden + units])
    second = activate(total[:, hidden : 2 * hidden], total[:, 2 * hidden + units :])
    mine = jnp.concatenate([*first, *second], axis=1).astype(BF16)
    copies = jnp.broadcast_to(mine[None], (n_dp, share, 3 * hidden))
    full = exchange(copies, "dp").reshape(rows, 3 * hidden)
    half = hidden + units

    back = exchange(scatter(full, own, oth, parties), ("expert", "y"))
    grad_tokens = combine(expert_ids, back, tok_rows, width, n_expert, n_y)

    xdy_r = swap(xdy)
    full_r = swap(full[:, half:])
    x, dy = xdy[:, :width], xdy[:, width:]
    x_r, dy_r = xdy_r[:, :width], xdy_r[:, width:]
    dh, act = full[:, :hidden], full[:, hidden:half]
    dh_r, act_r = full_r[:, :hidden], full_r[:, hidden:]
    sum_in = dot(x, dh, ((0,), (0,))) + dot(x_r, dh_r, ((0,), (0,)))
    sum_out = dot(act, dy, ((0,), (0,))) + dot(act_r, dy_r, ((0,), (0,)))
    grad_in = jnp.where(keep_mask(w_in, scale_in), sum_in, 0.0).astype(BF16)
    grad_out = jnp.where(keep_mask(w_out, scale_out), sum_out, 0.0).astype(BF16)
    return grad_tokens, grad_in[None], grad_out[None]


def solution(mesh):
    names = ("expert", "y", "core", "dp")
    n_expert, n_tensor, n_dp = (mesh.shape[a] for a in ("expert", "tensor", "dp"))
    fine = Mesh(mesh.devices.reshape(n_expert, n_tensor // CORES, CORES, n_dp), names)
    tensor = ("y", "core")
    block = ("expert", "y", "core")
    placed = (
        P(block, "dp"),
        P(block, "dp"),
        P(block, None),
        P(block, None),
        P("expert", "dp", tensor),
        P("expert", tensor),
        P("expert", tensor, "dp"),
        P("expert", "dp"),
    )
    return jax.shard_map(
        per_device,
        mesh=fine,
        in_specs=placed,
        out_specs=(P(block, "dp"), P("expert", "dp", tensor), P("expert", tensor, "dp")),
        check_vma=False,
    )
```

```python
import functools
import jax
import jax.numpy as jnp
from jax import lax
from jax.experimental import pallas as pl
from jax.experimental.pallas import tpu as pltpu
from jax.sharding import Mesh, PartitionSpec as P

CAP = 3
CORES = 2
LANE = 128
VMEM_LIMIT = 24 * 1024 * 1024
F32 = jnp.float32
BF16 = jnp.bfloat16


def swap(x):
    return lax.ppermute(x, "core", [(0, 1), (1, 0)])


def exchange(x, axes):
    return lax.all_to_all(x, axes, split_axis=0, concat_axis=0, tiled=True)


def dot(a, b, dims):
    return lax.dot_general(a, b, (dims, ((), ())), preferred_element_type=F32)


def up(n, m):
    return -(-n // m) * m


def routing(ids, n_expert):
    tok_rows, top = ids.shape
    at = lax.broadcasted_iota(jnp.int32, (n_expert, LANE), 0)
    seen = jnp.zeros((n_expert, LANE), jnp.int32)
    masks, named = [], []
    for i in range(tok_rows):
        hits = [jnp.broadcast_to(ids[i : i + 1, k : k + 1], at.shape) == at for k in range(top)]
        any_hit = functools.reduce(jnp.logical_or, hits)
        masks.append([any_hit & (seen == j) for j in range(CAP)])
        named.append(hits)
        seen = seen + any_hit.astype(jnp.int32)
    return masks, named


def slots_kernel(n_expert, n_y, size, ids_ref, gates_ref, tok_ref, cot_ref, out_ref, wide):
    tok_rows, width = tok_ref.shape
    tiles = width // LANE
    masks, named = routing(ids_ref[...], n_expert)
    gates = gates_ref[...].astype(F32)
    lane = lax.broadcasted_iota(jnp.int32, (n_expert, LANE), 1)
    wide[...] = jnp.zeros_like(wide)
    gate_row = jnp.zeros((n_expert, LANE), F32)
    for i in range(tok_rows):
        weight = jnp.zeros((n_expert, LANE), F32)
        for k, hit in enumerate(named[i]):
            weight = jnp.where(hit, jnp.broadcast_to(gates[i : i + 1, k : k + 1], hit.shape), weight)
        for j in range(CAP):
            gate_row = jnp.where(masks[i][j] & (lane == j), weight, gate_row)
    wide[pl.ds(2 * tiles * CAP, n_expert, stride=size), :] = gate_row
    both = [tok_ref[...].astype(F32), cot_ref[...].astype(F32)]
    for k in range(2 * tiles):
        at = (k % tiles) * LANE
        cols = both[k // tiles][:, at : at + LANE]
        for j in range(CAP):
            value = jnp.zeros((n_expert, LANE), F32)
            for i in range(tok_rows):
                value = jnp.where(masks[i][j], jnp.broadcast_to(cols[i : i + 1], value.shape), value)
            wide[pl.ds(j * 2 * tiles + k, n_expert, stride=size), :] = value
    for e in range(n_expert):
        message = wide[e * size : (e + 1) * size, :].astype(BF16)
        for y in range(n_y):
            out_ref[e * n_y + y] = message


def gather_kernel(
    parties, size, got_ref, own_ref, oth_in_ref, oth_out_ref, part_ref, rows_ref, gate_ref, got, wide, own, oth, rows, part, sems
):
    width = own.shape[1]
    hidden = width
    units = own.shape[0] - width
    tiles = width // LANE
    pairs = [
        (got_ref, got),
        (own_ref, own),
        (oth_in_ref, oth.at[0:width, :]),
        (oth_out_ref, oth.at[width : width + units, :]),
    ]
    copies = [pltpu.make_async_copy(src, dst, sems.at[n]) for n, (src, dst) in enumerate(pairs)]
    for c in copies:
        c.start()
    copies[0].wait()
    wide[...] = got[...].astype(F32)
    gates = wide[pl.ds(2 * tiles * CAP, parties, stride=size), :]
    for j in range(CAP):
        at = slice(j * parties, (j + 1) * parties)
        gate_ref[at, :] = jnp.broadcast_to(gates[:, j : j + 1], (parties, LANE))
        for k in range(2 * tiles):
            value = wide[pl.ds(j * 2 * tiles + k, parties, stride=size), :]
            rows[at, k * LANE : (k + 1) * LANE] = value.astype(BF16)
    outs = [pltpu.make_async_copy(rows, rows_ref, sems.at[4])]
    outs[0].start()
    for n, weights in enumerate((own, oth)):
        for c in copies[n + 1 : 2 + 2 * n]:
            c.wait()
        pre = dot(rows[:, :width], weights[:width, :], ((1,), (0,)))
        back = dot(rows[:, width:], weights[width:, :], ((1,), (1,)))
        for q, (value, at) in enumerate(((pre, n * hidden), (back, CORES * hidden + n * units))):
            cols = slice(at, at + value.shape[1])
            part[:, cols] = value.astype(BF16)
            c = pltpu.make_async_copy(part.at[:, cols], part_ref.at[:, cols], sems.at[5 + 2 * n + q])
            c.start()
            outs.append(c)
    for c in outs:
        c.wait()


def clip_kernel(step, after_ref, w_in_ref, scale_in_ref, w_out_ref, scale_out_ref, out_ref, *piece_refs):
    del after_ref
    start = 0
    for weights, scales, piece in zip((w_in_ref, w_out_ref), (scale_in_ref, scale_out_ref), piece_refs):
        bound = 448.0 * scales[...].astype(F32)
        for r in range(0, weights.shape[0], step):
            block = weights[r : r + step, :].astype(F32)
            block = jnp.clip(block, -bound, bound).astype(BF16)
            out_ref[start + r : start + r + step, :] = block
            piece[r : r + step, :] = block
        start += weights.shape[0]


def activate_kernel(share, units, z_ref, parts_ref, gate_ref, out_ref):
    n_dp = parts_ref.shape[0]
    hidden = 2 * units
    gates = gate_ref[pl.ds(pl.multiple_of(z_ref[0] * share, 8), share), :]

    def total(at):
        value = parts_ref[0, :, at : at + LANE].astype(F32)
        for p in range(1, n_dp):
            value = value + parts_ref[p, :, at : at + LANE].astype(F32)
        return value

    for n in range(CORES):
        for c in range(0, units, LANE):
            gate_pre = total(n * hidden + c)
            up_pre = total(n * hidden + units + c)
            d_act = gates * total(CORES * hidden + n * units + c)
            sigmoid_gate = jax.nn.sigmoid(gate_pre)
            silu_gate = gate_pre * sigmoid_gate
            slope = sigmoid_gate * (1.0 + gate_pre * (1.0 - sigmoid_gate))
            values = (d_act * up_pre * slope, d_act * silu_gate, gates * silu_gate * up_pre)
            for q, value in enumerate(values):
                at = n * (hidden + units) + q * units + c
                value = value.astype(BF16)
                for p in range(n_dp):
                    out_ref[p, :, at : at + LANE] = value


def scatter_kernel(
    parties, size, offset, after_ref, full_ref, own_ref, oth_ref, out_ref, dh_ref, act_ref, dh, own, oth, wide, out, sems
):
    del after_ref
    width = own.shape[0]
    hidden = own.shape[1]
    tiles = width // LANE
    pairs = [
        (full_ref.at[:, 0:hidden], dh.at[0]),
        (own_ref.at[0:width, :], own),
        (full_ref.at[:, offset : offset + hidden], dh.at[1]),
        (oth_ref, oth),
        (full_ref.at[:, offset : offset + hidden], dh_ref),
        (full_ref.at[:, offset + hidden : 2 * offset], act_ref),
    ]
    copies = [pltpu.make_async_copy(src, dst, sems.at[n]) for n, (src, dst) in enumerate(pairs)]
    for c in copies:
        c.start()
    wide[...] = jnp.zeros_like(wide)
    copies[0].wait()
    copies[1].wait()
    dx = dot(dh[0], own[...], ((1,), (1,)))
    copies[2].wait()
    copies[3].wait()
    dx = dx + dot(dh[1], oth[...], ((1,), (1,)))
    for j in range(CAP):
        for k in range(tiles):
            value = dx[j * parties : (j + 1) * parties, k * LANE : (k + 1) * LANE]
            wide[pl.ds(j * tiles + k, parties, stride=size), :] = value
    out[...] = wide[...].astype(BF16)
    copies.append(pltpu.make_async_copy(out, out_ref, sems.at[6]))
    copies[6].start()
    for c in copies[4:]:
        c.wait()


def grads_kernel(
    step, mine_ref, theirs_ref, full_ref, dh_ref, act_ref, w_in_ref, scale_in_ref, w_out_ref, scale_out_ref, in_ref, out_ref
):
    width, hidden = w_in_ref.shape
    for weights, scales, grad in ((w_in_ref, scale_in_ref, in_ref), (w_out_ref, scale_out_ref, out_ref)):
        bound = 448.0 * scales[...].astype(F32)
        for r in range(0, weights.shape[0], step):
            at = slice(r, r + step)
            if grad is in_ref:
                total = dot(mine_ref[:, at], full_ref[:, :hidden], ((0,), (0,)))
                total = total + dot(theirs_ref[:, at], dh_ref[...], ((0,), (0,)))
            else:
                own_act = full_ref[:, hidden + r : hidden + r + step]
                total = dot(own_act, mine_ref[:, width:], ((0,), (0,)))
                total = total + dot(act_ref[:, at], theirs_ref[:, width:], ((0,), (0,)))
            keep = jnp.abs(weights[at, :].astype(F32)) <= bound
            grad[at, :] = jnp.where(keep, total, 0.0).astype(BF16)


def combine_kernel(n_expert, n_y, size, ids_ref, back_ref, out_ref, wide):
    tok_rows, width = out_ref.shape
    tiles = width // LANE
    parties = n_expert * n_y
    masks, _ = routing(ids_ref[...], n_expert)
    wide[...] = back_ref[...].astype(F32)
    for k in range(tiles):
        totals = [jnp.zeros((1, LANE), F32) for _ in range(tok_rows)]
        for j in range(CAP):
            value = wide[pl.ds(j * tiles + k, parties, stride=size), :]
            value = jnp.sum(value.reshape(n_expert, n_y, LANE), axis=1)
            for i in range(tok_rows):
                totals[i] = totals[i] + jnp.sum(jnp.where(masks[i][j], value, 0.0), axis=0, keepdims=True)
        out_ref[:, k * LANE : (k + 1) * LANE] = jnp.concatenate(totals, axis=0).astype(BF16)


def call(kernel, out_shape, in_specs, out_specs, scratch, flops, moved):
    return pl.pallas_call(
        kernel,
        out_shape=out_shape,
        in_specs=in_specs,
        out_specs=out_specs,
        scratch_shapes=scratch,
        compiler_params=pltpu.CompilerParams(vmem_limit_bytes=VMEM_LIMIT),
        cost_estimate=pl.CostEstimate(flops=flops, bytes_accessed=moved, transcendentals=0),
    )


VM = pl.BlockSpec(memory_space=pltpu.VMEM)
ANY = pl.BlockSpec(memory_space=pl.ANY)
HBM = pl.BlockSpec(memory_space=pltpu.HBM)


def make_slots(ids, gates, tokens, cotangents, n_expert, n_y):
    width = tokens.shape[1]
    size = up(2 * CAP * width // LANE + 1, 8)
    shape = jax.ShapeDtypeStruct((n_expert * n_y, size, LANE), BF16)
    scratch = [pltpu.VMEM((n_expert * size, LANE), F32)]
    kernel = functools.partial(slots_kernel, n_expert, n_y, size)
    return call(kernel, shape, [VM] * 4, VM, scratch, 1 << 20, 1 << 20)(ids, gates, tokens, cotangents)


def clip_weights(after, w_in, scale_in, w_out, scale_out):
    width = w_in.shape[1]
    heights = (w_in.shape[0] + w_out.shape[0], w_in.shape[0], w_out.shape[0])
    shapes = tuple(jax.ShapeDtypeStruct((h, width), BF16) for h in heights)
    size = w_in.size + w_out.size
    kernel = functools.partial(clip_kernel, 64)
    return call(kernel, shapes, [ANY] + [VM] * 4, (VM,) * 3, [], 4 * size, 4 * size)(after, w_in, scale_in, w_out, scale_out)


def activate(z, parts, gate_rows, units):
    share = parts.shape[1]
    shape = jax.ShapeDtypeStruct(parts.shape, BF16)
    kernel = functools.partial(activate_kernel, share, units)
    specs = [pl.BlockSpec(memory_space=pltpu.SMEM), VM, VM]
    return call(kernel, shape, specs, VM, [], 2 * parts.size, 4 * parts.size)(z, parts, gate_rows)


def gather(got, own, oth_in, oth_out):
    parties, size, _ = got.shape
    width = own.shape[1]
    rows = parties * CAP
    shapes = (
        jax.ShapeDtypeStruct((rows, 2 * own.shape[0]), BF16),
        jax.ShapeDtypeStruct((rows, 2 * width), BF16),
        jax.ShapeDtypeStruct((rows, LANE), F32),
    )
    scratch = [
        pltpu.VMEM((parties * size, LANE), BF16),
        pltpu.VMEM((parties * size, LANE), F32),
        pltpu.VMEM(own.shape, BF16),
        pltpu.VMEM(own.shape, BF16),
        pltpu.VMEM((rows, 2 * width), BF16),
        pltpu.VMEM((rows, 2 * own.shape[0]), BF16),
        pltpu.SemaphoreType.DMA((5 + 2 * CORES,)),
    ]
    kernel = functools.partial(gather_kernel, parties, size)
    moved = 4 * own.size + 6 * got.size
    return call(kernel, shapes, [ANY, HBM, HBM, HBM], (HBM, HBM, VM), scratch, 4 * rows * own.size, moved)(
        got.reshape(parties * size, LANE), own, oth_in, oth_out
    )


def scatter(after, full, own, oth, parties):
    rows = full.shape[0]
    width = own.shape[1]
    hidden = width
    size = up(CAP * width // LANE, 8)
    shapes = (
        jax.ShapeDtypeStruct((parties * size, LANE), BF16),
        jax.ShapeDtypeStruct((rows, hidden), BF16),
        jax.ShapeDtypeStruct((rows, own.shape[0] - width), BF16),
    )
    scratch = [
        pltpu.VMEM((2, rows, hidden), BF16),
        pltpu.VMEM((width, hidden), BF16),
        pltpu.VMEM((width, hidden), BF16),
        pltpu.VMEM((parties * size, LANE), F32),
        pltpu.VMEM((parties * size, LANE), BF16),
        pltpu.SemaphoreType.DMA((7,)),
    ]
    kernel = functools.partial(scatter_kernel, parties, size, own.shape[0])
    flops, moved = 4 * rows * width * hidden, 4 * own.size
    out, dh, act = call(kernel, shapes, [HBM, HBM, ANY, ANY], (HBM,) * 3, scratch, flops, moved)(after, full, own, oth)
    return out.reshape(parties, size, LANE), dh, act


def weight_grads(mine, theirs, full, dh, act, w_in, scale_in, w_out, scale_out):
    shapes = (jax.ShapeDtypeStruct(w_in.shape, BF16), jax.ShapeDtypeStruct(w_out.shape, BF16))
    kernel = functools.partial(grads_kernel, 128)
    args = (mine, theirs, full, dh, act, w_in, scale_in, w_out, scale_out)
    return call(kernel, shapes, [VM] * 9, (VM, VM), [], 1 << 20, 1 << 20)(*args)


def combine(ids, back, tok_rows, width, n_expert, n_y):
    parties, size, _ = back.shape
    shape = jax.ShapeDtypeStruct((tok_rows, width), BF16)
    scratch = [pltpu.VMEM((parties * size, LANE), F32)]
    kernel = functools.partial(combine_kernel, n_expert, n_y, size)
    return call(kernel, shape, [VM] * 2, VM, scratch, 1 << 20, 1 << 20)(ids, back.reshape(parties * size, LANE))


def per_device(tokens, grad_output, expert_ids, gate_weights, w_in, scale_in, w_out, scale_out):
    n_expert = lax.axis_size("expert")
    n_y = lax.axis_size("y")
    n_dp = lax.axis_size("dp")
    tok_rows, width = tokens.shape
    units = w_out.shape[1]
    hidden = 2 * units
    w_in, w_out = w_in[0], w_out[0]
    parties = n_expert * n_y
    rows = parties * CAP
    share = rows // n_dp

    messages = make_slots(expert_ids, gate_weights, tokens, grad_output, n_expert, n_y)
    got = exchange(messages, ("expert", "y"))

    own, own_in, own_out = clip_weights(messages, w_in, scale_in, w_out, scale_out)
    oth_in, oth_out = swap(own_in), swap(own_out)

    part, xdy, gate_rows = gather(got, own, oth_in, oth_out)
    parts = exchange(part.reshape(n_dp, share, 3 * hidden), "dp")
    z = lax.axis_index("dp").astype(jnp.int32).reshape(1)
    copies = activate(z, parts, gate_rows, units)
    full = exchange(copies, "dp").reshape(rows, 3 * hidden)

    xdy_r = swap(xdy)
    returns, dh_oth, act_oth = scatter(xdy_r, full, own, oth_in, parties)
    back = exchange(returns, ("expert", "y"))
    grad_tokens = combine(expert_ids, back, tok_rows, width, n_expert, n_y)

    dh_r, act_r = swap(dh_oth), swap(act_oth)
    grad_in, grad_out = weight_grads(xdy, xdy_r, full, dh_r, act_r, w_in, scale_in, w_out, scale_out)
    return grad_tokens, grad_in[None], grad_out[None]


def solution(mesh):
    names = ("expert", "y", "core", "dp")
    n_expert, n_tensor, n_dp = (mesh.shape[a] for a in ("expert", "tensor", "dp"))
    fine = Mesh(mesh.devices.reshape(n_expert, n_tensor // CORES, CORES, n_dp), names)
    tensor = ("y", "core")
    block = ("expert", "y", "core")
    placed = (
        P(block, "dp"),
        P(block, "dp"),
        P(block, None),
        P(block, None),
        P("expert", "dp", tensor),
        P("expert", tensor),
        P("expert", tensor, "dp"),
        P("expert", "dp"),
    )
    return jax.shard_map(
        per_device,
        mesh=fine,
        in_specs=placed,
        out_specs=(P(block, "dp"), P("expert", "dp", tensor), P("expert", tensor, "dp")),
        check_vma=False,
    )
```

```python
import functools
import jax
import jax.numpy as jnp
from jax import lax
from jax.experimental import pallas as pl
from jax.experimental.pallas import tpu as pltpu
from jax.sharding import Mesh, PartitionSpec as P

CAP = 3
CORES = 2
LANE = 128
MIB = 1024 * 1024
ROOMY, FULL = 28 * MIB, 60 * MIB
F32 = jnp.float32
BF16 = jnp.bfloat16


def swap(x):
    return lax.ppermute(x, "core", [(0, 1), (1, 0)])


def exchange(x, axes):
    return lax.all_to_all(x, axes, split_axis=0, concat_axis=0, tiled=True)


def dot(a, b, dims):
    return lax.dot_general(a, b, (dims, ((), ())), preferred_element_type=F32)


def up(n, m):
    return -(-n // m) * m


def routing(ids, n_expert):
    tok_rows, top = ids.shape
    at = lax.broadcasted_iota(jnp.int32, (n_expert, LANE), 0)
    seen = jnp.zeros((n_expert, LANE), jnp.int32)
    masks, named = [], []
    for i in range(tok_rows):
        hits = [jnp.broadcast_to(ids[i : i + 1, k : k + 1], at.shape) == at for k in range(top)]
        any_hit = functools.reduce(jnp.logical_or, hits)
        masks.append([any_hit & (seen == j) for j in range(CAP)])
        named.append(hits)
        seen = seen + any_hit.astype(jnp.int32)
    return masks, named


def start_all(pairs, sems, first=0):
    copies = [pltpu.make_async_copy(src, dst, sems.at[first + n]) for n, (src, dst) in enumerate(pairs)]
    for c in copies:
        c.start()
    return copies


def wait_all(copies):
    for c in copies:
        c.wait()


def slots_kernel(
    n_expert, n_y, size, ids_ref, gates_ref, tok_ref, cot_ref, out_ref, ids, gates, tok, cot, wide, narrow, sems
):
    tok_rows, width = tok.shape
    tiles = width // LANE
    copies = start_all([(ids_ref, ids), (gates_ref, gates), (tok_ref, tok), (cot_ref, cot)], sems)
    wide[...] = jnp.zeros_like(wide)
    wait_all(copies)
    masks, named = routing(ids[...], n_expert)
    gate = gates[...].astype(F32)
    lane = lax.broadcasted_iota(jnp.int32, (n_expert, LANE), 1)
    gate_row = jnp.zeros((n_expert, LANE), F32)
    for i in range(tok_rows):
        weight = jnp.zeros((n_expert, LANE), F32)
        for k, hit in enumerate(named[i]):
            weight = jnp.where(hit, jnp.broadcast_to(gate[i : i + 1, k : k + 1], hit.shape), weight)
        for j in range(CAP):
            gate_row = jnp.where(masks[i][j] & (lane == j), weight, gate_row)
    wide[pl.ds(2 * tiles * CAP, n_expert, stride=size), :] = gate_row
    both = [tok[...].astype(F32), cot[...].astype(F32)]
    for k in range(2 * tiles):
        at = (k % tiles) * LANE
        cols = both[k // tiles][:, at : at + LANE]
        for j in range(CAP):
            value = jnp.zeros((n_expert, LANE), F32)
            for i in range(tok_rows):
                value = jnp.where(masks[i][j], jnp.broadcast_to(cols[i : i + 1], value.shape), value)
            wide[pl.ds(j * 2 * tiles + k, n_expert, stride=size), :] = value
    narrow[...] = wide[...].reshape(n_expert, size, LANE).astype(BF16)
    wait_all(start_all([(narrow, out_ref.at[:, y]) for y in range(n_y)], sems, 4))


def gather_kernel(
    parties, size, got_ref, own_ref, oth_in_ref, oth_out_ref, part_ref, rows_ref, gate_ref,
    got, wide, own, oth, rows, part, gate, sems,
):
    width = own.shape[1]
    units = own.shape[0] - width
    tiles = width // LANE
    half = width + units
    copies = start_all(
        [
            (got_ref, got),
            (own_ref, own),
            (oth_in_ref, oth.at[0:width, :]),
            (oth_out_ref, oth.at[width:half, :]),
        ],
        sems,
    )
    copies[0].wait()
    wide[...] = got[...].astype(F32)
    gates = wide[pl.ds(2 * tiles * CAP, parties, stride=size), :]
    for j in range(CAP):
        at = slice(j * parties, (j + 1) * parties)
        gate[at, :] = jnp.broadcast_to(gates[:, j : j + 1], (parties, LANE))
        for k in range(2 * tiles):
            value = wide[pl.ds(j * 2 * tiles + k, parties, stride=size), :]
            rows[at, k * LANE : (k + 1) * LANE] = value.astype(BF16)
    outs = start_all([(rows, rows_ref), (gate, gate_ref)], sems, 4)
    for n, weights in enumerate((own, oth)):
        wait_all(copies[n + 1 : 2 + 2 * n])
        pre = dot(rows[:, :width], weights[:width, :], ((1,), (0,)))
        part[:, n * half : n * half + width] = pre.astype(BF16)
        back = dot(rows[:, width:], weights[width:, :], ((1,), (1,)))
        part[:, n * half + width : (n + 1) * half] = back.astype(BF16)
        cols = slice(n * half, (n + 1) * half)
        outs += start_all([(part.at[:, cols], part_ref.at[:, cols])], sems, 6 + n)
    wait_all(outs)


def clip_kernel(
    step, after_ref, w_in_ref, scale_in_ref, w_out_ref, scale_out_ref, own_ref, in_ref, out_ref,
    w_in, scale_in, w_out, scale_out, own, sems,
):
    del after_ref
    wait_all(
        start_all([(w_in_ref, w_in), (scale_in_ref, scale_in), (w_out_ref, w_out), (scale_out_ref, scale_out)], sems)
    )
    start = 0
    for weights, scales in ((w_in, scale_in), (w_out, scale_out)):
        bound = 448.0 * scales[...].astype(F32)
        for r in range(0, weights.shape[0], step):
            block = weights[r : r + step, :].astype(F32)
            own[start + r : start + r + step, :] = jnp.clip(block, -bound, bound).astype(BF16)
        start += weights.shape[0]
    tall = w_in.shape[0]
    wait_all(start_all([(own, own_ref), (own.at[0:tall, :], in_ref), (own.at[tall:start, :], out_ref)], sems, 4))


def activate_kernel(share, units, z_ref, parts_ref, gate_ref, out_ref, parts, gate, out, sems):
    n_dp = parts.shape[0]
    half = 3 * units
    at = pl.multiple_of(z_ref[0] * share, 8)
    halves = [slice(n * half, (n + 1) * half) for n in range(CORES)]
    copies = start_all(
        [(gate_ref.at[pl.ds(at, share), :], gate)] + [(parts_ref.at[:, :, h], parts.at[:, :, h]) for h in halves], sems
    )
    copies[0].wait()
    gates = gate[...]

    def total(at):
        value = parts[0, :, at : at + LANE].astype(F32)
        for p in range(1, n_dp):
            value = value + parts[p, :, at : at + LANE].astype(F32)
        return value

    outs = []
    for n in range(CORES):
        copies[1 + n].wait()
        for c in range(n * half, n * half + units, LANE):
            gate_pre = total(c)
            up_pre = total(c + units)
            d_act = gates * total(c + 2 * units)
            sigmoid_gate = jax.nn.sigmoid(gate_pre)
            silu_gate = gate_pre * sigmoid_gate
            slope = sigmoid_gate * (1.0 + gate_pre * (1.0 - sigmoid_gate))
            out[:, c : c + LANE] = (d_act * up_pre * slope).astype(BF16)
            out[:, c + units : c + units + LANE] = (d_act * silu_gate).astype(BF16)
            out[:, c + 2 * units : c + 2 * units + LANE] = (gates * silu_gate * up_pre).astype(BF16)
        pairs = [(out.at[:, halves[n]], out_ref.at[p, :, halves[n]]) for p in range(n_dp)]
        outs += start_all(pairs, sems, 1 + CORES + n * n_dp)
    wait_all(outs)


def scatter_kernel(
    parties, size, offset, after_ref, full_ref, own_ref, oth_ref, out_ref, dh_ref, act_ref, dh, own, oth, wide, out, sems
):
    del after_ref
    width = own.shape[0]
    hidden = own.shape[1]
    tiles = width // LANE
    copies = start_all(
        [
            (full_ref.at[:, 0:hidden], dh.at[0]),
            (own_ref.at[0:width, :], own),
            (full_ref.at[:, offset : offset + hidden], dh.at[1]),
            (oth_ref, oth),
            (full_ref.at[:, offset : offset + hidden], dh_ref),
            (full_ref.at[:, offset + hidden : 2 * offset], act_ref),
        ],
        sems,
    )
    wide[...] = jnp.zeros_like(wide)
    wait_all(copies[0:2])
    dx = dot(dh[0], own[...], ((1,), (1,)))
    wait_all(copies[2:4])
    dx = dx + dot(dh[1], oth[...], ((1,), (1,)))
    for j in range(CAP):
        for k in range(tiles):
            value = dx[j * parties : (j + 1) * parties, k * LANE : (k + 1) * LANE]
            wide[pl.ds(j * tiles + k, parties, stride=size), :] = value
    out[...] = wide[...].astype(BF16)
    wait_all(copies[4:] + start_all([(out, out_ref)], sems, 6))


def grads_kernel(step, *refs):
    n_in = 9
    sources, (in_ref, out_ref) = refs[:n_in], refs[n_in : n_in + 2]
    held, (in_v, out_v, sems) = refs[n_in + 2 : 2 * n_in + 2], refs[2 * n_in + 2 :]
    mine, theirs, full, dh, act, w_in, scale_in, w_out, scale_out = held
    half = full.shape[1]
    pairs = [(src.at[:, 0:half] if dst is full else src, dst) for src, dst in zip(sources, held)]
    wait_all(start_all(pairs, sems))
    width, hidden = w_in.shape
    outs = []
    for n, (weights, scales, grad, dst) in enumerate(((w_in, scale_in, in_v, in_ref), (w_out, scale_out, out_v, out_ref))):
        bound = 448.0 * scales[...].astype(F32)
        for r in range(0, weights.shape[0], step):
            at = slice(r, r + step)
            if grad is in_v:
                total = dot(mine[:, at], full[:, :hidden], ((0,), (0,)))
                total = total + dot(theirs[:, at], dh[...], ((0,), (0,)))
            else:
                total = dot(full[:, hidden + r : hidden + r + step], mine[:, width:], ((0,), (0,)))
                total = total + dot(act[:, at], theirs[:, width:], ((0,), (0,)))
            keep = jnp.abs(weights[at, :].astype(F32)) <= bound
            grad[at, :] = jnp.where(keep, total, 0.0).astype(BF16)
        outs += start_all([(grad, dst)], sems, n_in + n)
    wait_all(outs)


def combine_kernel(n_expert, n_y, size, ids_ref, back_ref, out_ref, ids, back, wide, out, sems):
    tok_rows, width = out.shape
    tiles = width // LANE
    parties = n_expert * n_y
    copies = start_all([(ids_ref, ids), (back_ref, back)], sems)
    copies[0].wait()
    masks, _ = routing(ids[...], n_expert)
    copies[1].wait()
    wide[...] = back[...].astype(F32)
    for k in range(tiles):
        totals = [jnp.zeros((1, LANE), F32) for _ in range(tok_rows)]
        for j in range(CAP):
            value = wide[pl.ds(j * tiles + k, parties, stride=size), :]
            value = jnp.sum(value.reshape(n_expert, n_y, LANE), axis=1)
            for i in range(tok_rows):
                totals[i] = totals[i] + jnp.sum(jnp.where(masks[i][j], value, 0.0), axis=0, keepdims=True)
        out[:, k * LANE : (k + 1) * LANE] = jnp.concatenate(totals, axis=0).astype(BF16)
    wait_all(start_all([(out, out_ref)], sems, 2))


ANY = pl.BlockSpec(memory_space=pl.ANY)
SMEM = pl.BlockSpec(memory_space=pltpu.SMEM)


def array(shape, dtype=BF16):
    return jax.ShapeDtypeStruct(shape, dtype)


def call(kernel, outs, scratch, n_sems, flops, moved, *args, limit=FULL):
    return pl.pallas_call(
        kernel,
        out_shape=outs,
        in_specs=[SMEM if a.shape == (1,) else ANY for a in args],
        out_specs=jax.tree.map(lambda _: ANY, outs),
        scratch_shapes=[pltpu.VMEM(*s) for s in scratch] + [pltpu.SemaphoreType.DMA((n_sems,))],
        compiler_params=pltpu.CompilerParams(vmem_limit_bytes=limit),
        cost_estimate=pl.CostEstimate(flops=flops, bytes_accessed=moved, transcendentals=0),
    )(*args)


def like(*arrays):
    return [(a.shape, a.dtype) for a in arrays]


def make_slots(ids, gates, tokens, cotangents, n_expert, n_y):
    size = up(2 * CAP * tokens.shape[1] // LANE + 1, 8)
    args = (ids, gates, tokens, cotangents)
    scratch = like(*args) + [((n_expert * size, LANE), F32), ((n_expert, size, LANE), BF16)]
    kernel = functools.partial(slots_kernel, n_expert, n_y, size)
    out = call(kernel, array((n_expert, n_y, size, LANE)), scratch, 4 + n_y, 1 << 20, 1 << 20, *args)
    return out.reshape(n_expert * n_y, size, LANE)


def clip_weights(after, w_in, scale_in, w_out, scale_out):
    width = w_in.shape[1]
    args = (w_in, scale_in, w_out, scale_out)
    heights = (w_in.shape[0] + w_out.shape[0], w_in.shape[0], w_out.shape[0])
    scratch = like(*args) + [((heights[0], width), BF16)]
    size = heights[0] * width
    kernel = functools.partial(clip_kernel, 64)
    return call(kernel, tuple(array((h, width)) for h in heights), scratch, 7, 4 * size, 4 * size, after, *args)


def activate(z, parts, gate_rows, units):
    n_dp, share, cols = parts.shape
    scratch = like(parts) + [((share, LANE), F32), ((share, cols), BF16)]
    kernel = functools.partial(activate_kernel, share, units)
    n_sems = 1 + CORES + CORES * n_dp
    return call(kernel, array(parts.shape), scratch, n_sems, 2 * parts.size, 4 * parts.size, z, parts, gate_rows, limit=ROOMY)


def gather(got, own, oth_in, oth_out):
    parties, size, _ = got.shape
    height, width = own.shape
    rows = parties * CAP
    flat = got.reshape(parties * size, LANE)
    shapes = (array((rows, 2 * height)), array((rows, 2 * width)), array((rows, LANE), F32))
    scratch = like(flat) + [(flat.shape, F32)] + like(own, own, shapes[1], shapes[0], shapes[2])
    kernel = functools.partial(gather_kernel, parties, size)
    moved = 4 * own.size + 6 * got.size
    return call(kernel, shapes, scratch, 6 + CORES, 4 * rows * own.size, moved, flat, own, oth_in, oth_out)


def scatter(after, full, own, oth, parties):
    rows = full.shape[0]
    height, width = own.shape
    hidden = width
    size = up(CAP * width // LANE, 8)
    flat = array((parties * size, LANE))
    shapes = (flat, array((rows, hidden)), array((rows, height - width)))
    scratch = [((2, rows, hidden), BF16), (oth.shape, BF16), (oth.shape, BF16), (flat.shape, F32), (flat.shape, BF16)]
    kernel = functools.partial(scatter_kernel, parties, size, height)
    flops, moved = 4 * rows * width * hidden, 4 * own.size
    out, dh, act = call(kernel, shapes, scratch, 7, flops, moved, after, full, own, oth)
    return out.reshape(parties, size, LANE), dh, act


def weight_grads(mine, theirs, full, dh, act, w_in, scale_in, w_out, scale_out):
    shapes = (array(w_in.shape), array(w_out.shape))
    kernel = functools.partial(grads_kernel, 128)
    args = (mine, theirs, full, dh, act, w_in, scale_in, w_out, scale_out)
    held = like(*args)
    held[2] = ((full.shape[0], full.shape[1] // CORES), BF16)
    return call(kernel, shapes, held + like(*shapes), len(args) + 2, 1 << 20, 1 << 20, *args)


def combine(ids, back, tok_rows, width, n_expert, n_y):
    parties, size, _ = back.shape
    flat = back.reshape(parties * size, LANE)
    shape = array((tok_rows, width))
    scratch = like(ids, flat) + [(flat.shape, F32)] + like(shape)
    kernel = functools.partial(combine_kernel, n_expert, n_y, size)
    return call(kernel, shape, scratch, 3, 1 << 20, 1 << 20, ids, flat, limit=ROOMY)


def per_device(tokens, grad_output, expert_ids, gate_weights, w_in, scale_in, w_out, scale_out):
    n_expert = lax.axis_size("expert")
    n_y = lax.axis_size("y")
    n_dp = lax.axis_size("dp")
    tok_rows, width = tokens.shape
    units = w_out.shape[1]
    hidden = 2 * units
    w_in, w_out = w_in[0], w_out[0]
    parties = n_expert * n_y
    rows = parties * CAP
    share = rows // n_dp

    messages = make_slots(expert_ids, gate_weights, tokens, grad_output, n_expert, n_y)
    got = exchange(messages, ("expert", "y"))

    own, own_in, own_out = clip_weights(messages, w_in, scale_in, w_out, scale_out)
    oth_in, oth_out = swap(own_in), swap(own_out)

    part, xdy, gate_rows = gather(got, own, oth_in, oth_out)
    parts = exchange(part.reshape(n_dp, share, 3 * hidden), "dp")
    z = lax.axis_index("dp").astype(jnp.int32).reshape(1)
    copies = activate(z, parts, gate_rows, units)
    full = exchange(copies, "dp").reshape(rows, 3 * hidden)

    xdy_r = swap(xdy)
    returns, dh_oth, act_oth = scatter(xdy_r, full, own, oth_in, parties)
    back = exchange(returns, ("expert", "y"))
    grad_tokens = combine(expert_ids, back, tok_rows, width, n_expert, n_y)

    dh_r, act_r = swap(dh_oth), swap(act_oth)
    grad_in, grad_out = weight_grads(xdy, xdy_r, full, dh_r, act_r, w_in, scale_in, w_out, scale_out)
    return grad_tokens, grad_in[None], grad_out[None]


def solution(mesh):
    names = ("expert", "y", "core", "dp")
    n_expert, n_tensor, n_dp = (mesh.shape[a] for a in ("expert", "tensor", "dp"))
    fine = Mesh(mesh.devices.reshape(n_expert, n_tensor // CORES, CORES, n_dp), names)
    tensor = ("y", "core")
    block = ("expert", "y", "core")
    placed = (
        P(block, "dp"),
        P(block, "dp"),
        P(block, None),
        P(block, None),
        P("expert", "dp", tensor),
        P("expert", tensor),
        P("expert", tensor, "dp"),
        P("expert", "dp"),
    )
    return jax.shard_map(
        per_device,
        mesh=fine,
        in_specs=placed,
        out_specs=(P(block, "dp"), P("expert", "dp", tensor), P("expert", tensor, "dp")),
        check_vma=False,
    )
```

```python
import functools
import jax
import jax.numpy as jnp
from jax import lax
from jax.experimental import pallas as pl
from jax.experimental.pallas import tpu as pltpu
from jax.sharding import Mesh, PartitionSpec as P

CAP = 3
CORES = 2
LANE = 128
MIB = 1024 * 1024
ROOMY, FULL = 28 * MIB, 60 * MIB
F32 = jnp.float32
BF16 = jnp.bfloat16


def swap(x):
    return lax.ppermute(x, "core", [(0, 1), (1, 0)])


def exchange(x, axes):
    return lax.all_to_all(x, axes, split_axis=0, concat_axis=0, tiled=True)


def dot(a, b, dims):
    return lax.dot_general(a, b, (dims, ((), ())), preferred_element_type=F32)


def up(n, m):
    return -(-n // m) * m


def routing(ids, n_expert):
    tok_rows, top = ids.shape
    at = lax.broadcasted_iota(jnp.int32, (n_expert, LANE), 0)
    seen = jnp.zeros((n_expert, LANE), jnp.int32)
    masks, named = [], []
    for i in range(tok_rows):
        hits = [jnp.broadcast_to(ids[i : i + 1, k : k + 1], at.shape) == at for k in range(top)]
        any_hit = functools.reduce(jnp.logical_or, hits)
        masks.append([any_hit & (seen == j) for j in range(CAP)])
        named.append(hits)
        seen = seen + any_hit.astype(jnp.int32)
    return masks, named


def start_all(pairs, sems, first=0):
    copies = [pltpu.make_async_copy(src, dst, sems.at[first + n]) for n, (src, dst) in enumerate(pairs)]
    for c in copies:
        c.start()
    return copies


def wait_all(copies):
    for c in copies:
        c.wait()


def slots_kernel(
    n_expert, n_y, size, ids_ref, gates_ref, tok_ref, cot_ref, out_ref, ids, gates, tok, cot, wide, narrow, sems
):
    tok_rows, width = tok.shape
    tiles = width // LANE
    copies = start_all([(ids_ref, ids), (gates_ref, gates), (tok_ref, tok), (cot_ref, cot)], sems)
    wide[...] = jnp.zeros_like(wide)
    wait_all(copies)
    masks, named = routing(ids[...], n_expert)
    gate = gates[...].astype(F32)
    lane = lax.broadcasted_iota(jnp.int32, (n_expert, LANE), 1)
    gate_row = jnp.zeros((n_expert, LANE), F32)
    for i in range(tok_rows):
        weight = jnp.zeros((n_expert, LANE), F32)
        for k, hit in enumerate(named[i]):
            weight = jnp.where(hit, jnp.broadcast_to(gate[i : i + 1, k : k + 1], hit.shape), weight)
        for j in range(CAP):
            gate_row = jnp.where(masks[i][j] & (lane == j), weight, gate_row)
    wide[pl.ds(2 * tiles * CAP, n_expert, stride=size), :] = gate_row
    both = [tok[...].astype(F32), cot[...].astype(F32)]
    for k in range(2 * tiles):
        at = (k % tiles) * LANE
        cols = both[k // tiles][:, at : at + LANE]
        for j in range(CAP):
            value = jnp.zeros((n_expert, LANE), F32)
            for i in range(tok_rows):
                value = jnp.where(masks[i][j], jnp.broadcast_to(cols[i : i + 1], value.shape), value)
            wide[pl.ds(j * 2 * tiles + k, n_expert, stride=size), :] = value
    narrow[...] = wide[...].reshape(n_expert, size, LANE).astype(BF16)
    wait_all(start_all([(narrow, out_ref.at[:, y]) for y in range(n_y)], sems, 4))


def gather_kernel(
    parties, size, got_ref, own_ref, oth_in_ref, oth_out_ref, part_ref, rows_ref, gate_ref,
    got, wide, own, oth, rows, part, gate, sems,
):
    width = own.shape[1]
    units = own.shape[0] - width
    tiles = width // LANE
    half = width + units
    copies = start_all(
        [
            (got_ref, got),
            (own_ref, own),
            (oth_in_ref, oth.at[0:width, :]),
            (oth_out_ref, oth.at[width:half, :]),
        ],
        sems,
    )
    copies[0].wait()
    wide[...] = got[...].astype(F32)
    gates = wide[pl.ds(2 * tiles * CAP, parties, stride=size), :]
    for j in range(CAP):
        at = slice(j * parties, (j + 1) * parties)
        gate[at, :] = jnp.broadcast_to(gates[:, j : j + 1], (parties, LANE))
        for k in range(2 * tiles):
            value = wide[pl.ds(j * 2 * tiles + k, parties, stride=size), :]
            rows[at, k * LANE : (k + 1) * LANE] = value.astype(BF16)
    outs = start_all([(rows, rows_ref), (gate, gate_ref)], sems, 4)
    for n, weights in enumerate((own, oth)):
        wait_all(copies[n + 1 : 2 + 2 * n])
        pre = dot(rows[:, :width], weights[:width, :], ((1,), (0,)))
        part[:, n * half : n * half + width] = pre.astype(BF16)
        back = dot(rows[:, width:], weights[width:, :], ((1,), (1,)))
        part[:, n * half + width : (n + 1) * half] = back.astype(BF16)
        cols = slice(n * half, (n + 1) * half)
        outs += start_all([(part.at[:, cols], part_ref.at[:, cols])], sems, 6 + n)
    wait_all(outs)


def clip_kernel(
    step, after_ref, w_in_ref, scale_in_ref, w_out_ref, scale_out_ref, own_ref, in_ref, out_ref,
    w_in, scale_in, w_out, scale_out, own, sems,
):
    del after_ref
    wait_all(
        start_all([(w_in_ref, w_in), (scale_in_ref, scale_in), (w_out_ref, w_out), (scale_out_ref, scale_out)], sems)
    )
    start = 0
    for weights, scales in ((w_in, scale_in), (w_out, scale_out)):
        bound = 448.0 * scales[...].astype(F32)
        for r in range(0, weights.shape[0], step):
            block = weights[r : r + step, :].astype(F32)
            own[start + r : start + r + step, :] = jnp.clip(block, -bound, bound).astype(BF16)
        start += weights.shape[0]
    tall = w_in.shape[0]
    wait_all(start_all([(own, own_ref), (own.at[0:tall, :], in_ref), (own.at[tall:start, :], out_ref)], sems, 4))


def activate_kernel(share, units, z_ref, parts_ref, gate_ref, out_ref, parts, gate, out, sems):
    n_dp = parts.shape[0]
    half = 3 * units
    at = pl.multiple_of(z_ref[0] * share, 8)
    halves = [slice(n * half, (n + 1) * half) for n in range(CORES)]
    copies = start_all(
        [(gate_ref.at[pl.ds(at, share), :], gate)] + [(parts_ref.at[:, :, h], parts.at[:, :, h]) for h in halves], sems
    )
    copies[0].wait()
    gates = gate[...]

    def total(at):
        value = parts[0, :, at : at + LANE].astype(F32)
        for p in range(1, n_dp):
            value = value + parts[p, :, at : at + LANE].astype(F32)
        return value

    outs = []
    for n in range(CORES):
        copies[1 + n].wait()
        for c in range(n * half, n * half + units, LANE):
            gate_pre = total(c)
            up_pre = total(c + units)
            d_act = gates * total(c + 2 * units)
            sigmoid_gate = jax.nn.sigmoid(gate_pre)
            silu_gate = gate_pre * sigmoid_gate
            slope = sigmoid_gate * (1.0 + gate_pre * (1.0 - sigmoid_gate))
            out[:, c : c + LANE] = (d_act * up_pre * slope).astype(BF16)
            out[:, c + units : c + units + LANE] = (d_act * silu_gate).astype(BF16)
            out[:, c + 2 * units : c + 2 * units + LANE] = (gates * silu_gate * up_pre).astype(BF16)
        pairs = [(out.at[:, halves[n]], out_ref.at[p, :, halves[n]]) for p in range(n_dp)]
        outs += start_all(pairs, sems, 1 + CORES + n * n_dp)
    wait_all(outs)


def scatter_kernel(
    parties, size, offset, after_ref, full_ref, own_ref, oth_ref, out_ref, dh_ref, act_ref, dh, act, own, oth, wide, out, sems
):
    del after_ref
    width = own.shape[0]
    hidden = own.shape[1]
    tiles = width // LANE
    copies = start_all(
        [
            (full_ref.at[:, 0:hidden], dh.at[0]),
            (own_ref.at[0:width, :], own),
            (full_ref.at[:, offset : offset + hidden], dh.at[1]),
            (oth_ref, oth),
            (full_ref.at[:, offset + hidden : 2 * offset], act),
        ],
        sems,
    )
    wide[...] = jnp.zeros_like(wide)
    wait_all(copies[0:2])
    dx = dot(dh[0], own[...], ((1,), (1,)))
    wait_all(copies[2:4])
    copies[4].wait()
    outs = start_all([(dh.at[1], dh_ref), (act, act_ref)], sems, 5)
    dx = dx + dot(dh[1], oth[...], ((1,), (1,)))
    for j in range(CAP):
        for k in range(tiles):
            value = dx[j * parties : (j + 1) * parties, k * LANE : (k + 1) * LANE]
            wide[pl.ds(j * tiles + k, parties, stride=size), :] = value
    out[...] = wide[...].astype(BF16)
    wait_all(outs + start_all([(out, out_ref)], sems, 7))


def grads_kernel(step, *refs):
    n_in = 9
    sources, (in_ref, out_ref) = refs[:n_in], refs[n_in : n_in + 2]
    held, (in_v, out_v, sems) = refs[n_in + 2 : 2 * n_in + 2], refs[2 * n_in + 2 :]
    mine, theirs, full, dh, act, w_in, scale_in, w_out, scale_out = held
    half = full.shape[1]
    pairs = [(src.at[:, 0:half] if dst is full else src, dst) for src, dst in zip(sources, held)]
    wait_all(start_all(pairs, sems))
    width, hidden = w_in.shape
    outs = []
    for n, (weights, scales, grad, dst) in enumerate(((w_in, scale_in, in_v, in_ref), (w_out, scale_out, out_v, out_ref))):
        bound = 448.0 * scales[...].astype(F32)
        for r in range(0, weights.shape[0], step):
            at = slice(r, r + step)
            if grad is in_v:
                total = dot(mine[:, at], full[:, :hidden], ((0,), (0,)))
                total = total + dot(theirs[:, at], dh[...], ((0,), (0,)))
            else:
                total = dot(full[:, hidden + r : hidden + r + step], mine[:, width:], ((0,), (0,)))
                total = total + dot(act[:, at], theirs[:, width:], ((0,), (0,)))
            keep = jnp.abs(weights[at, :].astype(F32)) <= bound
            grad[at, :] = jnp.where(keep, total, 0.0).astype(BF16)
        outs += start_all([(grad, dst)], sems, n_in + n)
    wait_all(outs)


def combine_kernel(n_expert, n_y, size, ids_ref, back_ref, out_ref, ids, back, wide, out, sems):
    tok_rows, width = out.shape
    tiles = width // LANE
    parties = n_expert * n_y
    copies = start_all([(ids_ref, ids), (back_ref, back)], sems)
    copies[0].wait()
    masks, _ = routing(ids[...], n_expert)
    copies[1].wait()
    wide[...] = back[...].astype(F32)
    for k in range(tiles):
        totals = [jnp.zeros((1, LANE), F32) for _ in range(tok_rows)]
        for j in range(CAP):
            value = wide[pl.ds(j * tiles + k, parties, stride=size), :]
            value = jnp.sum(value.reshape(n_expert, n_y, LANE), axis=1)
            for i in range(tok_rows):
                totals[i] = totals[i] + jnp.sum(jnp.where(masks[i][j], value, 0.0), axis=0, keepdims=True)
        out[:, k * LANE : (k + 1) * LANE] = jnp.concatenate(totals, axis=0).astype(BF16)
    wait_all(start_all([(out, out_ref)], sems, 2))


ANY = pl.BlockSpec(memory_space=pl.ANY)
SMEM = pl.BlockSpec(memory_space=pltpu.SMEM)


def array(shape, dtype=BF16):
    return jax.ShapeDtypeStruct(shape, dtype)


def call(kernel, outs, scratch, n_sems, flops, moved, *args, limit=FULL):
    return pl.pallas_call(
        kernel,
        out_shape=outs,
        in_specs=[SMEM if a.shape == (1,) else ANY for a in args],
        out_specs=jax.tree.map(lambda _: ANY, outs),
        scratch_shapes=[pltpu.VMEM(*s) for s in scratch] + [pltpu.SemaphoreType.DMA((n_sems,))],
        compiler_params=pltpu.CompilerParams(vmem_limit_bytes=limit),
        cost_estimate=pl.CostEstimate(flops=flops, bytes_accessed=moved, transcendentals=0),
    )(*args)


def like(*arrays):
    return [(a.shape, a.dtype) for a in arrays]


def make_slots(ids, gates, tokens, cotangents, n_expert, n_y):
    size = up(2 * CAP * tokens.shape[1] // LANE + 1, 8)
    args = (ids, gates, tokens, cotangents)
    scratch = like(*args) + [((n_expert * size, LANE), F32), ((n_expert, size, LANE), BF16)]
    kernel = functools.partial(slots_kernel, n_expert, n_y, size)
    out = call(kernel, array((n_expert, n_y, size, LANE)), scratch, 4 + n_y, 1 << 20, 1 << 20, *args)
    return out.reshape(n_expert * n_y, size, LANE)


def clip_weights(after, w_in, scale_in, w_out, scale_out):
    width = w_in.shape[1]
    args = (w_in, scale_in, w_out, scale_out)
    heights = (w_in.shape[0] + w_out.shape[0], w_in.shape[0], w_out.shape[0])
    scratch = like(*args) + [((heights[0], width), BF16)]
    size = heights[0] * width
    kernel = functools.partial(clip_kernel, 64)
    return call(kernel, tuple(array((h, width)) for h in heights), scratch, 7, 4 * size, 4 * size, after, *args)


def activate(z, parts, gate_rows, units):
    n_dp, share, cols = parts.shape
    scratch = like(parts) + [((share, LANE), F32), ((share, cols), BF16)]
    kernel = functools.partial(activate_kernel, share, units)
    n_sems = 1 + CORES + CORES * n_dp
    return call(kernel, array(parts.shape), scratch, n_sems, 2 * parts.size, 4 * parts.size, z, parts, gate_rows, limit=ROOMY)


def gather(got, own, oth_in, oth_out):
    parties, size, _ = got.shape
    height, width = own.shape
    rows = parties * CAP
    flat = got.reshape(parties * size, LANE)
    shapes = (array((rows, 2 * height)), array((rows, 2 * width)), array((rows, LANE), F32))
    scratch = like(flat) + [(flat.shape, F32)] + like(own, own, shapes[1], shapes[0], shapes[2])
    kernel = functools.partial(gather_kernel, parties, size)
    moved = 4 * own.size + 6 * got.size
    return call(kernel, shapes, scratch, 6 + CORES, 4 * rows * own.size, moved, flat, own, oth_in, oth_out)


def scatter(after, full, own, oth, parties):
    rows = full.shape[0]
    height, width = own.shape
    hidden = width
    size = up(CAP * width // LANE, 8)
    flat = array((parties * size, LANE))
    shapes = (flat, array((rows, hidden)), array((rows, height - width)))
    scratch = [((2, rows, hidden), BF16)] + like(shapes[2], oth, oth) + [(flat.shape, F32), (flat.shape, BF16)]
    kernel = functools.partial(scatter_kernel, parties, size, height)
    flops, moved = 4 * rows * width * hidden, 4 * own.size
    out, dh, act = call(kernel, shapes, scratch, 8, flops, moved, after, full, own, oth)
    return out.reshape(parties, size, LANE), dh, act


def weight_grads(mine, theirs, full, dh, act, w_in, scale_in, w_out, scale_out):
    shapes = (array(w_in.shape), array(w_out.shape))
    kernel = functools.partial(grads_kernel, 128)
    args = (mine, theirs, full, dh, act, w_in, scale_in, w_out, scale_out)
    held = like(*args)
    held[2] = ((full.shape[0], full.shape[1] // CORES), BF16)
    return call(kernel, shapes, held + like(*shapes), len(args) + 2, 1 << 20, 1 << 20, *args)


def combine(ids, back, tok_rows, width, n_expert, n_y):
    parties, size, _ = back.shape
    flat = back.reshape(parties * size, LANE)
    shape = array((tok_rows, width))
    scratch = like(ids, flat) + [(flat.shape, F32)] + like(shape)
    kernel = functools.partial(combine_kernel, n_expert, n_y, size)
    return call(kernel, shape, scratch, 3, 1 << 20, 1 << 20, ids, flat, limit=ROOMY)


def per_device(tokens, grad_output, expert_ids, gate_weights, w_in, scale_in, w_out, scale_out):
    n_expert = lax.axis_size("expert")
    n_y = lax.axis_size("y")
    n_dp = lax.axis_size("dp")
    tok_rows, width = tokens.shape
    units = w_out.shape[1]
    hidden = 2 * units
    w_in, w_out = w_in[0], w_out[0]
    parties = n_expert * n_y
    rows = parties * CAP
    share = rows // n_dp

    messages = make_slots(expert_ids, gate_weights, tokens, grad_output, n_expert, n_y)
    got = exchange(messages, ("expert", "y"))

    own, own_in, own_out = clip_weights(messages, w_in, scale_in, w_out, scale_out)
    oth_in, oth_out = swap(own_in), swap(own_out)

    part, xdy, gate_rows = gather(got, own, oth_in, oth_out)
    parts = exchange(part.reshape(n_dp, share, 3 * hidden), "dp")
    z = lax.axis_index("dp").astype(jnp.int32).reshape(1)
    copies = activate(z, parts, gate_rows, units)
    full = exchange(copies, "dp").reshape(rows, 3 * hidden)

    xdy_r = swap(xdy)
    returns, dh_oth, act_oth = scatter(xdy_r, full, own, oth_in, parties)
    back = exchange(returns, ("expert", "y"))
    grad_tokens = combine(expert_ids, back, tok_rows, width, n_expert, n_y)

    dh_r, act_r = swap(dh_oth), swap(act_oth)
    grad_in, grad_out = weight_grads(xdy, xdy_r, full, dh_r, act_r, w_in, scale_in, w_out, scale_out)
    return grad_tokens, grad_in[None], grad_out[None]


def solution(mesh):
    names = ("expert", "y", "core", "dp")
    n_expert, n_tensor, n_dp = (mesh.shape[a] for a in ("expert", "tensor", "dp"))
    fine = Mesh(mesh.devices.reshape(n_expert, n_tensor // CORES, CORES, n_dp), names)
    tensor = ("y", "core")
    block = ("expert", "y", "core")
    placed = (
        P(block, "dp"),
        P(block, "dp"),
        P(block, None),
        P(block, None),
        P("expert", "dp", tensor),
        P("expert", tensor),
        P("expert", tensor, "dp"),
        P("expert", "dp"),
    )
    return jax.shard_map(
        per_device,
        mesh=fine,
        in_specs=placed,
        out_specs=(P(block, "dp"), P("expert", "dp", tensor), P("expert", tensor, "dp")),
        check_vma=False,
    )
```

```python
import functools
import jax
import jax.numpy as jnp
from jax import lax
from jax.experimental import pallas as pl
from jax.experimental.pallas import tpu as pltpu
from jax.sharding import Mesh, PartitionSpec as P

CAP = 3
CORES = 2
LANE = 128
MIB = 1024 * 1024
ROOMY, FULL = 28 * MIB, 60 * MIB
F32 = jnp.float32
BF16 = jnp.bfloat16


def swap(x):
    return lax.ppermute(x, "core", [(0, 1), (1, 0)])


def exchange(x, axes):
    return lax.all_to_all(x, axes, split_axis=0, concat_axis=0, tiled=True)


def dot(a, b, dims):
    return lax.dot_general(a, b, (dims, ((), ())), preferred_element_type=F32)


def up(n, m):
    return -(-n // m) * m


def routing(ids, n_expert):
    tok_rows, top = ids.shape
    at = lax.broadcasted_iota(jnp.int32, (n_expert, LANE), 0)
    seen = jnp.zeros((n_expert, LANE), jnp.int32)
    masks, named = [], []
    for i in range(tok_rows):
        hits = [jnp.broadcast_to(ids[i : i + 1, k : k + 1], at.shape) == at for k in range(top)]
        any_hit = functools.reduce(jnp.logical_or, hits)
        masks.append([any_hit & (seen == j) for j in range(CAP)])
        named.append(hits)
        seen = seen + any_hit.astype(jnp.int32)
    return masks, named


def start_all(pairs, sems, first=0):
    copies = [pltpu.make_async_copy(src, dst, sems.at[first + n]) for n, (src, dst) in enumerate(pairs)]
    for c in copies:
        c.start()
    return copies


def wait_all(copies):
    for c in copies:
        c.wait()


def slots_kernel(
    n_expert, n_y, size, ids_ref, gates_ref, tok_ref, cot_ref, out_ref, ids, gates, tok, cot, wide, narrow, sems
):
    tok_rows, width = tok.shape
    tiles = width // LANE
    copies = start_all([(ids_ref, ids), (gates_ref, gates), (tok_ref, tok), (cot_ref, cot)], sems)
    wide[...] = jnp.zeros_like(wide)
    wait_all(copies)
    masks, named = routing(ids[...], n_expert)
    gate = gates[...].astype(F32)
    lane = lax.broadcasted_iota(jnp.int32, (n_expert, LANE), 1)
    gate_row = jnp.zeros((n_expert, LANE), F32)
    for i in range(tok_rows):
        weight = jnp.zeros((n_expert, LANE), F32)
        for k, hit in enumerate(named[i]):
            weight = jnp.where(hit, jnp.broadcast_to(gate[i : i + 1, k : k + 1], hit.shape), weight)
        for j in range(CAP):
            gate_row = jnp.where(masks[i][j] & (lane == j), weight, gate_row)
    wide[pl.ds(2 * tiles * CAP, n_expert, stride=size), :] = gate_row
    both = [tok[...].astype(F32), cot[...].astype(F32)]
    for k in range(2 * tiles):
        at = (k % tiles) * LANE
        cols = both[k // tiles][:, at : at + LANE]
        for j in range(CAP):
            value = jnp.zeros((n_expert, LANE), F32)
            for i in range(tok_rows):
                value = jnp.where(masks[i][j], jnp.broadcast_to(cols[i : i + 1], value.shape), value)
            wide[pl.ds(j * 2 * tiles + k, n_expert, stride=size), :] = value
    narrow[...] = wide[...].reshape(n_expert, size, LANE).astype(BF16)
    wait_all(start_all([(narrow, out_ref.at[:, y]) for y in range(n_y)], sems, 4))


def gather_kernel(
    parties, size, got, own, oth_in, oth_out, part_ref, rows_ref, gate_ref, keep_ref, wide, rows, part, gate, sems
):
    width = own.shape[1]
    units = own.shape[0] - width
    tiles = width // LANE
    half = width + units
    outs = start_all([(oth_in, keep_ref)], sems)
    wide[...] = got[...].astype(F32)
    gates = wide[pl.ds(2 * tiles * CAP, parties, stride=size), :]
    for j in range(CAP):
        at = slice(j * parties, (j + 1) * parties)
        gate[at, :] = jnp.broadcast_to(gates[:, j : j + 1], (parties, LANE))
        for k in range(2 * tiles):
            value = wide[pl.ds(j * 2 * tiles + k, parties, stride=size), :]
            rows[at, k * LANE : (k + 1) * LANE] = value.astype(BF16)
    outs += start_all([(rows, rows_ref), (gate, gate_ref)], sems, 1)
    for n, (w_in, w_out) in enumerate(((own.at[:width, :], own.at[width:, :]), (oth_in, oth_out))):
        pre = dot(rows[:, :width], w_in[...], ((1,), (0,)))
        part[:, n * half : n * half + width] = pre.astype(BF16)
        back = dot(rows[:, width:], w_out[...], ((1,), (1,)))
        part[:, n * half + width : (n + 1) * half] = back.astype(BF16)
        cols = slice(n * half, (n + 1) * half)
        outs += start_all([(part.at[:, cols], part_ref.at[:, cols])], sems, 3 + n)
    wait_all(outs)


def clip_kernel(
    step, after_ref, w_in_ref, scale_in_ref, w_out_ref, scale_out_ref, own_ref, in_ref, out_ref,
    w_in, scale_in, w_out, scale_out, own, sems,
):
    del after_ref
    wait_all(
        start_all([(w_in_ref, w_in), (scale_in_ref, scale_in), (w_out_ref, w_out), (scale_out_ref, scale_out)], sems)
    )
    start = 0
    for weights, scales in ((w_in, scale_in), (w_out, scale_out)):
        bound = 448.0 * scales[...].astype(F32)
        for r in range(0, weights.shape[0], step):
            block = weights[r : r + step, :].astype(F32)
            own[start + r : start + r + step, :] = jnp.clip(block, -bound, bound).astype(BF16)
        start += weights.shape[0]
    tall = w_in.shape[0]
    wait_all(start_all([(own, own_ref), (own.at[0:tall, :], in_ref), (own.at[tall:start, :], out_ref)], sems, 4))


def activate_kernel(share, units, z_ref, parts_ref, gate_ref, out_ref, parts, gate, out, sems):
    n_dp = parts.shape[0]
    half = 3 * units
    at = pl.multiple_of(z_ref[0] * share, 8)
    halves = [slice(n * half, (n + 1) * half) for n in range(CORES)]
    copies = start_all(
        [(gate_ref.at[pl.ds(at, share), :], gate)] + [(parts_ref.at[:, :, h], parts.at[:, :, h]) for h in halves], sems
    )
    copies[0].wait()
    gates = gate[...]

    def total(at):
        value = parts[0, :, at : at + LANE].astype(F32)
        for p in range(1, n_dp):
            value = value + parts[p, :, at : at + LANE].astype(F32)
        return value

    outs = []
    for n in range(CORES):
        copies[1 + n].wait()
        for c in range(n * half, n * half + units, LANE):
            gate_pre = total(c)
            up_pre = total(c + units)
            d_act = gates * total(c + 2 * units)
            sigmoid_gate = jax.nn.sigmoid(gate_pre)
            silu_gate = gate_pre * sigmoid_gate
            slope = sigmoid_gate * (1.0 + gate_pre * (1.0 - sigmoid_gate))
            out[:, c : c + LANE] = (d_act * up_pre * slope).astype(BF16)
            out[:, c + units : c + units + LANE] = (d_act * silu_gate).astype(BF16)
            out[:, c + 2 * units : c + 2 * units + LANE] = (gates * silu_gate * up_pre).astype(BF16)
        pairs = [(out.at[:, halves[n]], out_ref.at[p, :, halves[n]]) for p in range(n_dp)]
        outs += start_all(pairs, sems, 1 + CORES + n * n_dp)
    wait_all(outs)


def scatter_kernel(
    parties, size, offset, after_ref, full_ref, own_ref, oth_ref, out_ref, dh_ref, act_ref, dh, act, own, oth, wide, out, sems
):
    del after_ref
    width = own.shape[0]
    hidden = own.shape[1]
    tiles = width // LANE
    copies = start_all(
        [
            (full_ref.at[:, 0:hidden], dh.at[0]),
            (own_ref, own),
            (full_ref.at[:, offset : offset + hidden], dh.at[1]),
            (oth_ref, oth),
            (full_ref.at[:, offset + hidden : 2 * offset], act),
        ],
        sems,
    )
    wide[...] = jnp.zeros_like(wide)
    wait_all(copies[0:2])
    dx = dot(dh[0], own[...], ((1,), (1,)))
    wait_all(copies[2:4])
    copies[4].wait()
    outs = start_all([(dh.at[1], dh_ref), (act, act_ref)], sems, 5)
    dx = dx + dot(dh[1], oth[...], ((1,), (1,)))
    for j in range(CAP):
        for k in range(tiles):
            value = dx[j * parties : (j + 1) * parties, k * LANE : (k + 1) * LANE]
            wide[pl.ds(j * tiles + k, parties, stride=size), :] = value
    out[...] = wide[...].astype(BF16)
    wait_all(outs + start_all([(out, out_ref)], sems, 7))


def grads_kernel(step, *refs):
    n_in = 9
    sources, (in_ref, out_ref) = refs[:n_in], refs[n_in : n_in + 2]
    held, (in_v, out_v, sems) = refs[n_in + 2 : 2 * n_in + 2], refs[2 * n_in + 2 :]
    mine, theirs, full, dh, act, w_in, scale_in, w_out, scale_out = held
    half = full.shape[1]
    pairs = [(src.at[:, 0:half] if dst is full else src, dst) for src, dst in zip(sources, held)]
    wait_all(start_all(pairs, sems))
    width, hidden = w_in.shape
    outs = []
    for n, (weights, scales, grad, dst) in enumerate(((w_in, scale_in, in_v, in_ref), (w_out, scale_out, out_v, out_ref))):
        bound = 448.0 * scales[...].astype(F32)
        for r in range(0, weights.shape[0], step):
            at = slice(r, r + step)
            if grad is in_v:
                total = dot(mine[:, at], full[:, :hidden], ((0,), (0,)))
                total = total + dot(theirs[:, at], dh[...], ((0,), (0,)))
            else:
                total = dot(full[:, hidden + r : hidden + r + step], mine[:, width:], ((0,), (0,)))
                total = total + dot(act[:, at], theirs[:, width:], ((0,), (0,)))
            keep = jnp.abs(weights[at, :].astype(F32)) <= bound
            grad[at, :] = jnp.where(keep, total, 0.0).astype(BF16)
        outs += start_all([(grad, dst)], sems, n_in + n)
    wait_all(outs)


def combine_kernel(n_expert, n_y, size, ids_ref, back_ref, out_ref, ids, back, wide, out, sems):
    tok_rows, width = out.shape
    tiles = width // LANE
    parties = n_expert * n_y
    copies = start_all([(ids_ref, ids), (back_ref, back)], sems)
    copies[0].wait()
    masks, _ = routing(ids[...], n_expert)
    copies[1].wait()
    wide[...] = back[...].astype(F32)
    for k in range(tiles):
        totals = [jnp.zeros((1, LANE), F32) for _ in range(tok_rows)]
        for j in range(CAP):
            value = wide[pl.ds(j * tiles + k, parties, stride=size), :]
            value = jnp.sum(value.reshape(n_expert, n_y, LANE), axis=1)
            for i in range(tok_rows):
                totals[i] = totals[i] + jnp.sum(jnp.where(masks[i][j], value, 0.0), axis=0, keepdims=True)
        out[:, k * LANE : (k + 1) * LANE] = jnp.concatenate(totals, axis=0).astype(BF16)
    wait_all(start_all([(out, out_ref)], sems, 2))


ANY = pl.BlockSpec(memory_space=pl.ANY)
VM = pl.BlockSpec(memory_space=pltpu.VMEM)
SMEM = pl.BlockSpec(memory_space=pltpu.SMEM)


def array(shape, dtype=BF16):
    return jax.ShapeDtypeStruct(shape, dtype)


def call(kernel, outs, scratch, n_sems, flops, moved, *args, limit=FULL, spec=ANY):
    return pl.pallas_call(
        kernel,
        out_shape=outs,
        in_specs=[SMEM if a.shape == (1,) else spec for a in args],
        out_specs=jax.tree.map(lambda _: ANY, outs),
        scratch_shapes=[pltpu.VMEM(*s) for s in scratch] + [pltpu.SemaphoreType.DMA((n_sems,))],
        compiler_params=pltpu.CompilerParams(vmem_limit_bytes=limit),
        cost_estimate=pl.CostEstimate(flops=flops, bytes_accessed=moved, transcendentals=0),
    )(*args)


def like(*arrays):
    return [(a.shape, a.dtype) for a in arrays]


def make_slots(ids, gates, tokens, cotangents, n_expert, n_y):
    size = up(2 * CAP * tokens.shape[1] // LANE + 1, 8)
    args = (ids, gates, tokens, cotangents)
    scratch = like(*args) + [((n_expert * size, LANE), F32), ((n_expert, size, LANE), BF16)]
    kernel = functools.partial(slots_kernel, n_expert, n_y, size)
    out = call(kernel, array((n_expert, n_y, size, LANE)), scratch, 4 + n_y, 1 << 20, 1 << 20, *args)
    return out.reshape(n_expert * n_y, size, LANE)


def clip_weights(after, w_in, scale_in, w_out, scale_out):
    width = w_in.shape[1]
    args = (w_in, scale_in, w_out, scale_out)
    heights = (w_in.shape[0] + w_out.shape[0], w_in.shape[0], w_out.shape[0])
    scratch = like(*args) + [((heights[0], width), BF16)]
    size = heights[0] * width
    kernel = functools.partial(clip_kernel, 64)
    return call(kernel, tuple(array((h, width)) for h in heights), scratch, 7, 4 * size, 4 * size, after, *args, limit=ROOMY)


def activate(z, parts, gate_rows, units):
    n_dp, share, cols = parts.shape
    scratch = like(parts) + [((share, LANE), F32), ((share, cols), BF16)]
    kernel = functools.partial(activate_kernel, share, units)
    n_sems = 1 + CORES + CORES * n_dp
    return call(kernel, array(parts.shape), scratch, n_sems, 2 * parts.size, 4 * parts.size, z, parts, gate_rows, limit=ROOMY)


def gather(got, own, oth_in, oth_out):
    parties, size, _ = got.shape
    height, width = own.shape
    rows = parties * CAP
    flat = got.reshape(parties * size, LANE)
    shapes = (array((rows, 2 * height)), array((rows, 2 * width)), array((rows, LANE), F32), array(oth_in.shape))
    scratch = [(flat.shape, F32)] + like(shapes[1], shapes[0], shapes[2])
    kernel = functools.partial(gather_kernel, parties, size)
    flops, moved = 4 * rows * own.size, 4 * own.size + 6 * got.size
    return call(kernel, shapes, scratch, 3 + CORES, flops, moved, flat, own, oth_in, oth_out, limit=ROOMY, spec=VM)


def scatter(after, full, own, oth, parties):
    rows = full.shape[0]
    width, hidden = own.shape
    height = full.shape[1] // CORES
    size = up(CAP * width // LANE, 8)
    flat = array((parties * size, LANE))
    shapes = (flat, array((rows, hidden)), array((rows, height - hidden)))
    scratch = [((2, rows, hidden), BF16)] + like(shapes[2], oth, oth) + [(flat.shape, F32), (flat.shape, BF16)]
    kernel = functools.partial(scatter_kernel, parties, size, height)
    flops, moved = 4 * rows * width * hidden, 4 * own.size
    out, dh, act = call(kernel, shapes, scratch, 8, flops, moved, after, full, own, oth, limit=ROOMY)
    return out.reshape(parties, size, LANE), dh, act


def weight_grads(mine, theirs, full, dh, act, w_in, scale_in, w_out, scale_out):
    shapes = (array(w_in.shape), array(w_out.shape))
    kernel = functools.partial(grads_kernel, 128)
    args = (mine, theirs, full, dh, act, w_in, scale_in, w_out, scale_out)
    held = like(*args)
    held[2] = ((full.shape[0], full.shape[1] // CORES), BF16)
    return call(kernel, shapes, held + like(*shapes), len(args) + 2, 1 << 20, 1 << 20, *args)


def combine(ids, back, tok_rows, width, n_expert, n_y):
    parties, size, _ = back.shape
    flat = back.reshape(parties * size, LANE)
    shape = array((tok_rows, width))
    scratch = like(ids, flat) + [(flat.shape, F32)] + like(shape)
    kernel = functools.partial(combine_kernel, n_expert, n_y, size)
    return call(kernel, shape, scratch, 3, 1 << 20, 1 << 20, ids, flat, limit=ROOMY)


def per_device(tokens, grad_output, expert_ids, gate_weights, w_in, scale_in, w_out, scale_out):
    n_expert = lax.axis_size("expert")
    n_y = lax.axis_size("y")
    n_dp = lax.axis_size("dp")
    tok_rows, width = tokens.shape
    units = w_out.shape[1]
    hidden = 2 * units
    w_in, w_out = w_in[0], w_out[0]
    parties = n_expert * n_y
    rows = parties * CAP
    share = rows // n_dp

    messages = make_slots(expert_ids, gate_weights, tokens, grad_output, n_expert, n_y)
    got = exchange(messages, ("expert", "y"))

    own, own_in, own_out = clip_weights(messages, w_in, scale_in, w_out, scale_out)
    oth_in, oth_out = swap(own_in), swap(own_out)

    part, xdy, gate_rows, keep_in = gather(got, own, oth_in, oth_out)
    parts = exchange(part.reshape(n_dp, share, 3 * hidden), "dp")
    z = lax.axis_index("dp").astype(jnp.int32).reshape(1)
    copies = activate(z, parts, gate_rows, units)
    full = exchange(copies, "dp").reshape(rows, 3 * hidden)

    xdy_r = swap(xdy)
    returns, dh_oth, act_oth = scatter(xdy_r, full, own_in, keep_in, parties)
    back = exchange(returns, ("expert", "y"))
    grad_tokens = combine(expert_ids, back, tok_rows, width, n_expert, n_y)

    dh_r, act_r = swap(dh_oth), swap(act_oth)
    grad_in, grad_out = weight_grads(xdy, xdy_r, full, dh_r, act_r, w_in, scale_in, w_out, scale_out)
    return grad_tokens, grad_in[None], grad_out[None]


def solution(mesh):
    names = ("expert", "y", "core", "dp")
    n_expert, n_tensor, n_dp = (mesh.shape[a] for a in ("expert", "tensor", "dp"))
    fine = Mesh(mesh.devices.reshape(n_expert, n_tensor // CORES, CORES, n_dp), names)
    tensor = ("y", "core")
    block = ("expert", "y", "core")
    placed = (
        P(block, "dp"),
        P(block, "dp"),
        P(block, None),
        P(block, None),
        P("expert", "dp", tensor),
        P("expert", tensor),
        P("expert", tensor, "dp"),
        P("expert", "dp"),
    )
    return jax.shard_map(
        per_device,
        mesh=fine,
        in_specs=placed,
        out_specs=(P(block, "dp"), P("expert", "dp", tensor), P("expert", tensor, "dp")),
        check_vma=False,
    )
```

```python
import functools
import jax
import jax.numpy as jnp
from jax import lax
from jax.experimental import pallas as pl
from jax.experimental.pallas import tpu as pltpu
from jax.sharding import Mesh, PartitionSpec as P

CAP = 3
CORES = 2
LANE = 128
MIB = 1024 * 1024
ROOMY, SNUG, FULL = 28 * MIB, 51 * MIB, 60 * MIB
F32 = jnp.float32
BF16 = jnp.bfloat16


def swap(x):
    return lax.ppermute(x, "core", [(0, 1), (1, 0)])


def exchange(x, axes):
    return lax.all_to_all(x, axes, split_axis=0, concat_axis=0, tiled=True)


def dot(a, b, dims):
    return lax.dot_general(a, b, (dims, ((), ())), preferred_element_type=F32)


def up(n, m):
    return -(-n // m) * m


def routing(ids, n_expert):
    tok_rows, top = ids.shape
    at = lax.broadcasted_iota(jnp.int32, (n_expert, LANE), 0)
    seen = jnp.zeros((n_expert, LANE), jnp.int32)
    masks, named = [], []
    for i in range(tok_rows):
        hits = [jnp.broadcast_to(ids[i : i + 1, k : k + 1], at.shape) == at for k in range(top)]
        any_hit = functools.reduce(jnp.logical_or, hits)
        masks.append([any_hit & (seen == j) for j in range(CAP)])
        named.append(hits)
        seen = seen + any_hit.astype(jnp.int32)
    return masks, named


def start_all(pairs, sems, first=0):
    copies = [pltpu.make_async_copy(src, dst, sems.at[first + n]) for n, (src, dst) in enumerate(pairs)]
    for c in copies:
        c.start()
    return copies


def wait_all(copies):
    for c in copies:
        c.wait()


def slots_kernel(
    n_expert, n_y, size, ids_ref, gates_ref, tok_ref, cot_ref, out_ref, ids, gates, tok, cot, wide, narrow, sems
):
    tok_rows, width = tok.shape
    tiles = width // LANE
    copies = start_all([(ids_ref, ids), (gates_ref, gates), (tok_ref, tok), (cot_ref, cot)], sems)
    wide[...] = jnp.zeros_like(wide)
    wait_all(copies)
    masks, named = routing(ids[...], n_expert)
    gate = gates[...].astype(F32)
    lane = lax.broadcasted_iota(jnp.int32, (n_expert, LANE), 1)
    gate_row = jnp.zeros((n_expert, LANE), F32)
    for i in range(tok_rows):
        weight = jnp.zeros((n_expert, LANE), F32)
        for k, hit in enumerate(named[i]):
            weight = jnp.where(hit, jnp.broadcast_to(gate[i : i + 1, k : k + 1], hit.shape), weight)
        for j in range(CAP):
            gate_row = jnp.where(masks[i][j] & (lane == j), weight, gate_row)
    wide[pl.ds(2 * tiles * CAP, n_expert, stride=size), :] = gate_row
    both = [tok[...].astype(F32), cot[...].astype(F32)]
    for k in range(2 * tiles):
        at = (k % tiles) * LANE
        cols = both[k // tiles][:, at : at + LANE]
        for j in range(CAP):
            value = jnp.zeros((n_expert, LANE), F32)
            for i in range(tok_rows):
                value = jnp.where(masks[i][j], jnp.broadcast_to(cols[i : i + 1], value.shape), value)
            wide[pl.ds(j * 2 * tiles + k, n_expert, stride=size), :] = value
    narrow[...] = wide[...].reshape(n_expert, size, LANE).astype(BF16)
    wait_all(start_all([(narrow, out_ref.at[:, y]) for y in range(n_y)], sems, 4))


def gather_kernel(
    parties, size, got_ref, own_ref, oth_in_ref, oth_out_ref, part_ref, rows_ref, gate_ref,
    got, wide, own, oth, rows, part, gate, sems,
):
    width = own.shape[1]
    units = own.shape[0] - width
    tiles = width // LANE
    half = width + units
    copies = start_all(
        [
            (got_ref, got),
            (own_ref, own),
            (oth_in_ref, oth.at[0:width, :]),
            (oth_out_ref, oth.at[width:half, :]),
        ],
        sems,
    )
    copies[0].wait()
    wide[...] = got[...].astype(F32)
    gates = wide[pl.ds(2 * tiles * CAP, parties, stride=size), :]
    for j in range(CAP):
        at = slice(j * parties, (j + 1) * parties)
        gate[at, :] = jnp.broadcast_to(gates[:, j : j + 1], (parties, LANE))
        for k in range(2 * tiles):
            value = wide[pl.ds(j * 2 * tiles + k, parties, stride=size), :]
            rows[at, k * LANE : (k + 1) * LANE] = value.astype(BF16)
    outs = start_all([(rows, rows_ref), (gate, gate_ref)], sems, 4)
    for n, weights in enumerate((own, oth)):
        wait_all(copies[n + 1 : 2 + 2 * n])
        pre = dot(rows[:, :width], weights[:width, :], ((1,), (0,)))
        part[:, n * half : n * half + width] = pre.astype(BF16)
        back = dot(rows[:, width:], weights[width:, :], ((1,), (1,)))
        part[:, n * half + width : (n + 1) * half] = back.astype(BF16)
        cols = slice(n * half, (n + 1) * half)
        outs += start_all([(part.at[:, cols], part_ref.at[:, cols])], sems, 6 + n)
    wait_all(outs)


def clip_kernel(
    step, after_ref, w_in_ref, scale_in_ref, w_out_ref, scale_out_ref, own_ref, in_ref, out_ref,
    w_in, scale_in, w_out, scale_out, own, sems,
):
    del after_ref
    wait_all(
        start_all([(w_in_ref, w_in), (scale_in_ref, scale_in), (w_out_ref, w_out), (scale_out_ref, scale_out)], sems)
    )
    start = 0
    for weights, scales in ((w_in, scale_in), (w_out, scale_out)):
        bound = 448.0 * scales[...].astype(F32)
        for r in range(0, weights.shape[0], step):
            block = weights[r : r + step, :].astype(F32)
            own[start + r : start + r + step, :] = jnp.clip(block, -bound, bound).astype(BF16)
        start += weights.shape[0]
    tall = w_in.shape[0]
    wait_all(start_all([(own, own_ref), (own.at[0:tall, :], in_ref), (own.at[tall:start, :], out_ref)], sems, 4))


def activate_kernel(share, units, z_ref, parts_ref, gate_ref, out_ref, parts, gate, out, sems):
    n_dp = parts.shape[0]
    half = 3 * units
    at = pl.multiple_of(z_ref[0] * share, 8)
    halves = [slice(n * half, (n + 1) * half) for n in range(CORES)]
    copies = start_all(
        [(gate_ref.at[pl.ds(at, share), :], gate)] + [(parts_ref.at[:, :, h], parts.at[:, :, h]) for h in halves], sems
    )
    copies[0].wait()
    gates = gate[...]

    def total(at):
        value = parts[0, :, at : at + LANE].astype(F32)
        for p in range(1, n_dp):
            value = value + parts[p, :, at : at + LANE].astype(F32)
        return value

    outs = []
    for n in range(CORES):
        copies[1 + n].wait()
        for c in range(n * half, n * half + units, LANE):
            gate_pre = total(c)
            up_pre = total(c + units)
            d_act = gates * total(c + 2 * units)
            sigmoid_gate = jax.nn.sigmoid(gate_pre)
            silu_gate = gate_pre * sigmoid_gate
            slope = sigmoid_gate * (1.0 + gate_pre * (1.0 - sigmoid_gate))
            out[:, c : c + LANE] = (d_act * up_pre * slope).astype(BF16)
            out[:, c + units : c + units + LANE] = (d_act * silu_gate).astype(BF16)
            out[:, c + 2 * units : c + 2 * units + LANE] = (gates * silu_gate * up_pre).astype(BF16)
        pairs = [(out.at[:, halves[n]], out_ref.at[p, :, halves[n]]) for p in range(n_dp)]
        outs += start_all(pairs, sems, 1 + CORES + n * n_dp)
    wait_all(outs)


def place(n, ref):
    tiles = ref.shape[2] // LANE
    at = n % tiles * LANE
    return n // tiles, slice(at, at + LANE)


def scatter_kernel(
    parties, offset, after_ref, full_ref, own_ref, oth_ref, out_ref, dh_ref, act_ref, dh, act, own, oth, wide, out, sems
):
    del after_ref
    width = own.shape[0]
    hidden = own.shape[1]
    tiles = width // LANE
    copies = start_all(
        [
            (full_ref.at[:, 0:hidden], dh.at[0]),
            (own_ref.at[0:width, :], own),
            (full_ref.at[:, offset : offset + hidden], dh.at[1]),
            (oth_ref, oth),
            (full_ref.at[:, offset + hidden : 2 * offset], act),
        ],
        sems,
    )
    wait_all(copies[0:2])
    dx = dot(dh[0], own[...], ((1,), (1,)))
    wait_all(copies[2:4])
    copies[4].wait()
    outs = start_all([(dh.at[1], dh_ref), (act, act_ref)], sems, 5)
    dx = dx + dot(dh[1], oth[...], ((1,), (1,)))
    for j in range(CAP):
        for k in range(tiles):
            row, cols = place(j * tiles + k, wide)
            wide[:, row, cols] = dx[j * parties : (j + 1) * parties, k * LANE : (k + 1) * LANE]
    out[...] = wide[...].astype(BF16)
    wait_all(outs + start_all([(out, out_ref)], sems, 7))


def grads_kernel(step, *refs):
    n_in = 9
    sources, (in_ref, out_ref) = refs[:n_in], refs[n_in : n_in + 2]
    held, (in_v, out_v, sems) = refs[n_in + 2 : 2 * n_in + 2], refs[2 * n_in + 2 :]
    mine, theirs, full, dh, act, w_in, scale_in, w_out, scale_out = held
    half = full.shape[1]
    pairs = [(src.at[:, 0:half] if dst is full else src, dst) for src, dst in zip(sources, held)]
    wait_all(start_all(pairs, sems))
    width, hidden = w_in.shape
    outs = []
    for n, (weights, scales, grad, dst) in enumerate(((w_in, scale_in, in_v, in_ref), (w_out, scale_out, out_v, out_ref))):
        bound = 448.0 * scales[...].astype(F32)
        for r in range(0, weights.shape[0], step):
            at = slice(r, r + step)
            if grad is in_v:
                total = dot(mine[:, at], full[:, :hidden], ((0,), (0,)))
                total = total + dot(theirs[:, at], dh[...], ((0,), (0,)))
            else:
                total = dot(full[:, hidden + r : hidden + r + step], mine[:, width:], ((0,), (0,)))
                total = total + dot(act[:, at], theirs[:, width:], ((0,), (0,)))
            keep = jnp.abs(weights[at, :].astype(F32)) <= bound
            grad[at, :] = jnp.where(keep, total, 0.0).astype(BF16)
        outs += start_all([(grad, dst)], sems, n_in + n)
    wait_all(outs)


def combine_kernel(n_expert, n_y, ids_ref, back_ref, out_ref, ids, back, wide, out, sems):
    tok_rows, width = out.shape
    tiles = width // LANE
    copies = start_all([(ids_ref, ids), (back_ref, back)], sems)
    copies[0].wait()
    masks, _ = routing(ids[...], n_expert)
    copies[1].wait()
    wide[...] = back[...].astype(F32)
    for k in range(tiles):
        totals = [jnp.zeros((1, LANE), F32) for _ in range(tok_rows)]
        for j in range(CAP):
            row, cols = place(j * tiles + k, wide)
            value = wide[:, row, cols]
            value = jnp.sum(value.reshape(n_expert, n_y, LANE), axis=1)
            for i in range(tok_rows):
                totals[i] = totals[i] + jnp.sum(jnp.where(masks[i][j], value, 0.0), axis=0, keepdims=True)
        out[:, k * LANE : (k + 1) * LANE] = jnp.concatenate(totals, axis=0).astype(BF16)
    wait_all(start_all([(out, out_ref)], sems, 2))


ANY = pl.BlockSpec(memory_space=pl.ANY)
SMEM = pl.BlockSpec(memory_space=pltpu.SMEM)


def array(shape, dtype=BF16):
    return jax.ShapeDtypeStruct(shape, dtype)


def call(kernel, outs, scratch, n_sems, flops, moved, *args, limit=FULL):
    return pl.pallas_call(
        kernel,
        out_shape=outs,
        in_specs=[SMEM if a.shape == (1,) else ANY for a in args],
        out_specs=jax.tree.map(lambda _: ANY, outs),
        scratch_shapes=[pltpu.VMEM(*s) for s in scratch] + [pltpu.SemaphoreType.DMA((n_sems,))],
        compiler_params=pltpu.CompilerParams(vmem_limit_bytes=limit),
        cost_estimate=pl.CostEstimate(flops=flops, bytes_accessed=moved, transcendentals=0),
    )(*args)


def like(*arrays):
    return [(a.shape, a.dtype) for a in arrays]


def make_slots(ids, gates, tokens, cotangents, n_expert, n_y):
    size = up(2 * CAP * tokens.shape[1] // LANE + 1, 8)
    args = (ids, gates, tokens, cotangents)
    scratch = like(*args) + [((n_expert * size, LANE), F32), ((n_expert, size, LANE), BF16)]
    kernel = functools.partial(slots_kernel, n_expert, n_y, size)
    out = call(kernel, array((n_expert, n_y, size, LANE)), scratch, 4 + n_y, 1 << 20, 1 << 20, *args)
    return out.reshape(n_expert * n_y, size, LANE)


def clip_weights(after, w_in, scale_in, w_out, scale_out):
    width = w_in.shape[1]
    args = (w_in, scale_in, w_out, scale_out)
    heights = (w_in.shape[0] + w_out.shape[0], w_in.shape[0], w_out.shape[0])
    scratch = like(*args) + [((heights[0], width), BF16)]
    size = heights[0] * width
    kernel = functools.partial(clip_kernel, 64)
    return call(kernel, tuple(array((h, width)) for h in heights), scratch, 7, 4 * size, 4 * size, after, *args)


def activate(z, parts, gate_rows, units):
    n_dp, share, cols = parts.shape
    scratch = like(parts) + [((share, LANE), F32), ((share, cols), BF16)]
    kernel = functools.partial(activate_kernel, share, units)
    n_sems = 1 + CORES + CORES * n_dp
    return call(kernel, array(parts.shape), scratch, n_sems, 2 * parts.size, 4 * parts.size, z, parts, gate_rows, limit=ROOMY)


def gather(got, own, oth_in, oth_out):
    parties, size, _ = got.shape
    height, width = own.shape
    rows = parties * CAP
    flat = got.reshape(parties * size, LANE)
    shapes = (array((rows, 2 * height)), array((rows, 2 * width)), array((rows, LANE), F32))
    scratch = like(flat) + [(flat.shape, F32)] + like(own, own, shapes[1], shapes[0], shapes[2])
    kernel = functools.partial(gather_kernel, parties, size)
    moved = 4 * own.size + 6 * got.size
    return call(kernel, shapes, scratch, 6 + CORES, 4 * rows * own.size, moved, flat, own, oth_in, oth_out, limit=SNUG)


def scatter(after, full, own, oth, parties):
    rows = full.shape[0]
    height, width = own.shape
    hidden = width
    flat = array((parties, 2, CAP * width // 2))
    shapes = (flat, array((rows, hidden)), array((rows, height - width)))
    scratch = [((2, rows, hidden), BF16)] + like(shapes[2], oth, oth) + [(flat.shape, F32), (flat.shape, BF16)]
    kernel = functools.partial(scatter_kernel, parties, height)
    flops, moved = 4 * rows * width * hidden, 4 * own.size
    return call(kernel, shapes, scratch, 8, flops, moved, after, full, own, oth, limit=SNUG)


def weight_grads(mine, theirs, full, dh, act, w_in, scale_in, w_out, scale_out):
    shapes = (array(w_in.shape), array(w_out.shape))
    kernel = functools.partial(grads_kernel, 128)
    args = (mine, theirs, full, dh, act, w_in, scale_in, w_out, scale_out)
    held = like(*args)
    held[2] = ((full.shape[0], full.shape[1] // CORES), BF16)
    return call(kernel, shapes, held + like(*shapes), len(args) + 2, 1 << 20, 1 << 20, *args)


def combine(ids, back, tok_rows, width, n_expert, n_y):
    shape = array((tok_rows, width))
    scratch = like(ids, back) + [(back.shape, F32)] + like(shape)
    kernel = functools.partial(combine_kernel, n_expert, n_y)
    return call(kernel, shape, scratch, 3, 1 << 20, 1 << 20, ids, back, limit=ROOMY)


def per_device(tokens, grad_output, expert_ids, gate_weights, w_in, scale_in, w_out, scale_out):
    n_expert = lax.axis_size("expert")
    n_y = lax.axis_size("y")
    n_dp = lax.axis_size("dp")
    tok_rows, width = tokens.shape
    units = w_out.shape[1]
    hidden = 2 * units
    w_in, w_out = w_in[0], w_out[0]
    parties = n_expert * n_y
    rows = parties * CAP
    share = rows // n_dp

    messages = make_slots(expert_ids, gate_weights, tokens, grad_output, n_expert, n_y)
    got = exchange(messages, ("expert", "y"))

    own, own_in, own_out = clip_weights(messages, w_in, scale_in, w_out, scale_out)
    oth_in, oth_out = swap(own_in), swap(own_out)

    part, xdy, gate_rows = gather(got, own, oth_in, oth_out)
    parts = exchange(part.reshape(n_dp, share, 3 * hidden), "dp")
    z = lax.axis_index("dp").astype(jnp.int32).reshape(1)
    copies = activate(z, parts, gate_rows, units)
    full = exchange(copies, "dp").reshape(rows, 3 * hidden)

    xdy_r = swap(xdy)
    returns, dh_oth, act_oth = scatter(xdy_r, full, own, oth_in, parties)
    back = exchange(returns, ("expert", "y"))
    grad_tokens = combine(expert_ids, back, tok_rows, width, n_expert, n_y)

    dh_r, act_r = swap(dh_oth), swap(act_oth)
    grad_in, grad_out = weight_grads(xdy, xdy_r, full, dh_r, act_r, w_in, scale_in, w_out, scale_out)
    return grad_tokens, grad_in[None], grad_out[None]


def solution(mesh):
    names = ("expert", "y", "core", "dp")
    n_expert, n_tensor, n_dp = (mesh.shape[a] for a in ("expert", "tensor", "dp"))
    fine = Mesh(mesh.devices.reshape(n_expert, n_tensor // CORES, CORES, n_dp), names)
    tensor = ("y", "core")
    block = ("expert", "y", "core")
    placed = (
        P(block, "dp"),
        P(block, "dp"),
        P(block, None),
        P(block, None),
        P("expert", "dp", tensor),
        P("expert", tensor),
        P("expert", tensor, "dp"),
        P("expert", "dp"),
    )
    return jax.shard_map(
        per_device,
        mesh=fine,
        in_specs=placed,
        out_specs=(P(block, "dp"), P("expert", "dp", tensor), P("expert", tensor, "dp")),
        check_vma=False,
    )
```

```python
import functools
import jax
import jax.numpy as jnp
from jax import lax
from jax.experimental import pallas as pl
from jax.experimental.pallas import tpu as pltpu
from jax.sharding import Mesh, PartitionSpec as P

CAP = 3
CORES = 2
PIECES = 3
LANE = 128
MIB = 1024 * 1024
ROOMY, SNUG, FULL = 28 * MIB, 51 * MIB, 60 * MIB
F32 = jnp.float32
BF16 = jnp.bfloat16


def swap(x):
    return lax.ppermute(x, "core", [(0, 1), (1, 0)])


def exchange(x, axes):
    return lax.all_to_all(x, axes, split_axis=0, concat_axis=0, tiled=True)


def dot(a, b, dims):
    return lax.dot_general(a, b, (dims, ((), ())), preferred_element_type=F32)


def up(n, m):
    return -(-n // m) * m


def routing(ids, n_expert):
    tok_rows, top = ids.shape
    at = lax.broadcasted_iota(jnp.int32, (n_expert, LANE), 0)
    seen = jnp.zeros((n_expert, LANE), jnp.int32)
    masks, named = [], []
    for i in range(tok_rows):
        hits = [jnp.broadcast_to(ids[i : i + 1, k : k + 1], at.shape) == at for k in range(top)]
        any_hit = functools.reduce(jnp.logical_or, hits)
        masks.append([any_hit & (seen == j) for j in range(CAP)])
        named.append(hits)
        seen = seen + any_hit.astype(jnp.int32)
    return masks, named


def start_all(pairs, sems, first=0):
    copies = [pltpu.make_async_copy(src, dst, sems.at[first + n]) for n, (src, dst) in enumerate(pairs)]
    for c in copies:
        c.start()
    return copies


def wait_all(copies):
    for c in copies:
        c.wait()


def slots_kernel(
    n_expert, n_y, size, ids_ref, gates_ref, tok_ref, cot_ref, out_ref, ids, gates, tok, cot, wide, narrow, sems
):
    tok_rows, width = tok.shape
    tiles = width // LANE
    copies = start_all([(ids_ref, ids), (gates_ref, gates), (tok_ref, tok), (cot_ref, cot)], sems)
    wide[...] = jnp.zeros_like(wide)
    wait_all(copies)
    masks, named = routing(ids[...], n_expert)
    gate = gates[...].astype(F32)
    lane = lax.broadcasted_iota(jnp.int32, (n_expert, LANE), 1)
    gate_row = jnp.zeros((n_expert, LANE), F32)
    for i in range(tok_rows):
        weight = jnp.zeros((n_expert, LANE), F32)
        for k, hit in enumerate(named[i]):
            weight = jnp.where(hit, jnp.broadcast_to(gate[i : i + 1, k : k + 1], hit.shape), weight)
        for j in range(CAP):
            gate_row = jnp.where(masks[i][j] & (lane == j), weight, gate_row)
    wide[pl.ds(2 * tiles * CAP, n_expert, stride=size), :] = gate_row
    both = [tok[...].astype(F32), cot[...].astype(F32)]
    for k in range(2 * tiles):
        at = (k % tiles) * LANE
        cols = both[k // tiles][:, at : at + LANE]
        for j in range(CAP):
            value = jnp.zeros((n_expert, LANE), F32)
            for i in range(tok_rows):
                value = jnp.where(masks[i][j], jnp.broadcast_to(cols[i : i + 1], value.shape), value)
            wide[pl.ds(j * 2 * tiles + k, n_expert, stride=size), :] = value
    narrow[...] = wide[...].reshape(n_expert, size, LANE).astype(BF16)
    wait_all(start_all([(narrow, out_ref.at[:, y]) for y in range(n_y)], sems, 4))


def gather_kernel(
    parties, size, got_ref, own_ref, oth_in_ref, oth_out_ref, part_ref, rows_ref, gate_ref,
    got, wide, own, oth, rows, part, gate, sems,
):
    width = own.shape[1]
    units = own.shape[0] - width
    tiles = width // LANE
    half = width + units
    copies = start_all([(got_ref, got), (own_ref, own)], sems)
    copies[0].wait()
    wide[...] = got[...].astype(F32)
    copies += start_all([(oth_in_ref, oth.at[0:width, :]), (oth_out_ref, oth.at[width:half, :])], sems, 2)
    gates = wide[pl.ds(2 * tiles * CAP, parties, stride=size), :]
    for j in range(CAP):
        at = slice(j * parties, (j + 1) * parties)
        gate[at, :] = jnp.broadcast_to(gates[:, j : j + 1], (parties, LANE))
        for k in range(2 * tiles):
            value = wide[pl.ds(j * 2 * tiles + k, parties, stride=size), :]
            rows[at, k * LANE : (k + 1) * LANE] = value.astype(BF16)
    outs = start_all([(rows, rows_ref), (gate, gate_ref)], sems, 4)
    for n, weights in enumerate((own, oth)):
        wait_all(copies[n + 1 : 2 + 2 * n])
        pre = dot(rows[:, :width], weights[:width, :], ((1,), (0,)))
        part[:, n * half : n * half + width] = pre.astype(BF16)
        back = dot(rows[:, width:], weights[width:, :], ((1,), (1,)))
        part[:, n * half + width : (n + 1) * half] = back.astype(BF16)
        cols = slice(n * half, (n + 1) * half)
        outs += start_all([(part.at[:, cols], part_ref.at[:, cols])], sems, 6 + n)
    wait_all(outs)


def clip_kernel(
    step, after_ref, w_in_ref, scale_in_ref, w_out_ref, scale_out_ref, own_ref, in_ref, out_ref,
    w_in, scale_in, w_out, scale_out, own, sems,
):
    del after_ref
    wait_all(
        start_all([(w_in_ref, w_in), (scale_in_ref, scale_in), (w_out_ref, w_out), (scale_out_ref, scale_out)], sems)
    )
    start = 0
    for weights, scales in ((w_in, scale_in), (w_out, scale_out)):
        bound = 448.0 * scales[...].astype(F32)
        for r in range(0, weights.shape[0], step):
            block = weights[r : r + step, :].astype(F32)
            own[start + r : start + r + step, :] = jnp.clip(block, -bound, bound).astype(BF16)
        start += weights.shape[0]
    tall = w_in.shape[0]
    wait_all(start_all([(own, own_ref), (own.at[0:tall, :], in_ref), (own.at[tall:start, :], out_ref)], sems, 4))


def activate_kernel(share, units, z_ref, parts_ref, gate_ref, out_ref, parts, gate, out, sems):
    n_dp = parts.shape[0]
    half = 3 * units
    at = pl.multiple_of(z_ref[0] * share, 8)
    halves = [slice(n * half, (n + 1) * half) for n in range(CORES)]
    copies = start_all(
        [(gate_ref.at[pl.ds(at, share), :], gate)] + [(parts_ref.at[:, :, h], parts.at[:, :, h]) for h in halves], sems
    )
    copies[0].wait()
    gates = gate[...]

    def total(at):
        value = parts[0, :, at : at + LANE].astype(F32)
        for p in range(1, n_dp):
            value = value + parts[p, :, at : at + LANE].astype(F32)
        return value

    outs = []
    for n in range(CORES):
        copies[1 + n].wait()
        for c in range(n * half, n * half + units, LANE):
            gate_pre = total(c)
            up_pre = total(c + units)
            d_act = gates * total(c + 2 * units)
            sigmoid_gate = jax.nn.sigmoid(gate_pre)
            silu_gate = gate_pre * sigmoid_gate
            slope = sigmoid_gate * (1.0 + gate_pre * (1.0 - sigmoid_gate))
            out[:, c : c + LANE] = (d_act * up_pre * slope).astype(BF16)
            out[:, c + units : c + units + LANE] = (d_act * silu_gate).astype(BF16)
            out[:, c + 2 * units : c + 2 * units + LANE] = (gates * silu_gate * up_pre).astype(BF16)
        pairs = [(out.at[:, halves[n]], out_ref.at[p, :, halves[n]]) for p in range(n_dp)]
        outs += start_all(pairs, sems, 1 + CORES + n * n_dp)
    wait_all(outs)


def place(n, ref):
    tiles = ref.shape[2] // LANE
    at = n % tiles * LANE
    return n // tiles, slice(at, at + LANE)


def scatter_kernel(
    parties, offset, after_ref, full_ref, own_ref, oth_ref, out_ref, dh_ref, act_ref, dh, act, own, oth, wide, out, sems
):
    del after_ref
    width = own.shape[0]
    hidden = own.shape[1]
    tiles = width // LANE
    step = width // PIECES
    copies = start_all(
        [
            (full_ref.at[:, 0:hidden], dh.at[0]),
            (full_ref.at[:, offset : offset + hidden], dh.at[1]),
            (full_ref.at[:, offset + hidden : 2 * offset], act),
        ],
        sems,
    )
    spans = [slice(p * step, (p + 1) * step) for p in range(PIECES)]
    pieces = [
        start_all([(own_ref.at[at, :], own.at[at, :]), (oth_ref.at[at, :], oth.at[at, :])], sems, 3 + 2 * p)
        for p, at in enumerate(spans)
    ]
    wait_all(copies)
    outs = start_all([(dh.at[1], dh_ref), (act, act_ref)], sems, 3 + 2 * PIECES)
    for p, at in enumerate(spans):
        wait_all(pieces[p])
        dx = dot(dh[0], own[at, :], ((1,), (1,))) + dot(dh[1], oth[at, :], ((1,), (1,)))
        for j in range(CAP):
            for k in range(step // LANE):
                row, cols = place(j * tiles + p * (step // LANE) + k, wide)
                wide[:, row, cols] = dx[j * parties : (j + 1) * parties, k * LANE : (k + 1) * LANE]
    out[...] = wide[...].astype(BF16)
    wait_all(outs + start_all([(out, out_ref)], sems, 5 + 2 * PIECES))


def grads_kernel(step, *refs):
    n_in = 9
    sources, (in_ref, out_ref) = refs[:n_in], refs[n_in : n_in + 2]
    held, (in_v, out_v, sems) = refs[n_in + 2 : 2 * n_in + 2], refs[2 * n_in + 2 :]
    mine, theirs, full, dh, act, w_in, scale_in, w_out, scale_out = held
    half = full.shape[1]
    pairs = [(src.at[:, 0:half] if dst is full else src, dst) for src, dst in zip(sources, held)]
    wait_all(start_all(pairs, sems))
    width, hidden = w_in.shape
    outs = []
    for n, (weights, scales, grad, dst) in enumerate(((w_in, scale_in, in_v, in_ref), (w_out, scale_out, out_v, out_ref))):
        bound = 448.0 * scales[...].astype(F32)
        for r in range(0, weights.shape[0], step):
            at = slice(r, r + step)
            if grad is in_v:
                total = dot(mine[:, at], full[:, :hidden], ((0,), (0,)))
                total = total + dot(theirs[:, at], dh[...], ((0,), (0,)))
            else:
                total = dot(full[:, hidden + r : hidden + r + step], mine[:, width:], ((0,), (0,)))
                total = total + dot(act[:, at], theirs[:, width:], ((0,), (0,)))
            keep = jnp.abs(weights[at, :].astype(F32)) <= bound
            grad[at, :] = jnp.where(keep, total, 0.0).astype(BF16)
        outs += start_all([(grad, dst)], sems, n_in + n)
    wait_all(outs)


def combine_kernel(n_expert, n_y, ids_ref, back_ref, out_ref, ids, back, wide, out, sems):
    tok_rows, width = out.shape
    tiles = width // LANE
    copies = start_all([(ids_ref, ids), (back_ref, back)], sems)
    copies[0].wait()
    masks, _ = routing(ids[...], n_expert)
    copies[1].wait()
    wide[...] = back[...].astype(F32)
    for k in range(tiles):
        totals = [jnp.zeros((1, LANE), F32) for _ in range(tok_rows)]
        for j in range(CAP):
            row, cols = place(j * tiles + k, wide)
            value = wide[:, row, cols]
            value = jnp.sum(value.reshape(n_expert, n_y, LANE), axis=1)
            for i in range(tok_rows):
                totals[i] = totals[i] + jnp.sum(jnp.where(masks[i][j], value, 0.0), axis=0, keepdims=True)
        out[:, k * LANE : (k + 1) * LANE] = jnp.concatenate(totals, axis=0).astype(BF16)
    wait_all(start_all([(out, out_ref)], sems, 2))


ANY = pl.BlockSpec(memory_space=pl.ANY)
SMEM = pl.BlockSpec(memory_space=pltpu.SMEM)


def array(shape, dtype=BF16):
    return jax.ShapeDtypeStruct(shape, dtype)


def call(kernel, outs, scratch, n_sems, flops, moved, *args, limit=FULL):
    return pl.pallas_call(
        kernel,
        out_shape=outs,
        in_specs=[SMEM if a.shape == (1,) else ANY for a in args],
        out_specs=jax.tree.map(lambda _: ANY, outs),
        scratch_shapes=[pltpu.VMEM(*s) for s in scratch] + [pltpu.SemaphoreType.DMA((n_sems,))],
        compiler_params=pltpu.CompilerParams(vmem_limit_bytes=limit),
        cost_estimate=pl.CostEstimate(flops=flops, bytes_accessed=moved, transcendentals=0),
    )(*args)


def like(*arrays):
    return [(a.shape, a.dtype) for a in arrays]


def make_slots(ids, gates, tokens, cotangents, n_expert, n_y):
    size = up(2 * CAP * tokens.shape[1] // LANE + 1, 8)
    args = (ids, gates, tokens, cotangents)
    scratch = like(*args) + [((n_expert * size, LANE), F32), ((n_expert, size, LANE), BF16)]
    kernel = functools.partial(slots_kernel, n_expert, n_y, size)
    out = call(kernel, array((n_expert, n_y, size, LANE)), scratch, 4 + n_y, 1 << 20, 1 << 20, *args)
    return out.reshape(n_expert * n_y, size, LANE)


def clip_weights(after, w_in, scale_in, w_out, scale_out):
    width = w_in.shape[1]
    args = (w_in, scale_in, w_out, scale_out)
    heights = (w_in.shape[0] + w_out.shape[0], w_in.shape[0], w_out.shape[0])
    scratch = like(*args) + [((heights[0], width), BF16)]
    size = heights[0] * width
    kernel = functools.partial(clip_kernel, 64)
    return call(kernel, tuple(array((h, width)) for h in heights), scratch, 7, 4 * size, 4 * size, after, *args)


def activate(z, parts, gate_rows, units):
    n_dp, share, cols = parts.shape
    scratch = like(parts) + [((share, LANE), F32), ((share, cols), BF16)]
    kernel = functools.partial(activate_kernel, share, units)
    n_sems = 1 + CORES + CORES * n_dp
    return call(kernel, array(parts.shape), scratch, n_sems, 2 * parts.size, 4 * parts.size, z, parts, gate_rows, limit=ROOMY)


def gather(got, own, oth_in, oth_out):
    parties, size, _ = got.shape
    height, width = own.shape
    rows = parties * CAP
    flat = got.reshape(parties * size, LANE)
    shapes = (array((rows, 2 * height)), array((rows, 2 * width)), array((rows, LANE), F32))
    scratch = like(flat) + [(flat.shape, F32)] + like(own, own, shapes[1], shapes[0], shapes[2])
    kernel = functools.partial(gather_kernel, parties, size)
    moved = 4 * own.size + 6 * got.size
    return call(kernel, shapes, scratch, 6 + CORES, 4 * rows * own.size, moved, flat, own, oth_in, oth_out, limit=SNUG)


def scatter(after, full, own, oth, parties):
    rows = full.shape[0]
    height, width = own.shape
    hidden = width
    flat = array((parties, 2, CAP * width // 2))
    shapes = (flat, array((rows, hidden)), array((rows, height - width)))
    scratch = [((2, rows, hidden), BF16)] + like(shapes[2], oth, oth) + [(flat.shape, F32), (flat.shape, BF16)]
    kernel = functools.partial(scatter_kernel, parties, height)
    flops, moved = 4 * rows * width * hidden, 4 * own.size
    return call(kernel, shapes, scratch, 6 + 2 * PIECES, flops, moved, after, full, own, oth, limit=SNUG)


def weight_grads(mine, theirs, full, dh, act, w_in, scale_in, w_out, scale_out):
    shapes = (array(w_in.shape), array(w_out.shape))
    kernel = functools.partial(grads_kernel, 128)
    args = (mine, theirs, full, dh, act, w_in, scale_in, w_out, scale_out)
    held = like(*args)
    held[2] = ((full.shape[0], full.shape[1] // CORES), BF16)
    return call(kernel, shapes, held + like(*shapes), len(args) + 2, 1 << 20, 1 << 20, *args, limit=SNUG)


def combine(ids, back, tok_rows, width, n_expert, n_y):
    shape = array((tok_rows, width))
    scratch = like(ids, back) + [(back.shape, F32)] + like(shape)
    kernel = functools.partial(combine_kernel, n_expert, n_y)
    return call(kernel, shape, scratch, 3, 1 << 20, 1 << 20, ids, back, limit=ROOMY)


def per_device(tokens, grad_output, expert_ids, gate_weights, w_in, scale_in, w_out, scale_out):
    n_expert = lax.axis_size("expert")
    n_y = lax.axis_size("y")
    n_dp = lax.axis_size("dp")
    tok_rows, width = tokens.shape
    units = w_out.shape[1]
    hidden = 2 * units
    w_in, w_out = w_in[0], w_out[0]
    parties = n_expert * n_y
    rows = parties * CAP
    share = rows // n_dp

    messages = make_slots(expert_ids, gate_weights, tokens, grad_output, n_expert, n_y)
    got = exchange(messages, ("expert", "y"))

    own, own_in, own_out = clip_weights(messages, w_in, scale_in, w_out, scale_out)
    oth_in, oth_out = swap(own_in), swap(own_out)

    part, xdy, gate_rows = gather(got, own, oth_in, oth_out)
    parts = exchange(part.reshape(n_dp, share, 3 * hidden), "dp")
    z = lax.axis_index("dp").astype(jnp.int32).reshape(1)
    copies = activate(z, parts, gate_rows, units)
    full = exchange(copies, "dp").reshape(rows, 3 * hidden)

    xdy_r = swap(xdy)
    returns, dh_oth, act_oth = scatter(xdy_r, full, own, oth_in, parties)
    back = exchange(returns, ("expert", "y"))
    grad_tokens = combine(expert_ids, back, tok_rows, width, n_expert, n_y)

    dh_r, act_r = swap(dh_oth), swap(act_oth)
    grad_in, grad_out = weight_grads(xdy, xdy_r, full, dh_r, act_r, w_in, scale_in, w_out, scale_out)
    return grad_tokens, grad_in[None], grad_out[None]


def solution(mesh):
    names = ("expert", "y", "core", "dp")
    n_expert, n_tensor, n_dp = (mesh.shape[a] for a in ("expert", "tensor", "dp"))
    fine = Mesh(mesh.devices.reshape(n_expert, n_tensor // CORES, CORES, n_dp), names)
    tensor = ("y", "core")
    block = ("expert", "y", "core")
    placed = (
        P(block, "dp"),
        P(block, "dp"),
        P(block, None),
        P(block, None),
        P("expert", "dp", tensor),
        P("expert", tensor),
        P("expert", tensor, "dp"),
        P("expert", "dp"),
    )
    return jax.shard_map(
        per_device,
        mesh=fine,
        in_specs=placed,
        out_specs=(P(block, "dp"), P("expert", "dp", tensor), P("expert", tensor, "dp")),
        check_vma=False,
    )
```

```python
import functools
import jax
import jax.numpy as jnp
from jax import lax
from jax.experimental import pallas as pl
from jax.experimental.pallas import tpu as pltpu
from jax.sharding import Mesh, PartitionSpec as P

CAP = 3
CORES = 2
PIECES = 3
LANE = 128
MIB = 1024 * 1024
ROOMY, SNUG, FULL = 28 * MIB, 51 * MIB, 60 * MIB
F32 = jnp.float32
BF16 = jnp.bfloat16


def swap(x):
    return lax.ppermute(x, "core", [(0, 1), (1, 0)])


def exchange(x, axes):
    return lax.all_to_all(x, axes, split_axis=0, concat_axis=0, tiled=True)


def dot(a, b, dims):
    return lax.dot_general(a, b, (dims, ((), ())), preferred_element_type=F32)


def up(n, m):
    return -(-n // m) * m


def routing(ids, n_expert):
    tok_rows, top = ids.shape
    at = lax.broadcasted_iota(jnp.int32, (n_expert, LANE), 0)
    seen = jnp.zeros((n_expert, LANE), jnp.int32)
    masks, named = [], []
    for i in range(tok_rows):
        hits = [jnp.broadcast_to(ids[i : i + 1, k : k + 1], at.shape) == at for k in range(top)]
        any_hit = functools.reduce(jnp.logical_or, hits)
        masks.append([any_hit & (seen == j) for j in range(CAP)])
        named.append(hits)
        seen = seen + any_hit.astype(jnp.int32)
    return masks, named


def start_all(pairs, sems, first=0):
    copies = [pltpu.make_async_copy(src, dst, sems.at[first + n]) for n, (src, dst) in enumerate(pairs)]
    for c in copies:
        c.start()
    return copies


def wait_all(copies):
    for c in copies:
        c.wait()


def slots_kernel(
    n_expert, n_y, size, ids_ref, gates_ref, tok_ref, cot_ref, out_ref, ids, gates, tok, cot, wide, narrow, sems
):
    tok_rows, width = tok.shape
    tiles = width // LANE
    copies = start_all([(ids_ref, ids), (gates_ref, gates), (tok_ref, tok), (cot_ref, cot)], sems)
    wide[...] = jnp.zeros_like(wide)
    wait_all(copies)
    masks, named = routing(ids[...], n_expert)
    gate = gates[...].astype(F32)
    lane = lax.broadcasted_iota(jnp.int32, (n_expert, LANE), 1)
    gate_row = jnp.zeros((n_expert, LANE), F32)
    for i in range(tok_rows):
        weight = jnp.zeros((n_expert, LANE), F32)
        for k, hit in enumerate(named[i]):
            weight = jnp.where(hit, jnp.broadcast_to(gate[i : i + 1, k : k + 1], hit.shape), weight)
        for j in range(CAP):
            gate_row = jnp.where(masks[i][j] & (lane == j), weight, gate_row)
    wide[pl.ds(2 * tiles * CAP, n_expert, stride=size), :] = gate_row
    both = [tok[...].astype(F32), cot[...].astype(F32)]
    for k in range(2 * tiles):
        at = (k % tiles) * LANE
        cols = both[k // tiles][:, at : at + LANE]
        for j in range(CAP):
            value = jnp.zeros((n_expert, LANE), F32)
            for i in range(tok_rows):
                value = jnp.where(masks[i][j], jnp.broadcast_to(cols[i : i + 1], value.shape), value)
            wide[pl.ds(j * 2 * tiles + k, n_expert, stride=size), :] = value
    narrow[...] = wide[...].reshape(n_expert, size, LANE).astype(BF16)
    wait_all(start_all([(narrow, out_ref.at[:, y]) for y in range(n_y)], sems, 4))


def gather_kernel(
    parties, size, got_ref, own_ref, oth_in_ref, oth_out_ref, part_ref, rows_ref, gate_ref,
    got, wide, own, oth, x, dy, part, gate, sems,
):
    width = own.shape[1]
    units = own.shape[0] - width
    tiles = width // LANE
    half = width + units
    copies = start_all([(got_ref, got), (own_ref, own)], sems)
    copies[0].wait()
    wide[...] = got[...].astype(F32)
    copies += start_all([(oth_in_ref, oth.at[0:width, :]), (oth_out_ref, oth.at[width:half, :])], sems, 2)
    for q, rows in enumerate((x, dy)):
        for j in range(CAP):
            for k in range(tiles):
                value = wide[pl.ds((2 * j + q) * tiles + k, parties, stride=size), :]
                rows[j * parties : (j + 1) * parties, k * LANE : (k + 1) * LANE] = value.astype(BF16)
    gates = wide[pl.ds(2 * tiles * CAP, parties, stride=size), :]
    for j in range(CAP):
        gate[j * parties : (j + 1) * parties, :] = jnp.broadcast_to(gates[:, j : j + 1], (parties, LANE))
    outs = start_all([(x, rows_ref.at[:, 0:width]), (dy, rows_ref.at[:, width : 2 * width]), (gate, gate_ref)], sems, 4)
    for n, weights in enumerate((own, oth)):
        wait_all(copies[n + 1 : 2 + 2 * n])
        for q in range(2):
            if q == 0:
                value, at = dot(x[...], weights[:width, :], ((1,), (0,))), n * half
            else:
                value, at = dot(dy[...], weights[width:, :], ((1,), (1,))), n * half + width
            cols = slice(at, at + value.shape[1])
            part[:, cols] = value.astype(BF16)
            outs += start_all([(part.at[:, cols], part_ref.at[:, cols])], sems, 7 + 2 * n + q)
    wait_all(outs)


def clip_kernel(
    step, after_ref, w_in_ref, scale_in_ref, w_out_ref, scale_out_ref, own_ref, in_ref, out_ref,
    w_in, scale_in, w_out, scale_out, own, sems,
):
    del after_ref
    wait_all(
        start_all([(w_in_ref, w_in), (scale_in_ref, scale_in), (w_out_ref, w_out), (scale_out_ref, scale_out)], sems)
    )
    start = 0
    for weights, scales in ((w_in, scale_in), (w_out, scale_out)):
        bound = 448.0 * scales[...].astype(F32)
        for r in range(0, weights.shape[0], step):
            block = weights[r : r + step, :].astype(F32)
            own[start + r : start + r + step, :] = jnp.clip(block, -bound, bound).astype(BF16)
        start += weights.shape[0]
    tall = w_in.shape[0]
    wait_all(start_all([(own, own_ref), (own.at[0:tall, :], in_ref), (own.at[tall:start, :], out_ref)], sems, 4))


def activate_kernel(share, units, z_ref, parts_ref, gate_ref, out_ref, parts, gate, out, sems):
    n_dp = parts.shape[0]
    half = 3 * units
    at = pl.multiple_of(z_ref[0] * share, 8)
    halves = [slice(n * half, (n + 1) * half) for n in range(CORES)]
    copies = start_all(
        [(gate_ref.at[pl.ds(at, share), :], gate)] + [(parts_ref.at[:, :, h], parts.at[:, :, h]) for h in halves], sems
    )
    copies[0].wait()
    gates = gate[...]

    def total(at):
        value = parts[0, :, at : at + LANE].astype(F32)
        for p in range(1, n_dp):
            value = value + parts[p, :, at : at + LANE].astype(F32)
        return value

    outs = []
    for n in range(CORES):
        copies[1 + n].wait()
        for c in range(n * half, n * half + units, LANE):
            gate_pre = total(c)
            up_pre = total(c + units)
            d_act = gates * total(c + 2 * units)
            sigmoid_gate = jax.nn.sigmoid(gate_pre)
            silu_gate = gate_pre * sigmoid_gate
            slope = sigmoid_gate * (1.0 + gate_pre * (1.0 - sigmoid_gate))
            out[:, c : c + LANE] = (d_act * up_pre * slope).astype(BF16)
            out[:, c + units : c + units + LANE] = (d_act * silu_gate).astype(BF16)
            out[:, c + 2 * units : c + 2 * units + LANE] = (gates * silu_gate * up_pre).astype(BF16)
        pairs = [(out.at[:, halves[n]], out_ref.at[p, :, halves[n]]) for p in range(n_dp)]
        outs += start_all(pairs, sems, 1 + CORES + n * n_dp)
    wait_all(outs)


def place(n, ref):
    tiles = ref.shape[2] // LANE
    at = n % tiles * LANE
    return n // tiles, slice(at, at + LANE)


def scatter_kernel(
    parties, offset, after_ref, full_ref, own_ref, oth_ref, out_ref, dh_ref, act_ref, dh, act, own, oth, wide, out, sems
):
    del after_ref
    width = own.shape[0]
    hidden = own.shape[1]
    tiles = width // LANE
    step = width // PIECES
    copies = start_all(
        [
            (full_ref.at[:, 0:hidden], dh.at[0]),
            (full_ref.at[:, offset : offset + hidden], dh.at[1]),
            (full_ref.at[:, offset + hidden : 2 * offset], act),
        ],
        sems,
    )
    spans = [slice(p * step, (p + 1) * step) for p in range(PIECES)]
    pieces = [
        start_all([(own_ref.at[at, :], own.at[at, :]), (oth_ref.at[at, :], oth.at[at, :])], sems, 3 + 2 * p)
        for p, at in enumerate(spans)
    ]
    wait_all(copies)
    outs = start_all([(dh.at[1], dh_ref), (act, act_ref)], sems, 3 + 2 * PIECES)
    for p, at in enumerate(spans):
        wait_all(pieces[p])
        dx = dot(dh[0], own[at, :], ((1,), (1,))) + dot(dh[1], oth[at, :], ((1,), (1,)))
        for j in range(CAP):
            for k in range(step // LANE):
                row, cols = place(j * tiles + p * (step // LANE) + k, wide)
                wide[:, row, cols] = dx[j * parties : (j + 1) * parties, k * LANE : (k + 1) * LANE]
    out[...] = wide[...].astype(BF16)
    wait_all(outs + start_all([(out, out_ref)], sems, 5 + 2 * PIECES))


def grads_kernel(step, *refs):
    n_in = 9
    sources, (in_ref, out_ref) = refs[:n_in], refs[n_in : n_in + 2]
    held, (in_v, out_v, sems) = refs[n_in + 2 : 2 * n_in + 2], refs[2 * n_in + 2 :]
    mine, theirs, full, dh, act, w_in, scale_in, w_out, scale_out = held
    half = full.shape[1]
    pairs = [(src.at[:, 0:half] if dst is full else src, dst) for src, dst in zip(sources, held)]
    wait_all(start_all(pairs, sems))
    width, hidden = w_in.shape
    outs = []
    for n, (weights, scales, grad, dst) in enumerate(((w_in, scale_in, in_v, in_ref), (w_out, scale_out, out_v, out_ref))):
        bound = 448.0 * scales[...].astype(F32)
        for r in range(0, weights.shape[0], step):
            at = slice(r, r + step)
            if grad is in_v:
                total = dot(mine[:, at], full[:, :hidden], ((0,), (0,)))
                total = total + dot(theirs[:, at], dh[...], ((0,), (0,)))
            else:
                total = dot(full[:, hidden + r : hidden + r + step], mine[:, width:], ((0,), (0,)))
                total = total + dot(act[:, at], theirs[:, width:], ((0,), (0,)))
            keep = jnp.abs(weights[at, :].astype(F32)) <= bound
            grad[at, :] = jnp.where(keep, total, 0.0).astype(BF16)
        outs += start_all([(grad, dst)], sems, n_in + n)
    wait_all(outs)


def combine_kernel(n_expert, n_y, ids_ref, back_ref, out_ref, ids, back, wide, out, sems):
    tok_rows, width = out.shape
    tiles = width // LANE
    copies = start_all([(ids_ref, ids), (back_ref, back)], sems)
    copies[0].wait()
    masks, _ = routing(ids[...], n_expert)
    copies[1].wait()
    wide[...] = back[...].astype(F32)
    for k in range(tiles):
        totals = [jnp.zeros((1, LANE), F32) for _ in range(tok_rows)]
        for j in range(CAP):
            row, cols = place(j * tiles + k, wide)
            value = wide[:, row, cols]
            value = jnp.sum(value.reshape(n_expert, n_y, LANE), axis=1)
            for i in range(tok_rows):
                totals[i] = totals[i] + jnp.sum(jnp.where(masks[i][j], value, 0.0), axis=0, keepdims=True)
        out[:, k * LANE : (k + 1) * LANE] = jnp.concatenate(totals, axis=0).astype(BF16)
    wait_all(start_all([(out, out_ref)], sems, 2))


ANY = pl.BlockSpec(memory_space=pl.ANY)
SMEM = pl.BlockSpec(memory_space=pltpu.SMEM)


def array(shape, dtype=BF16):
    return jax.ShapeDtypeStruct(shape, dtype)


def call(kernel, outs, scratch, n_sems, flops, moved, *args, limit=FULL):
    return pl.pallas_call(
        kernel,
        out_shape=outs,
        in_specs=[SMEM if a.shape == (1,) else ANY for a in args],
        out_specs=jax.tree.map(lambda _: ANY, outs),
        scratch_shapes=[pltpu.VMEM(*s) for s in scratch] + [pltpu.SemaphoreType.DMA((n_sems,))],
        compiler_params=pltpu.CompilerParams(vmem_limit_bytes=limit),
        cost_estimate=pl.CostEstimate(flops=flops, bytes_accessed=moved, transcendentals=0),
    )(*args)


def like(*arrays):
    return [(a.shape, a.dtype) for a in arrays]


def make_slots(ids, gates, tokens, cotangents, n_expert, n_y):
    size = up(2 * CAP * tokens.shape[1] // LANE + 1, 8)
    args = (ids, gates, tokens, cotangents)
    scratch = like(*args) + [((n_expert * size, LANE), F32), ((n_expert, size, LANE), BF16)]
    kernel = functools.partial(slots_kernel, n_expert, n_y, size)
    out = call(kernel, array((n_expert, n_y, size, LANE)), scratch, 4 + n_y, 1 << 20, 1 << 20, *args)
    return out.reshape(n_expert * n_y, size, LANE)


def clip_weights(after, w_in, scale_in, w_out, scale_out):
    width = w_in.shape[1]
    args = (w_in, scale_in, w_out, scale_out)
    heights = (w_in.shape[0] + w_out.shape[0], w_in.shape[0], w_out.shape[0])
    scratch = like(*args) + [((heights[0], width), BF16)]
    size = heights[0] * width
    kernel = functools.partial(clip_kernel, 64)
    return call(kernel, tuple(array((h, width)) for h in heights), scratch, 7, 4 * size, 4 * size, after, *args)


def activate(z, parts, gate_rows, units):
    n_dp, share, cols = parts.shape
    scratch = like(parts) + [((share, LANE), F32), ((share, cols), BF16)]
    kernel = functools.partial(activate_kernel, share, units)
    n_sems = 1 + CORES + CORES * n_dp
    return call(kernel, array(parts.shape), scratch, n_sems, 2 * parts.size, 4 * parts.size, z, parts, gate_rows, limit=ROOMY)


def gather(got, own, oth_in, oth_out):
    parties, size, _ = got.shape
    height, width = own.shape
    rows = parties * CAP
    flat = got.reshape(parties * size, LANE)
    shapes = (array((rows, 2 * height)), array((rows, 2 * width)), array((rows, LANE), F32))
    half = ((rows, width), BF16)
    scratch = like(flat) + [(flat.shape, F32)] + like(own, own) + [half, half] + like(shapes[0], shapes[2])
    kernel = functools.partial(gather_kernel, parties, size)
    moved = 4 * own.size + 6 * got.size
    return call(kernel, shapes, scratch, 7 + 2 * CORES, 4 * rows * own.size, moved, flat, own, oth_in, oth_out, limit=SNUG)


def scatter(after, full, own, oth, parties):
    rows = full.shape[0]
    height, width = own.shape
    hidden = width
    flat = array((parties, 2, CAP * width // 2))
    shapes = (flat, array((rows, hidden)), array((rows, height - width)))
    scratch = [((2, rows, hidden), BF16)] + like(shapes[2], oth, oth) + [(flat.shape, F32), (flat.shape, BF16)]
    kernel = functools.partial(scatter_kernel, parties, height)
    flops, moved = 4 * rows * width * hidden, 4 * own.size
    return call(kernel, shapes, scratch, 6 + 2 * PIECES, flops, moved, after, full, own, oth, limit=SNUG)


def weight_grads(mine, theirs, full, dh, act, w_in, scale_in, w_out, scale_out):
    shapes = (array(w_in.shape), array(w_out.shape))
    kernel = functools.partial(grads_kernel, 128)
    args = (mine, theirs, full, dh, act, w_in, scale_in, w_out, scale_out)
    held = like(*args)
    held[2] = ((full.shape[0], full.shape[1] // CORES), BF16)
    return call(kernel, shapes, held + like(*shapes), len(args) + 2, 1 << 20, 1 << 20, *args, limit=SNUG)


def combine(ids, back, tok_rows, width, n_expert, n_y):
    shape = array((tok_rows, width))
    scratch = like(ids, back) + [(back.shape, F32)] + like(shape)
    kernel = functools.partial(combine_kernel, n_expert, n_y)
    return call(kernel, shape, scratch, 3, 1 << 20, 1 << 20, ids, back, limit=ROOMY)


def per_device(tokens, grad_output, expert_ids, gate_weights, w_in, scale_in, w_out, scale_out):
    n_expert = lax.axis_size("expert")
    n_y = lax.axis_size("y")
    n_dp = lax.axis_size("dp")
    tok_rows, width = tokens.shape
    units = w_out.shape[1]
    hidden = 2 * units
    w_in, w_out = w_in[0], w_out[0]
    parties = n_expert * n_y
    rows = parties * CAP
    share = rows // n_dp

    messages = make_slots(expert_ids, gate_weights, tokens, grad_output, n_expert, n_y)
    got = exchange(messages, ("expert", "y"))

    own, own_in, own_out = clip_weights(messages, w_in, scale_in, w_out, scale_out)
    oth_in, oth_out = swap(own_in), swap(own_out)

    part, xdy, gate_rows = gather(got, own, oth_in, oth_out)
    parts = exchange(part.reshape(n_dp, share, 3 * hidden), "dp")
    z = lax.axis_index("dp").astype(jnp.int32).reshape(1)
    copies = activate(z, parts, gate_rows, units)
    full = exchange(copies, "dp").reshape(rows, 3 * hidden)

    xdy_r = swap(xdy)
    returns, dh_oth, act_oth = scatter(xdy_r, full, own, oth_in, parties)
    back = exchange(returns, ("expert", "y"))
    grad_tokens = combine(expert_ids, back, tok_rows, width, n_expert, n_y)

    dh_r, act_r = swap(dh_oth), swap(act_oth)
    grad_in, grad_out = weight_grads(xdy, xdy_r, full, dh_r, act_r, w_in, scale_in, w_out, scale_out)
    return grad_tokens, grad_in[None], grad_out[None]


def solution(mesh):
    names = ("expert", "y", "core", "dp")
    n_expert, n_tensor, n_dp = (mesh.shape[a] for a in ("expert", "tensor", "dp"))
    fine = Mesh(mesh.devices.reshape(n_expert, n_tensor // CORES, CORES, n_dp), names)
    tensor = ("y", "core")
    block = ("expert", "y", "core")
    placed = (
        P(block, "dp"),
        P(block, "dp"),
        P(block, None),
        P(block, None),
        P("expert", "dp", tensor),
        P("expert", tensor),
        P("expert", tensor, "dp"),
        P("expert", "dp"),
    )
    return jax.shard_map(
        per_device,
        mesh=fine,
        in_specs=placed,
        out_specs=(P(block, "dp"), P("expert", "dp", tensor), P("expert", tensor, "dp")),
        check_vma=False,
    )
```

```python
import functools
import jax
import jax.numpy as jnp
from jax import lax
from jax.experimental import pallas as pl
from jax.experimental.pallas import tpu as pltpu
from jax.sharding import Mesh, PartitionSpec as P

CAP = 3
CORES = 2
PIECES = 3
LANE = 128
MIB = 1024 * 1024
ROOMY, SNUG, FULL = 28 * MIB, 51 * MIB, 60 * MIB
F32 = jnp.float32
BF16 = jnp.bfloat16


def swap(x):
    return lax.ppermute(x, "core", [(0, 1), (1, 0)])


def exchange(x, axes):
    return lax.all_to_all(x, axes, split_axis=0, concat_axis=0, tiled=True)


def dot(a, b, dims):
    return lax.dot_general(a, b, (dims, ((), ())), preferred_element_type=F32)


def up(n, m):
    return -(-n // m) * m


def routing(ids, n_expert):
    tok_rows, top = ids.shape
    at = lax.broadcasted_iota(jnp.int32, (n_expert, LANE), 0)
    seen = jnp.zeros((n_expert, LANE), jnp.int32)
    masks, named = [], []
    for i in range(tok_rows):
        hits = [jnp.broadcast_to(ids[i : i + 1, k : k + 1], at.shape) == at for k in range(top)]
        any_hit = functools.reduce(jnp.logical_or, hits)
        masks.append([any_hit & (seen == j) for j in range(CAP)])
        named.append(hits)
        seen = seen + any_hit.astype(jnp.int32)
    return masks, named


def start_all(pairs, sems, first=0):
    copies = [pltpu.make_async_copy(src, dst, sems.at[first + n]) for n, (src, dst) in enumerate(pairs)]
    for c in copies:
        c.start()
    return copies


def wait_all(copies):
    for c in copies:
        c.wait()


def slots_kernel(
    n_expert, n_y, size, ids_ref, gates_ref, tok_ref, cot_ref, out_ref, ids, gates, tok, cot, wide, narrow, sems
):
    tok_rows, width = tok.shape
    tiles = width // LANE
    copies = start_all([(ids_ref, ids), (gates_ref, gates), (tok_ref, tok), (cot_ref, cot)], sems)
    wide[...] = jnp.zeros_like(wide)
    wait_all(copies)
    masks, named = routing(ids[...], n_expert)
    gate = gates[...].astype(F32)
    lane = lax.broadcasted_iota(jnp.int32, (n_expert, LANE), 1)
    gate_row = jnp.zeros((n_expert, LANE), F32)
    for i in range(tok_rows):
        weight = jnp.zeros((n_expert, LANE), F32)
        for k, hit in enumerate(named[i]):
            weight = jnp.where(hit, jnp.broadcast_to(gate[i : i + 1, k : k + 1], hit.shape), weight)
        for j in range(CAP):
            gate_row = jnp.where(masks[i][j] & (lane == j), weight, gate_row)
    wide[pl.ds(2 * tiles * CAP, n_expert, stride=size), :] = gate_row
    both = [tok[...].astype(F32), cot[...].astype(F32)]
    for k in range(2 * tiles):
        at = (k % tiles) * LANE
        cols = both[k // tiles][:, at : at + LANE]
        for j in range(CAP):
            value = jnp.zeros((n_expert, LANE), F32)
            for i in range(tok_rows):
                value = jnp.where(masks[i][j], jnp.broadcast_to(cols[i : i + 1], value.shape), value)
            wide[pl.ds(j * 2 * tiles + k, n_expert, stride=size), :] = value
    narrow[...] = wide[...].reshape(n_expert, size, LANE).astype(BF16)
    wait_all(start_all([(narrow, out_ref.at[:, y]) for y in range(n_y)], sems, 4))


def gather_kernel(
    parties, size, got_ref, own_ref, oth_in_ref, oth_out_ref, part_ref, rows_ref, gate_ref,
    got, wide, own, oth, rows, part, gate, sems,
):
    width = own.shape[1]
    units = own.shape[0] - width
    tiles = width // LANE
    half = width + units
    copies = start_all([(got_ref, got), (own_ref, own)], sems)
    copies[0].wait()
    wide[...] = got[...].astype(F32)
    copies += start_all([(oth_in_ref, oth.at[0:width, :]), (oth_out_ref, oth.at[width:half, :])], sems, 2)
    gates = wide[pl.ds(2 * tiles * CAP, parties, stride=size), :]
    for j in range(CAP):
        at = slice(j * parties, (j + 1) * parties)
        gate[at, :] = jnp.broadcast_to(gates[:, j : j + 1], (parties, LANE))
        for k in range(2 * tiles):
            value = wide[pl.ds(j * 2 * tiles + k, parties, stride=size), :]
            rows[at, k * LANE : (k + 1) * LANE] = value.astype(BF16)
    outs = start_all([(rows, rows_ref), (gate, gate_ref)], sems, 4)
    for n, weights in enumerate((own, oth)):
        wait_all(copies[n + 1 : 2 + 2 * n])
        pre = dot(rows[:, :width], weights[:width, :], ((1,), (0,)))
        part[:, n * half : n * half + width] = pre.astype(BF16)
        back = dot(rows[:, width:], weights[width:, :], ((1,), (1,)))
        part[:, n * half + width : (n + 1) * half] = back.astype(BF16)
        cols = slice(n * half, (n + 1) * half)
        outs += start_all([(part.at[:, cols], part_ref.at[:, cols])], sems, 6 + n)
    wait_all(outs)


def clip_kernel(
    step, after_ref, w_in_ref, scale_in_ref, w_out_ref, scale_out_ref, own_ref, in_ref, out_ref,
    w_in, scale_in, w_out, scale_out, own, sems,
):
    del after_ref
    wait_all(
        start_all([(w_in_ref, w_in), (scale_in_ref, scale_in), (w_out_ref, w_out), (scale_out_ref, scale_out)], sems)
    )
    start = 0
    for weights, scales in ((w_in, scale_in), (w_out, scale_out)):
        bound = 448.0 * scales[...].astype(F32)
        for r in range(0, weights.shape[0], step):
            block = weights[r : r + step, :].astype(F32)
            own[start + r : start + r + step, :] = jnp.clip(block, -bound, bound).astype(BF16)
        start += weights.shape[0]
    tall = w_in.shape[0]
    wait_all(start_all([(own, own_ref), (own.at[0:tall, :], in_ref), (own.at[tall:start, :], out_ref)], sems, 4))


def activate_kernel(share, units, z_ref, parts_ref, gate_ref, out_ref, parts, gate, out, sems):
    n_dp = parts.shape[0]
    half = 3 * units
    at = pl.multiple_of(z_ref[0] * share, 8)
    halves = [slice(n * half, (n + 1) * half) for n in range(CORES)]
    copies = start_all(
        [(gate_ref.at[pl.ds(at, share), :], gate)] + [(parts_ref.at[:, :, h], parts.at[:, :, h]) for h in halves], sems
    )
    copies[0].wait()
    gates = gate[...]

    def total(at):
        value = parts[0, :, at : at + LANE].astype(F32)
        for p in range(1, n_dp):
            value = value + parts[p, :, at : at + LANE].astype(F32)
        return value

    outs = []
    for n in range(CORES):
        copies[1 + n].wait()
        for c in range(n * half, n * half + units, LANE):
            gate_pre = total(c)
            up_pre = total(c + units)
            d_act = gates * total(c + 2 * units)
            sigmoid_gate = jax.nn.sigmoid(gate_pre)
            silu_gate = gate_pre * sigmoid_gate
            slope = sigmoid_gate * (1.0 + gate_pre * (1.0 - sigmoid_gate))
            out[:, c : c + LANE] = (d_act * up_pre * slope).astype(BF16)
            out[:, c + units : c + units + LANE] = (d_act * silu_gate).astype(BF16)
            out[:, c + 2 * units : c + 2 * units + LANE] = (gates * silu_gate * up_pre).astype(BF16)
        pairs = [(out.at[:, halves[n]], out_ref.at[p, :, halves[n]]) for p in range(n_dp)]
        outs += start_all(pairs, sems, 1 + CORES + n * n_dp)
    wait_all(outs)


def place(j, k):
    at = (k // 2 * CAP + j) * LANE
    return k % 2, slice(at, at + LANE)


def scatter_kernel(
    parties, offset, after_ref, full_ref, own_ref, oth_ref, out_ref, dh_ref, act_ref, dh, act, own, oth, wide, out, sems
):
    del after_ref
    width = own.shape[0]
    hidden = own.shape[1]
    step = width // PIECES
    span = out.shape[2] // PIECES
    copies = start_all(
        [
            (full_ref.at[:, 0:hidden], dh.at[0]),
            (full_ref.at[:, offset : offset + hidden], dh.at[1]),
            (full_ref.at[:, offset + hidden : 2 * offset], act),
        ],
        sems,
    )
    spans = [slice(p * step, (p + 1) * step) for p in range(PIECES)]
    pieces = [
        start_all([(own_ref.at[at, :], own.at[at, :]), (oth_ref.at[at, :], oth.at[at, :])], sems, 3 + 2 * p)
        for p, at in enumerate(spans)
    ]
    wait_all(copies)
    outs = start_all([(dh.at[1], dh_ref), (act, act_ref)], sems, 3 + 2 * PIECES)
    for p, at in enumerate(spans):
        wait_all(pieces[p])
        dx = dot(dh[0], own[at, :], ((1,), (1,))) + dot(dh[1], oth[at, :], ((1,), (1,)))
        for j in range(CAP):
            for k in range(step // LANE):
                row, cols = place(j, p * (step // LANE) + k)
                wide[:, row, cols] = dx[j * parties : (j + 1) * parties, k * LANE : (k + 1) * LANE]
        cols = slice(p * span, (p + 1) * span)
        out[:, :, cols] = wide[:, :, cols].astype(BF16)
        outs += start_all([(out.at[:, :, cols], out_ref.at[:, :, cols])], sems, 5 + 2 * PIECES + p)
    wait_all(outs)


def grads_kernel(step, *refs):
    n_in = 9
    sources, (in_ref, out_ref) = refs[:n_in], refs[n_in : n_in + 2]
    held, (in_v, out_v, sems) = refs[n_in + 2 : 2 * n_in + 2], refs[2 * n_in + 2 :]
    mine, theirs, full, dh, act, w_in, scale_in, w_out, scale_out = held
    half = full.shape[1]
    pairs = [(src.at[:, 0:half] if dst is full else src, dst) for src, dst in zip(sources, held)]
    wait_all(start_all(pairs, sems))
    width, hidden = w_in.shape
    outs = []
    for n, (weights, scales, grad, dst) in enumerate(((w_in, scale_in, in_v, in_ref), (w_out, scale_out, out_v, out_ref))):
        bound = 448.0 * scales[...].astype(F32)
        for r in range(0, weights.shape[0], step):
            at = slice(r, r + step)
            if grad is in_v:
                total = dot(mine[:, at], full[:, :hidden], ((0,), (0,)))
                total = total + dot(theirs[:, at], dh[...], ((0,), (0,)))
            else:
                total = dot(full[:, hidden + r : hidden + r + step], mine[:, width:], ((0,), (0,)))
                total = total + dot(act[:, at], theirs[:, width:], ((0,), (0,)))
            keep = jnp.abs(weights[at, :].astype(F32)) <= bound
            grad[at, :] = jnp.where(keep, total, 0.0).astype(BF16)
        outs += start_all([(grad, dst)], sems, n_in + n)
    wait_all(outs)


def combine_kernel(n_expert, n_y, ids_ref, back_ref, out_ref, ids, back, wide, out, sems):
    tok_rows, width = out.shape
    tiles = width // LANE
    copies = start_all([(ids_ref, ids), (back_ref, back)], sems)
    copies[0].wait()
    masks, _ = routing(ids[...], n_expert)
    copies[1].wait()
    wide[...] = back[...].astype(F32)
    for k in range(tiles):
        totals = [jnp.zeros((1, LANE), F32) for _ in range(tok_rows)]
        for j in range(CAP):
            row, cols = place(j, k)
            value = wide[:, row, cols]
            value = jnp.sum(value.reshape(n_expert, n_y, LANE), axis=1)
            for i in range(tok_rows):
                totals[i] = totals[i] + jnp.sum(jnp.where(masks[i][j], value, 0.0), axis=0, keepdims=True)
        out[:, k * LANE : (k + 1) * LANE] = jnp.concatenate(totals, axis=0).astype(BF16)
    wait_all(start_all([(out, out_ref)], sems, 2))


ANY = pl.BlockSpec(memory_space=pl.ANY)
SMEM = pl.BlockSpec(memory_space=pltpu.SMEM)


def array(shape, dtype=BF16):
    return jax.ShapeDtypeStruct(shape, dtype)


def call(kernel, outs, scratch, n_sems, flops, moved, *args, limit=FULL):
    return pl.pallas_call(
        kernel,
        out_shape=outs,
        in_specs=[SMEM if a.shape == (1,) else ANY for a in args],
        out_specs=jax.tree.map(lambda _: ANY, outs),
        scratch_shapes=[pltpu.VMEM(*s) for s in scratch] + [pltpu.SemaphoreType.DMA((n_sems,))],
        compiler_params=pltpu.CompilerParams(vmem_limit_bytes=limit),
        cost_estimate=pl.CostEstimate(flops=flops, bytes_accessed=moved, transcendentals=0),
    )(*args)


def like(*arrays):
    return [(a.shape, a.dtype) for a in arrays]


def make_slots(ids, gates, tokens, cotangents, n_expert, n_y):
    size = up(2 * CAP * tokens.shape[1] // LANE + 1, 8)
    args = (ids, gates, tokens, cotangents)
    scratch = like(*args) + [((n_expert * size, LANE), F32), ((n_expert, size, LANE), BF16)]
    kernel = functools.partial(slots_kernel, n_expert, n_y, size)
    out = call(kernel, array((n_expert, n_y, size, LANE)), scratch, 4 + n_y, 1 << 20, 1 << 20, *args)
    return out.reshape(n_expert * n_y, size, LANE)


def clip_weights(after, w_in, scale_in, w_out, scale_out):
    width = w_in.shape[1]
    args = (w_in, scale_in, w_out, scale_out)
    heights = (w_in.shape[0] + w_out.shape[0], w_in.shape[0], w_out.shape[0])
    scratch = like(*args) + [((heights[0], width), BF16)]
    size = heights[0] * width
    kernel = functools.partial(clip_kernel, 64)
    return call(kernel, tuple(array((h, width)) for h in heights), scratch, 7, 4 * size, 4 * size, after, *args)


def activate(z, parts, gate_rows, units):
    n_dp, share, cols = parts.shape
    scratch = like(parts) + [((share, LANE), F32), ((share, cols), BF16)]
    kernel = functools.partial(activate_kernel, share, units)
    n_sems = 1 + CORES + CORES * n_dp
    return call(kernel, array(parts.shape), scratch, n_sems, 2 * parts.size, 4 * parts.size, z, parts, gate_rows, limit=ROOMY)


def gather(got, own, oth_in, oth_out):
    parties, size, _ = got.shape
    height, width = own.shape
    rows = parties * CAP
    flat = got.reshape(parties * size, LANE)
    shapes = (array((rows, 2 * height)), array((rows, 2 * width)), array((rows, LANE), F32))
    scratch = like(flat) + [(flat.shape, F32)] + like(own, own, shapes[1], shapes[0], shapes[2])
    kernel = functools.partial(gather_kernel, parties, size)
    moved = 4 * own.size + 6 * got.size
    return call(kernel, shapes, scratch, 6 + CORES, 4 * rows * own.size, moved, flat, own, oth_in, oth_out, limit=SNUG)


def scatter(after, full, own, oth, parties):
    rows = full.shape[0]
    height, width = own.shape
    hidden = width
    flat = array((parties, 2, CAP * width // 2))
    shapes = (flat, array((rows, hidden)), array((rows, height - width)))
    scratch = [((2, rows, hidden), BF16)] + like(shapes[2], oth, oth) + [(flat.shape, F32), (flat.shape, BF16)]
    kernel = functools.partial(scatter_kernel, parties, height)
    flops, moved = 4 * rows * width * hidden, 4 * own.size
    return call(kernel, shapes, scratch, 5 + 3 * PIECES, flops, moved, after, full, own, oth, limit=SNUG)


def weight_grads(mine, theirs, full, dh, act, w_in, scale_in, w_out, scale_out):
    shapes = (array(w_in.shape), array(w_out.shape))
    kernel = functools.partial(grads_kernel, 128)
    args = (mine, theirs, full, dh, act, w_in, scale_in, w_out, scale_out)
    held = like(*args)
    held[2] = ((full.shape[0], full.shape[1] // CORES), BF16)
    return call(kernel, shapes, held + like(*shapes), len(args) + 2, 1 << 20, 1 << 20, *args, limit=SNUG)


def combine(ids, back, tok_rows, width, n_expert, n_y):
    shape = array((tok_rows, width))
    scratch = like(ids, back) + [(back.shape, F32)] + like(shape)
    kernel = functools.partial(combine_kernel, n_expert, n_y)
    return call(kernel, shape, scratch, 3, 1 << 20, 1 << 20, ids, back, limit=ROOMY)


def per_device(tokens, grad_output, expert_ids, gate_weights, w_in, scale_in, w_out, scale_out):
    n_expert = lax.axis_size("expert")
    n_y = lax.axis_size("y")
    n_dp = lax.axis_size("dp")
    tok_rows, width = tokens.shape
    units = w_out.shape[1]
    hidden = 2 * units
    w_in, w_out = w_in[0], w_out[0]
    parties = n_expert * n_y
    rows = parties * CAP
    share = rows // n_dp

    messages = make_slots(expert_ids, gate_weights, tokens, grad_output, n_expert, n_y)
    got = exchange(messages, ("expert", "y"))

    own, own_in, own_out = clip_weights(messages, w_in, scale_in, w_out, scale_out)
    oth_in, oth_out = swap(own_in), swap(own_out)

    part, xdy, gate_rows = gather(got, own, oth_in, oth_out)
    parts = exchange(part.reshape(n_dp, share, 3 * hidden), "dp")
    z = lax.axis_index("dp").astype(jnp.int32).reshape(1)
    copies = activate(z, parts, gate_rows, units)
    full = exchange(copies, "dp").reshape(rows, 3 * hidden)

    xdy_r = swap(xdy)
    returns, dh_oth, act_oth = scatter(xdy_r, full, own, oth_in, parties)
    back = exchange(returns, ("expert", "y"))
    grad_tokens = combine(expert_ids, back, tok_rows, width, n_expert, n_y)

    dh_r, act_r = swap(dh_oth), swap(act_oth)
    grad_in, grad_out = weight_grads(xdy, xdy_r, full, dh_r, act_r, w_in, scale_in, w_out, scale_out)
    return grad_tokens, grad_in[None], grad_out[None]


def solution(mesh):
    names = ("expert", "y", "core", "dp")
    n_expert, n_tensor, n_dp = (mesh.shape[a] for a in ("expert", "tensor", "dp"))
    fine = Mesh(mesh.devices.reshape(n_expert, n_tensor // CORES, CORES, n_dp), names)
    tensor = ("y", "core")
    block = ("expert", "y", "core")
    placed = (
        P(block, "dp"),
        P(block, "dp"),
        P(block, None),
        P(block, None),
        P("expert", "dp", tensor),
        P("expert", tensor),
        P("expert", tensor, "dp"),
        P("expert", "dp"),
    )
    return jax.shard_map(
        per_device,
        mesh=fine,
        in_specs=placed,
        out_specs=(P(block, "dp"), P("expert", "dp", tensor), P("expert", tensor, "dp")),
        check_vma=False,
    )
```

```python
import functools
import jax
import jax.numpy as jnp
from jax import lax
from jax.experimental import pallas as pl
from jax.experimental.pallas import tpu as pltpu
from jax.sharding import Mesh, PartitionSpec as P

CAP = 3
CORES = 2
PIECES = 3
LANE = 128
MIB = 1024 * 1024
ROOMY, SNUG, FULL = 28 * MIB, 51 * MIB, 60 * MIB
F32 = jnp.float32
BF16 = jnp.bfloat16


def swap(x):
    return lax.ppermute(x, "core", [(0, 1), (1, 0)])


def exchange(x, axes):
    return lax.all_to_all(x, axes, split_axis=0, concat_axis=0, tiled=True)


def dot(a, b, dims):
    return lax.dot_general(a, b, (dims, ((), ())), preferred_element_type=F32)


def up(n, m):
    return -(-n // m) * m


def routing(ids, n_expert):
    tok_rows, top = ids.shape
    at = lax.broadcasted_iota(jnp.int32, (n_expert, LANE), 0)
    seen = jnp.zeros((n_expert, LANE), jnp.int32)
    masks, named = [], []
    for i in range(tok_rows):
        hits = [jnp.broadcast_to(ids[i : i + 1, k : k + 1], at.shape) == at for k in range(top)]
        any_hit = functools.reduce(jnp.logical_or, hits)
        masks.append([any_hit & (seen == j) for j in range(CAP)])
        named.append(hits)
        seen = seen + any_hit.astype(jnp.int32)
    return masks, named


def start_all(pairs, sems, first=0):
    copies = [pltpu.make_async_copy(src, dst, sems.at[first + n]) for n, (src, dst) in enumerate(pairs)]
    for c in copies:
        c.start()
    return copies


def wait_all(copies):
    for c in copies:
        c.wait()


def slots_kernel(
    n_expert, n_y, size, ids_ref, gates_ref, tok_ref, cot_ref, out_ref, ids, gates, tok, cot, wide, narrow, sems
):
    tok_rows, width = tok.shape
    tiles = width // LANE
    copies = start_all([(ids_ref, ids), (gates_ref, gates), (tok_ref, tok), (cot_ref, cot)], sems)
    wide[...] = jnp.zeros_like(wide)
    wait_all(copies)
    masks, named = routing(ids[...], n_expert)
    gate = gates[...].astype(F32)
    lane = lax.broadcasted_iota(jnp.int32, (n_expert, LANE), 1)
    gate_row = jnp.zeros((n_expert, LANE), F32)
    for i in range(tok_rows):
        weight = jnp.zeros((n_expert, LANE), F32)
        for k, hit in enumerate(named[i]):
            weight = jnp.where(hit, jnp.broadcast_to(gate[i : i + 1, k : k + 1], hit.shape), weight)
        for j in range(CAP):
            gate_row = jnp.where(masks[i][j] & (lane == j), weight, gate_row)
    wide[pl.ds(2 * tiles * CAP, n_expert, stride=size), :] = gate_row
    both = [tok[...].astype(F32), cot[...].astype(F32)]
    for k in range(2 * tiles):
        at = (k % tiles) * LANE
        cols = both[k // tiles][:, at : at + LANE]
        for j in range(CAP):
            value = jnp.zeros((n_expert, LANE), F32)
            for i in range(tok_rows):
                value = jnp.where(masks[i][j], jnp.broadcast_to(cols[i : i + 1], value.shape), value)
            wide[pl.ds(j * 2 * tiles + k, n_expert, stride=size), :] = value
    narrow[...] = wide[...].reshape(n_expert, size, LANE).astype(BF16)
    wait_all(start_all([(narrow, out_ref.at[:, y]) for y in range(n_y)], sems, 4))


def gather_kernel(
    parties, size, got_ref, own_ref, oth_in_ref, oth_out_ref, part_ref, rows_ref, gate_ref,
    got, wide, own, oth, rows, part, gate, sems,
):
    width = own.shape[1]
    units = own.shape[0] - width
    tiles = width // LANE
    half = width + units
    copies = start_all([(got_ref, got), (own_ref, own)], sems)
    copies[0].wait()
    wide[...] = got[...].astype(F32)
    copies += start_all([(oth_in_ref, oth.at[0:width, :]), (oth_out_ref, oth.at[width:half, :])], sems, 2)
    gates = wide[pl.ds(2 * tiles * CAP, parties, stride=size), :]
    for j in range(CAP):
        at = slice(j * parties, (j + 1) * parties)
        gate[at, :] = jnp.broadcast_to(gates[:, j : j + 1], (parties, LANE))
        for k in range(2 * tiles):
            value = wide[pl.ds(j * 2 * tiles + k, parties, stride=size), :]
            rows[at, k * LANE : (k + 1) * LANE] = value.astype(BF16)
    outs = start_all([(rows, rows_ref), (gate, gate_ref)], sems, 4)
    for n, weights in enumerate((own, oth)):
        wait_all(copies[n + 1 : 2 + 2 * n])
        pre = dot(rows[:, :width], weights[:width, :], ((1,), (0,)))
        part[:, n * half : n * half + width] = pre.astype(BF16)
        back = dot(rows[:, width:], weights[width:, :], ((1,), (1,)))
        part[:, n * half + width : (n + 1) * half] = back.astype(BF16)
        cols = slice(n * half, (n + 1) * half)
        outs += start_all([(part.at[:, cols], part_ref.at[:, cols])], sems, 6 + n)
    wait_all(outs)


def clip_kernel(
    step, after_ref, w_in_ref, scale_in_ref, w_out_ref, scale_out_ref, own_ref, in_ref, out_ref,
    w_in, scale_in, w_out, scale_out, own, sems,
):
    del after_ref
    wait_all(
        start_all([(w_in_ref, w_in), (scale_in_ref, scale_in), (w_out_ref, w_out), (scale_out_ref, scale_out)], sems)
    )
    start = 0
    for weights, scales in ((w_in, scale_in), (w_out, scale_out)):
        bound = 448.0 * scales[...].astype(F32)
        for r in range(0, weights.shape[0], step):
            block = weights[r : r + step, :].astype(F32)
            own[start + r : start + r + step, :] = jnp.clip(block, -bound, bound).astype(BF16)
        start += weights.shape[0]
    tall = w_in.shape[0]
    wait_all(start_all([(own, own_ref), (own.at[0:tall, :], in_ref), (own.at[tall:start, :], out_ref)], sems, 4))


def activate_kernel(share, units, z_ref, parts_ref, gate_ref, out_ref, parts, gate, out, sems):
    n_dp = parts.shape[0]
    half = 3 * units
    at = pl.multiple_of(z_ref[0] * share, 8)
    halves = [slice(n * half, (n + 1) * half) for n in range(CORES)]
    copies = start_all(
        [(gate_ref.at[pl.ds(at, share), :], gate)] + [(parts_ref.at[:, :, h], parts.at[:, :, h]) for h in halves], sems
    )
    copies[0].wait()
    gates = gate[...]

    def total(at):
        value = parts[0, :, at : at + LANE].astype(F32)
        for p in range(1, n_dp):
            value = value + parts[p, :, at : at + LANE].astype(F32)
        return value

    outs = []
    for n in range(CORES):
        copies[1 + n].wait()
        for c in range(n * half, n * half + units, LANE):
            gate_pre = total(c)
            up_pre = total(c + units)
            d_act = gates * total(c + 2 * units)
            sigmoid_gate = jax.nn.sigmoid(gate_pre)
            silu_gate = gate_pre * sigmoid_gate
            slope = sigmoid_gate * (1.0 + gate_pre * (1.0 - sigmoid_gate))
            out[:, c : c + LANE] = (d_act * up_pre * slope).astype(BF16)
            out[:, c + units : c + units + LANE] = (d_act * silu_gate).astype(BF16)
            out[:, c + 2 * units : c + 2 * units + LANE] = (gates * silu_gate * up_pre).astype(BF16)
        pairs = [(out.at[:, halves[n]], out_ref.at[p, :, halves[n]]) for p in range(n_dp)]
        outs += start_all(pairs, sems, 1 + CORES + n * n_dp)
    wait_all(outs)


def place(j, k):
    at = (k // 2 * CAP + j) * LANE
    return k % 2, slice(at, at + LANE)


def scatter_kernel(
    parties, offset, after_ref, full, own_ref, oth_ref, out_ref, dh_ref, act_ref, own, oth, wide, out, sems
):
    del after_ref
    width = own.shape[0]
    hidden = own.shape[1]
    step = width // PIECES
    span = out.shape[2] // PIECES
    spans = [slice(p * step, (p + 1) * step) for p in range(PIECES)]
    pieces = [
        start_all([(own_ref.at[at, :], own.at[at, :]), (oth_ref.at[at, :], oth.at[at, :])], sems, 3 + 2 * p)
        for p, at in enumerate(spans)
    ]
    dh, act = full.at[:, offset : offset + hidden], full.at[:, offset + hidden : 2 * offset]
    outs = start_all([(dh, dh_ref), (act, act_ref)], sems, 3 + 2 * PIECES)
    for p, at in enumerate(spans):
        wait_all(pieces[p])
        dx = dot(full[:, 0:hidden], own[at, :], ((1,), (1,))) + dot(dh[...], oth[at, :], ((1,), (1,)))
        for j in range(CAP):
            for k in range(step // LANE):
                row, cols = place(j, p * (step // LANE) + k)
                wide[:, row, cols] = dx[j * parties : (j + 1) * parties, k * LANE : (k + 1) * LANE]
        cols = slice(p * span, (p + 1) * span)
        out[:, :, cols] = wide[:, :, cols].astype(BF16)
        outs += start_all([(out.at[:, :, cols], out_ref.at[:, :, cols])], sems, 5 + 2 * PIECES + p)
    wait_all(outs)


def grads_kernel(step, *refs):
    n_in = 9
    sources, (in_ref, out_ref) = refs[:n_in], refs[n_in : n_in + 2]
    held, (in_v, out_v, sems) = refs[n_in + 2 : 2 * n_in + 2], refs[2 * n_in + 2 :]
    mine, theirs, full, dh, act, w_in, scale_in, w_out, scale_out = held
    half = full.shape[1]
    pairs = [(src.at[:, 0:half] if dst is full else src, dst) for src, dst in zip(sources, held)]
    wait_all(start_all(pairs, sems))
    width, hidden = w_in.shape
    outs = []
    for n, (weights, scales, grad, dst) in enumerate(((w_in, scale_in, in_v, in_ref), (w_out, scale_out, out_v, out_ref))):
        bound = 448.0 * scales[...].astype(F32)
        for r in range(0, weights.shape[0], step):
            at = slice(r, r + step)
            if grad is in_v:
                total = dot(mine[:, at], full[:, :hidden], ((0,), (0,)))
                total = total + dot(theirs[:, at], dh[...], ((0,), (0,)))
            else:
                total = dot(full[:, hidden + r : hidden + r + step], mine[:, width:], ((0,), (0,)))
                total = total + dot(act[:, at], theirs[:, width:], ((0,), (0,)))
            keep = jnp.abs(weights[at, :].astype(F32)) <= bound
            grad[at, :] = jnp.where(keep, total, 0.0).astype(BF16)
        outs += start_all([(grad, dst)], sems, n_in + n)
    wait_all(outs)


def combine_kernel(n_expert, n_y, ids_ref, back_ref, out_ref, ids, back, wide, out, sems):
    tok_rows, width = out.shape
    tiles = width // LANE
    copies = start_all([(ids_ref, ids), (back_ref, back)], sems)
    copies[0].wait()
    masks, _ = routing(ids[...], n_expert)
    copies[1].wait()
    wide[...] = back[...].astype(F32)
    for k in range(tiles):
        totals = [jnp.zeros((1, LANE), F32) for _ in range(tok_rows)]
        for j in range(CAP):
            row, cols = place(j, k)
            value = wide[:, row, cols]
            value = jnp.sum(value.reshape(n_expert, n_y, LANE), axis=1)
            for i in range(tok_rows):
                totals[i] = totals[i] + jnp.sum(jnp.where(masks[i][j], value, 0.0), axis=0, keepdims=True)
        out[:, k * LANE : (k + 1) * LANE] = jnp.concatenate(totals, axis=0).astype(BF16)
    wait_all(start_all([(out, out_ref)], sems, 2))


ANY = pl.BlockSpec(memory_space=pl.ANY)
VM = pl.BlockSpec(memory_space=pltpu.VMEM)
SMEM = pl.BlockSpec(memory_space=pltpu.SMEM)


def array(shape, dtype=BF16):
    return jax.ShapeDtypeStruct(shape, dtype)


def call(kernel, outs, scratch, n_sems, flops, moved, *args, limit=FULL, resident=()):
    return pl.pallas_call(
        kernel,
        out_shape=outs,
        in_specs=[SMEM if a.shape == (1,) else VM if n in resident else ANY for n, a in enumerate(args)],
        out_specs=jax.tree.map(lambda _: ANY, outs),
        scratch_shapes=[pltpu.VMEM(*s) for s in scratch] + [pltpu.SemaphoreType.DMA((n_sems,))],
        compiler_params=pltpu.CompilerParams(vmem_limit_bytes=limit),
        cost_estimate=pl.CostEstimate(flops=flops, bytes_accessed=moved, transcendentals=0),
    )(*args)


def like(*arrays):
    return [(a.shape, a.dtype) for a in arrays]


def make_slots(ids, gates, tokens, cotangents, n_expert, n_y):
    size = up(2 * CAP * tokens.shape[1] // LANE + 1, 8)
    args = (ids, gates, tokens, cotangents)
    scratch = like(*args) + [((n_expert * size, LANE), F32), ((n_expert, size, LANE), BF16)]
    kernel = functools.partial(slots_kernel, n_expert, n_y, size)
    out = call(kernel, array((n_expert, n_y, size, LANE)), scratch, 4 + n_y, 1 << 20, 1 << 20, *args)
    return out.reshape(n_expert * n_y, size, LANE)


def clip_weights(after, w_in, scale_in, w_out, scale_out):
    width = w_in.shape[1]
    args = (w_in, scale_in, w_out, scale_out)
    heights = (w_in.shape[0] + w_out.shape[0], w_in.shape[0], w_out.shape[0])
    scratch = like(*args) + [((heights[0], width), BF16)]
    size = heights[0] * width
    kernel = functools.partial(clip_kernel, 64)
    return call(kernel, tuple(array((h, width)) for h in heights), scratch, 7, 4 * size, 4 * size, after, *args)


def activate(z, parts, gate_rows, units):
    n_dp, share, cols = parts.shape
    scratch = like(parts) + [((share, LANE), F32), ((share, cols), BF16)]
    kernel = functools.partial(activate_kernel, share, units)
    n_sems = 1 + CORES + CORES * n_dp
    return call(kernel, array(parts.shape), scratch, n_sems, 2 * parts.size, 4 * parts.size, z, parts, gate_rows, limit=ROOMY)


def gather(got, own, oth_in, oth_out):
    parties, size, _ = got.shape
    height, width = own.shape
    rows = parties * CAP
    flat = got.reshape(parties * size, LANE)
    shapes = (array((rows, 2 * height)), array((rows, 2 * width)), array((rows, LANE), F32))
    scratch = like(flat) + [(flat.shape, F32)] + like(own, own, shapes[1], shapes[0], shapes[2])
    kernel = functools.partial(gather_kernel, parties, size)
    moved = 4 * own.size + 6 * got.size
    return call(kernel, shapes, scratch, 6 + CORES, 4 * rows * own.size, moved, flat, own, oth_in, oth_out, limit=SNUG)


def scatter(after, full, own, oth, parties):
    rows = full.shape[0]
    height, width = own.shape
    hidden = width
    flat = array((parties, 2, CAP * width // 2))
    shapes = (flat, array((rows, hidden)), array((rows, height - width)))
    scratch = like(oth, oth) + [(flat.shape, F32), (flat.shape, BF16)]
    kernel = functools.partial(scatter_kernel, parties, height)
    flops, moved = 4 * rows * width * hidden, 4 * own.size
    return call(kernel, shapes, scratch, 5 + 3 * PIECES, flops, moved, after, full, own, oth, limit=SNUG, resident=(1,))


def weight_grads(mine, theirs, full, dh, act, w_in, scale_in, w_out, scale_out):
    shapes = (array(w_in.shape), array(w_out.shape))
    kernel = functools.partial(grads_kernel, 128)
    args = (mine, theirs, full, dh, act, w_in, scale_in, w_out, scale_out)
    held = like(*args)
    held[2] = ((full.shape[0], full.shape[1] // CORES), BF16)
    return call(kernel, shapes, held + like(*shapes), len(args) + 2, 1 << 20, 1 << 20, *args, limit=SNUG)


def combine(ids, back, tok_rows, width, n_expert, n_y):
    shape = array((tok_rows, width))
    scratch = like(ids, back) + [(back.shape, F32)] + like(shape)
    kernel = functools.partial(combine_kernel, n_expert, n_y)
    return call(kernel, shape, scratch, 3, 1 << 20, 1 << 20, ids, back, limit=ROOMY)


def per_device(tokens, grad_output, expert_ids, gate_weights, w_in, scale_in, w_out, scale_out):
    n_expert = lax.axis_size("expert")
    n_y = lax.axis_size("y")
    n_dp = lax.axis_size("dp")
    tok_rows, width = tokens.shape
    units = w_out.shape[1]
    hidden = 2 * units
    w_in, w_out = w_in[0], w_out[0]
    parties = n_expert * n_y
    rows = parties * CAP
    share = rows // n_dp

    messages = make_slots(expert_ids, gate_weights, tokens, grad_output, n_expert, n_y)
    got = exchange(messages, ("expert", "y"))

    own, own_in, own_out = clip_weights(messages, w_in, scale_in, w_out, scale_out)
    oth_in, oth_out = swap(own_in), swap(own_out)

    part, xdy, gate_rows = gather(got, own, oth_in, oth_out)
    parts = exchange(part.reshape(n_dp, share, 3 * hidden), "dp")
    z = lax.axis_index("dp").astype(jnp.int32).reshape(1)
    copies = activate(z, parts, gate_rows, units)
    full = exchange(copies, "dp").reshape(rows, 3 * hidden)

    xdy_r = swap(xdy)
    returns, dh_oth, act_oth = scatter(xdy_r, full, own, oth_in, parties)
    back = exchange(returns, ("expert", "y"))
    grad_tokens = combine(expert_ids, back, tok_rows, width, n_expert, n_y)

    dh_r, act_r = swap(dh_oth), swap(act_oth)
    grad_in, grad_out = weight_grads(xdy, xdy_r, full, dh_r, act_r, w_in, scale_in, w_out, scale_out)
    return grad_tokens, grad_in[None], grad_out[None]


def solution(mesh):
    names = ("expert", "y", "core", "dp")
    n_expert, n_tensor, n_dp = (mesh.shape[a] for a in ("expert", "tensor", "dp"))
    fine = Mesh(mesh.devices.reshape(n_expert, n_tensor // CORES, CORES, n_dp), names)
    tensor = ("y", "core")
    block = ("expert", "y", "core")
    placed = (
        P(block, "dp"),
        P(block, "dp"),
        P(block, None),
        P(block, None),
        P("expert", "dp", tensor),
        P("expert", tensor),
        P("expert", tensor, "dp"),
        P("expert", "dp"),
    )
    return jax.shard_map(
        per_device,
        mesh=fine,
        in_specs=placed,
        out_specs=(P(block, "dp"), P("expert", "dp", tensor), P("expert", tensor, "dp")),
        check_vma=False,
    )
```
